32 devices in a mesh: tm: 16 (over z, x, core), head: 2 (over y).
Axes of the slice: x: 2, y: 2, z: 4, core: 2. Of those that a mesh axis runs over, the one named last changes fastest.
Arguments:
- query_proj: bfloat16 [2048, 768], P('tm', 'head'), may hold values from -80 to 80
- key_proj: bfloat16 [2048, 768], P('tm', 'head'), may hold values from -80 to 80
- value_proj: bfloat16 [2048, 768], P('tm', 'head'), may hold values from -12 to 12
- query_gain: float32 [768], P('head'), may hold values from 0.25 to 1.75
- key_gain: float32 [768], P('head'), may hold values from 0.25 to 1.75
- gate_table: float32 [50, 768], P(None, 'head'), may hold values from 0.5 to 2
- frame_step: int32 [2], replicated, may hold values from 0 to 49
- far_blocks: int32 [16, 16], P('tm'), may hold values from -1 to 1, as said below
Outputs:
- attended: bfloat16 [2048, 768], P('tm', 'head')
The draws below stay inside these ranges and needn't reach their ends.
Inputs may be any that keep to these rules, and one draw needn't show every extreme that they name: `far_blocks`: entry [i, j] is the index of the key block of 64 tokens that query block i takes from query block j's tokens, or -1 for none; it is -1 wherever |i - j| <= 1.
All inputs are finite; a program needn't handle non-finite values.
Results may differ from the reference program's by a relative error of at most 0.007.
The reference program's roundings to bfloat16 on the way count: a program that leaves them out, or rounds other values in their place, can miss the bound.
Values may be sent and summed in bfloat16 or wider, within the bound.
No kernel may reach another device: no remote copies, remote signals or barrier semaphores. Data moves between devices by JAX's collectives and lax.ppermute only.
A program may use at most 64 MiB of HBM per device.

```python
import jax
import jax.numpy as jnp
from jax import lax

HD = 128
TOK_DEV = 128
BLK = 64
FRAME_TOK = 1560
STEPS = 50
HEADS = 6
TOKENS = 2048
QBLOCKS = 16
FRAMES = 2


def head_rise(ratio):
    return ratio ** (jnp.arange(HEADS, dtype=jnp.float32) / max(HEADS - 1, 1))


def draw_query_proj(key, part):
    key = jax.random.fold_in(key, 11)
    values = jnp.clip(jax.random.normal(key, (TOKENS, HEADS, HD), jnp.float32), -6.0, 6.0) * head_rise(3.0)[None, :, None]
    return values.reshape(TOKENS, HEADS * HD).astype(jnp.bfloat16)


def draw_key_proj(key, part):
    key = jax.random.fold_in(key, 12)
    values = jnp.clip(jax.random.normal(key, (TOKENS, HEADS, HD), jnp.float32), -6.0, 6.0) * head_rise(3.0)[None, :, None]
    return values.reshape(TOKENS, HEADS * HD).astype(jnp.bfloat16)


def draw_far_blocks(key, part):
    key = jax.random.fold_in(key, 7)
    first_key, second_key = jax.random.split(key)
    row_ids = jnp.arange(QBLOCKS, dtype=jnp.int32)[:, None]
    col_ids = jnp.arange(QBLOCKS, dtype=jnp.int32)[None, :]
    distance = jnp.abs(row_ids - col_ids)
    halvings = jnp.minimum(distance * TOK_DEV // (2 * FRAME_TOK), 20)
    threshold = 800 + jnp.right_shift(jnp.full_like(halvings, 200), halvings)
    rolled = jax.random.randint(first_key, (QBLOCKS, QBLOCKS), 0, 1000, dtype=jnp.int32)
    chosen = jax.random.randint(second_key, (QBLOCKS, QBLOCKS), 0, TOK_DEV // BLK, dtype=jnp.int32)
    taken = (rolled < threshold) & (distance > 1)
    return jnp.where(taken, chosen, -1).astype(jnp.int32)


def level_of(own_key, extent, shards, low, top_value):
    loudness, own = 1.0, jax.random.fold_in(own_key, 6)
    for position, parts in shards:
        heights = jnp.exp(jax.random.uniform(jax.random.fold_in(own, position), (parts,), jnp.float32, low / len(shards), top_value / len(shards)))
        loudness = loudness * jnp.repeat(heights, extent[position] // parts).reshape([-1 if axis == position else 1 for axis in range(len(extent))])
    return loudness


def normal_values(key, extent, scale, reach, pieces=(), kind=jnp.bfloat16):
    values = jax.random.normal(key, extent, jnp.float32) * scale
    if len(pieces) > 0:
        values = level_of(key, extent, pieces, -0.22, 0.18) * values
    return jnp.clip(values, min=-reach, max=reach).astype(kind)


def setup_inputs(seed: int = 0) -> dict:
    key_list = jax.random.split(jax.random.key(seed), 9)
    query_proj = draw_query_proj(jax.random.fold_in(key_list[8], 71), 0)
    key_proj = draw_key_proj(jax.random.fold_in(key_list[8], 71), 0)
    value_proj = normal_values(key_list[2], (TOKENS, HEADS * HD), 2.0, 12.0, ((0, 16), (1, 2)))
    query_gain = jnp.clip(1.0 + 0.15 * jax.random.normal(key_list[3], (HEADS * HD,), jnp.float32), 0.25, 1.75)
    key_gain = jnp.clip(1.0 + 0.15 * jax.random.normal(key_list[4], (HEADS * HD,), jnp.float32), 0.25, 1.75)
    gate_table = jnp.clip(0.5 + 1.5 * jax.random.uniform(key_list[5], (STEPS, HEADS * HD), jnp.float32) ** level_of(key_list[5], (STEPS, HEADS * HD), ((1, 2),), -0.2, 0.2), 0.5, 2.0)
    frame_step = jax.random.randint(key_list[6], (FRAMES,), 0, STEPS).astype(jnp.int32)
    far_blocks = draw_far_blocks(jax.random.fold_in(key_list[8], 71), 0)
    return {"query_proj": query_proj, "key_proj": key_proj, "value_proj": value_proj, "query_gain": query_gain, "key_gain": key_gain, "gate_table": gate_table, "frame_step": frame_step, "far_blocks": far_blocks}


def normed(source, gain):
    source_f = source.astype(jnp.float32)
    mean_sq = lax.optimization_barrier(jnp.mean(source_f * source_f, axis=-1, keepdims=True))
    return (source_f * lax.rsqrt(mean_sq + 1e-06) * gain).astype(jnp.bfloat16)

def reference(query_proj, key_proj, value_proj, query_gain, key_gain, gate_table, frame_step, far_blocks):
    feat_width = HEADS * HD
    block_count = TOK_DEV // BLK
    query_norm = normed(query_proj, query_gain)
    key_norm = normed(key_proj, key_gain)
    padded_keys = jnp.pad(key_norm, ((TOK_DEV, TOK_DEV), (0, 0)))
    padded_values = jnp.pad(value_proj, ((TOK_DEV, TOK_DEV), (0, 0)))
    key_blocks = key_norm.reshape(QBLOCKS, block_count, BLK, feat_width)
    value_blocks = value_proj.reshape(QBLOCKS, block_count, BLK, feat_width)
    segment = jnp.arange(3 * TOK_DEV, dtype=jnp.int32) // TOK_DEV
    owners = jnp.arange(QBLOCKS, dtype=jnp.int32)
    score_scale = HD ** (-0.5)

    def one_block(block_id):
        start = (block_id * TOK_DEV).astype(jnp.int32)
        query_rows = lax.dynamic_slice_in_dim(query_norm, start, TOK_DEV, 0)
        band_keys = lax.dynamic_slice_in_dim(padded_keys, start, 3 * TOK_DEV, 0)
        band_values = lax.dynamic_slice_in_dim(padded_values, start, 3 * TOK_DEV, 0)
        band_mask = (segment == 1) | (segment == 0) & (block_id > 0) | (segment == 2) & (block_id < QBLOCKS - 1)
        chosen = far_blocks[block_id]
        picked = jnp.maximum(chosen, 0).astype(jnp.int32)
        far_keys = key_blocks[owners, picked].reshape(QBLOCKS * BLK, feat_width)
        far_values = value_blocks[owners, picked].reshape(QBLOCKS * BLK, feat_width)
        far_mask = jnp.repeat(chosen >= 0, BLK)
        all_keys = jnp.concatenate([band_keys, far_keys], axis=0)
        all_values = jnp.concatenate([band_values, far_values], axis=0)
        key_mask = jnp.concatenate([band_mask, far_mask], axis=0)
        query_heads = query_rows.astype(jnp.float32).reshape(TOK_DEV, HEADS, HD)
        key_heads = all_keys.astype(jnp.float32).reshape(-1, HEADS, HD)
        value_heads = all_values.astype(jnp.float32).reshape(-1, HEADS, HD)
        scores = jnp.einsum('qhd,khd->hqk', query_heads, key_heads) * score_scale
        scores = jnp.where(key_mask[None, None, :], scores, -jnp.inf)
        row_max = lax.optimization_barrier(jnp.max(scores, axis=-1, keepdims=True))
        weights = jnp.exp(scores - row_max)
        totals = lax.optimization_barrier(jnp.sum(weights, axis=-1))
        rounded = weights.astype(jnp.bfloat16).astype(jnp.float32)
        context = jnp.einsum('hqk,khd->qhd', rounded, value_heads) / jnp.transpose(totals)[:, :, None]
        positions = start + jnp.arange(TOK_DEV, dtype=jnp.int32)
        steps_here = frame_step[positions // FRAME_TOK]
        gate = gate_table[steps_here]
        return (context.reshape(TOK_DEV, feat_width) * gate).astype(jnp.bfloat16)
    result = lax.map(one_block, jnp.arange(QBLOCKS, dtype=jnp.int32))
    return result.reshape(TOKENS, feat_width)
```

```python
import functools

import jax
import jax.numpy as jnp
from jax import lax
from jax.experimental import pallas as pl
from jax.experimental.pallas import tpu as pltpu
from jax.sharding import PartitionSpec as P

HD = 128
BLK = 64
FRAME_TOK = 1560
EPSILON = 1e-06
LOG2E = 1.4426950408889634
MASKED = -1e30


def sums_kernel(query_ref, key_ref, out_ref):
    rows = query_ref.shape[0]
    for place, ref in enumerate((query_ref, key_ref)):
        wide = ref[...].astype(jnp.float32)
        out_ref[0:1, place * rows : (place + 1) * rows] = jnp.sum(
            (wide * wide).T, axis=0, keepdims=True
        )


def attention_kernel(
    far_ref,
    step_ref,
    query_ref,
    keys_ref,
    values_ref,
    sums_ref,
    query_gain_ref,
    key_gain_ref,
    gate_ref,
    out_ref,
    key_buf,
    value_buf,
    factor_buf,
):
    rows, width = query_ref.shape
    blocks = keys_ref.shape[0] // rows
    splits = sums_ref.shape[0] // blocks
    heads = width // HD
    full_width = width * splits
    me = lax.axis_index("tm")

    sums = jnp.sum(sums_ref[...].reshape(blocks, splits, 2 * rows), axis=1)
    factors = lax.rsqrt(sums / full_width + EPSILON)
    key_factors = factors[:, rows:]
    pad = -blocks % rows
    if pad:
        key_factors = jnp.concatenate([key_factors, jnp.zeros((pad, rows), jnp.float32)], axis=0)
    factor_buf[...] = key_factors.T[:, :blocks]
    block_ids = lax.broadcasted_iota(jnp.int32, (blocks, rows), 0)
    query_factor = jnp.sum(
        jnp.where(block_ids == me, factors[:, :rows], 0.0), axis=0, keepdims=True
    )
    query_factor = jnp.broadcast_to(query_factor, (rows, rows)).T[:, :1]

    query = (
        query_ref[...].astype(jnp.float32) * query_factor * query_gain_ref[...]
    ).astype(jnp.bfloat16)

    def place_block(slot, start, factor):
        wide = keys_ref[pl.ds(start, BLK), :].astype(jnp.float32)
        key_buf[slot * BLK : (slot + 1) * BLK, :] = (
            wide * factor * key_gain_ref[...]
        ).astype(jnp.bfloat16)
        value_buf[slot * BLK : (slot + 1) * BLK, :] = values_ref[pl.ds(start, BLK), :]

    wanted = []
    for j in range(blocks):
        choice = far_ref[0, j]
        first = jnp.maximum(choice, 0) * BLK
        place_block(
            j,
            pl.multiple_of(j * rows + first, BLK),
            factor_buf[pl.ds(pl.multiple_of(first, BLK), BLK), j : j + 1],
        )
        wanted.append((choice >= 0) | (jnp.abs(me - j) <= 1))
    lanes = lax.broadcasted_iota(jnp.int32, (BLK, blocks), 1)
    for side in range(3):
        near = me + side - 1
        held = jnp.clip(near, 0, blocks - 1)
        factor = jnp.sum(
            jnp.where(lanes == held, factor_buf[BLK:, :], 0.0), axis=1, keepdims=True
        )
        place_block(blocks + side, pl.multiple_of(held * rows + BLK, BLK), factor)
        wanted.append((near >= 0) & (near < blocks))
    slots = len(wanted)
    total = key_buf.shape[0] // BLK
    for slot in range(slots, total):
        key_buf[slot * BLK : (slot + 1) * BLK, :] = jnp.zeros((BLK, width), jnp.bfloat16)
        value_buf[slot * BLK : (slot + 1) * BLK, :] = jnp.zeros((BLK, width), jnp.bfloat16)
        wanted.append(jnp.bool_(False))

    half = lax.broadcasted_iota(jnp.int32, (1, 2 * BLK), 1) < BLK
    bias = jnp.concatenate(
        [
            jnp.where(
                half,
                jnp.where(wanted[2 * pair], 0.0, MASKED),
                jnp.where(wanted[2 * pair + 1], 0.0, MASKED),
            )
            for pair in range(total // 2)
        ],
        axis=1,
    )

    start = me * rows
    first_frame = start // FRAME_TOK
    last_frame = (start + rows - 1) // FRAME_TOK
    row_ids = lax.broadcasted_iota(jnp.int32, (rows, 1), 0)
    gate = jnp.where(
        row_ids < (first_frame + 1) * FRAME_TOK - start,
        gate_ref[pl.ds(step_ref[first_frame], 1), :],
        gate_ref[pl.ds(step_ref[last_frame], 1), :],
    )

    scale = HD ** (-0.5) * LOG2E
    for head in range(heads):
        low, high = head * HD, (head + 1) * HD
        scores = (
            lax.dot_general(
                query[:, low:high],
                key_buf[:, low:high],
                (((1,), (1,)), ((), ())),
                preferred_element_type=jnp.float32,
            )
            * scale
            + bias
        )
        weights = jnp.exp2(scores - jnp.max(scores, axis=1, keepdims=True))
        totals = jnp.sum(weights, axis=1, keepdims=True)
        context = jnp.dot(
            weights.astype(jnp.bfloat16),
            value_buf[:, low:high],
            preferred_element_type=jnp.float32,
        )
        out_ref[:, low:high] = (context / totals * gate[:, low:high]).astype(jnp.bfloat16)


def local(
    query_proj, key_proj, value_proj, query_gain, key_gain, gate_table, frame_step, far_blocks
):
    rows, width = query_proj.shape
    blocks = lax.axis_size("tm")
    smem = pl.BlockSpec(memory_space=pltpu.SMEM)
    vmem = pl.BlockSpec(memory_space=pltpu.VMEM)
    sums = pl.pallas_call(
        sums_kernel,
        out_shape=jax.ShapeDtypeStruct((1, 2 * rows), jnp.float32),
        in_specs=[vmem, vmem],
        out_specs=vmem,
    )(query_proj, key_proj)
    all_sums = lax.all_gather(sums, ("tm", "head"), axis=0, tiled=True)
    all_keys = lax.all_gather(key_proj, "tm", axis=0, tiled=True)
    all_values = lax.all_gather(value_proj, "tm", axis=0, tiled=True)
    slots = blocks + 3
    key_rows = (slots + slots % 2) * BLK
    return pl.pallas_call(
        attention_kernel,
        out_shape=jax.ShapeDtypeStruct((rows, width), jnp.bfloat16),
        in_specs=[smem, smem] + [vmem] * 7,
        out_specs=vmem,
        scratch_shapes=[
            pltpu.VMEM((key_rows, width), jnp.bfloat16),
            pltpu.VMEM((key_rows, width), jnp.bfloat16),
            pltpu.VMEM((rows, blocks), jnp.float32),
        ],
        compiler_params=pltpu.CompilerParams(vmem_limit_bytes=48 * 2**20),
    )(
        far_blocks,
        frame_step,
        query_proj,
        all_keys,
        all_values,
        all_sums,
        query_gain.reshape(1, width),
        key_gain.reshape(1, width),
        gate_table,
    )


def solution(mesh):
    return jax.shard_map(
        local,
        mesh=mesh,
        in_specs=(
            P("tm", "head"),
            P("tm", "head"),
            P("tm", "head"),
            P("head"),
            P("head"),
            P(None, "head"),
            P(),
            P("tm", None),
        ),
        out_specs=P("tm", "head"),
        check_vma=False,
    )
```

```python
import functools

import jax
import jax.numpy as jnp
from jax import lax
from jax.experimental import pallas as pl
from jax.experimental.pallas import tpu as pltpu
from jax.sharding import PartitionSpec as P

HD = 128
BLK = 64
FRAME_TOK = 1560
EPSILON = 1e-06
LOG2E = 1.4426950408889634
MASKED = -1e30
EXTRA = 16
QUERY_MASKS = (0, 2, 4, 6)
ANY = pl.BlockSpec(memory_space=pl.ANY)
VMEM = pl.BlockSpec(memory_space=pltpu.VMEM)


def sums_kernel(query_hbm, key_hbm, out_ref, query_ref, key_ref, sems):
    copies = [
        pltpu.make_async_copy(query_hbm, query_ref, sems.at[0]),
        pltpu.make_async_copy(key_hbm, key_ref, sems.at[1]),
    ]
    for copy in copies:
        copy.start()
    for place, ref in enumerate((query_ref, key_ref)):
        copies[place].wait()
        wide = ref[...].astype(jnp.float32)
        square = wide * wide
        part = square[:, :HD]
        for low in range(HD, square.shape[1], HD):
            part = part + square[:, low : low + HD]
        out_ref[place : place + 1, :] = jnp.sum(part.T, axis=0, keepdims=True)


def norm_kernel(
    full_width,
    query_hbm,
    key_hbm,
    value_hbm,
    query_gain_ref,
    key_gain_ref,
    far_ref,
    own_ref,
    other_ref,
    query_out,
    pair_out,
    query_ref,
    key_ref,
    sems,
):
    rows, width = query_ref.shape
    copies = [
        pltpu.make_async_copy(query_hbm, query_ref, sems.at[0]),
        pltpu.make_async_copy(key_hbm, key_ref, sems.at[1]),
        pltpu.make_async_copy(value_hbm, pair_out.at[rows:, :], sems.at[2]),
    ]
    for copy in copies:
        copy.start()
    factors = lax.rsqrt((own_ref[...] + other_ref[...]) / full_width + EPSILON)
    columns = [
        jnp.broadcast_to(factors[place : place + 1, :], (rows, rows)).T[:, :1]
        for place in range(2)
    ]
    far = far_ref[...].astype(jnp.float32).astype(jnp.bfloat16)
    pad = jnp.zeros((1, HD - far.shape[1]), jnp.bfloat16)
    far = jnp.concatenate([far, pad], axis=1).astype(jnp.float32)
    query_out[rows:, :HD] = jnp.broadcast_to(far, (EXTRA, HD)).astype(jnp.bfloat16)
    query_out[rows:, HD:] = jnp.zeros((EXTRA, width - HD), jnp.bfloat16)
    copies[1].wait()
    pair_out[:rows, :] = (
        key_ref[...].astype(jnp.float32) * columns[1] * key_gain_ref[...]
    ).astype(jnp.bfloat16)
    copies[0].wait()
    query_out[:rows, :] = (
        query_ref[...].astype(jnp.float32) * columns[0] * query_gain_ref[...]
    ).astype(jnp.bfloat16)
    copies[2].wait()


def attention_kernel(key_masks, *refs):
    queries = refs[: len(QUERY_MASKS)]
    pairs = refs[len(QUERY_MASKS) : len(QUERY_MASKS) + len(key_masks)]
    own_out, sums_out, *packets = refs[len(QUERY_MASKS) + len(key_masks) :]
    rows, width = own_out.shape
    heads = width // HD
    me = lax.axis_index("tm")
    lane = lax.broadcasted_iota(jnp.int32, (1, HD), 1)
    half = (lane >= BLK).astype(jnp.float32)
    biases = []
    for query_mask, query_ref in zip(QUERY_MASKS, queries):
        far = query_ref[rows:, :HD].astype(jnp.float32)[:1]
        parts = []
        for key_mask in key_masks:
            query_id, key_id = me ^ query_mask, me ^ key_mask
            choice = jnp.sum(jnp.where(lane == key_id, far, 0.0), axis=1, keepdims=True)
            taken = (choice == half) | (jnp.abs(query_id - key_id) <= 1)
            parts.append(jnp.where(taken, 0.0, MASKED))
        biases.append(jnp.concatenate(parts, axis=1))

    scale = HD ** (-0.5) * LOG2E
    logs = jnp.zeros((rows, HD), jnp.float32)
    for head in range(heads):
        low, high = head * HD, (head + 1) * HD
        keys = jnp.concatenate([pair[:rows, low:high] for pair in pairs], axis=0)
        values = jnp.concatenate([pair[rows:, low:high] for pair in pairs], axis=0)
        for place, query_ref in enumerate(queries):
            scores = (
                lax.dot_general(
                    query_ref[:rows, low:high],
                    keys,
                    (((1,), (1,)), ((), ())),
                    preferred_element_type=jnp.float32,
                )
                * scale
                + biases[place]
            )
            top = jnp.max(scores, axis=1, keepdims=True)
            weights = jnp.exp2(scores - top)
            totals = jnp.sum(weights, axis=1, keepdims=True)
            context = (
                jnp.dot(
                    weights.astype(jnp.bfloat16), values, preferred_element_type=jnp.float32
                )
                / totals
            )
            logs = jnp.where(lane == place * heads + head, top + jnp.log2(totals), logs)
            if place == 0:
                own_out[:, low:high] = context
            else:
                packets[place - 1][:rows, low:high] = context.astype(jnp.bfloat16)
    rows_form = logs.T
    sub = lax.broadcasted_iota(jnp.int32, (EXTRA, HD), 0)
    for place in range(len(queries)):
        for head in range(heads):
            low, high = head * HD, (head + 1) * HD
            line = place * heads + head
            value = rows_form[line : line + 1, :]
            if place == 0:
                sums_out[:, low:high] = jnp.broadcast_to(value, (8, HD))
            else:
                first = value.astype(jnp.bfloat16).astype(jnp.float32)
                second = (value - first).astype(jnp.bfloat16).astype(jnp.float32)
                third = value - first - second
                packets[place - 1][rows:, low:high] = jnp.where(
                    sub == 0, first, jnp.where(sub == 1, second, third)
                ).astype(jnp.bfloat16)


def merge_kernel(own_ref, sums_ref, *refs):
    *packets, gate_ref, out_ref = refs
    rows, width = own_ref.shape
    heads = width // HD
    logs = [sums_ref[:1, :]]
    for packet in packets:
        pieces = packet[rows:, :].astype(jnp.float32)
        logs.append(pieces[0:1] + pieces[1:2] + pieces[2:3])
    top = functools.reduce(jnp.maximum, logs)
    weights = [jnp.exp2(log - top) for log in logs]
    total = sum(weights)
    weights = [weight / total for weight in weights]
    lines = [weight[:, h * HD : (h + 1) * HD] for weight in weights for h in range(heads)]
    lines += [jnp.zeros((1, HD), jnp.float32)] * (-len(lines) % 8)
    columns = jnp.concatenate(lines, axis=0).T
    start = lax.axis_index("tm") * rows
    first_rows = (start // FRAME_TOK + 1) * FRAME_TOK - start
    row_ids = lax.broadcasted_iota(jnp.int32, (rows, 1), 0)
    for head in range(heads):
        low, high = head * HD, (head + 1) * HD
        context = own_ref[:, low:high] * columns[:, head : head + 1]
        for place, packet in enumerate(packets):
            line = (place + 1) * heads + head
            context += packet[:rows, low:high].astype(jnp.float32) * columns[:, line : line + 1]
        gate = jnp.where(
            row_ids < first_rows, gate_ref[0:1, low:high], gate_ref[1:2, low:high]
        )
        out_ref[:, low:high] = (context * gate).astype(jnp.bfloat16)


def exchange(array, mask):
    count = lax.axis_size("tm")
    return lax.ppermute(array, "tm", [(i, i ^ mask) for i in range(count)])


def local(
    query_proj, key_proj, value_proj, query_gain, key_gain, gate_table, frame_step, far_blocks
):
    rows, width = query_proj.shape
    count = lax.axis_size("tm")
    splits = lax.axis_size("head")
    heads = width // HD
    params = pltpu.CompilerParams(vmem_limit_bytes=(8 + count // 4) * 2**20)

    sums = pl.pallas_call(
        sums_kernel,
        out_shape=jax.ShapeDtypeStruct((2, rows), jnp.float32),
        in_specs=[ANY, ANY],
        out_specs=VMEM,
        scratch_shapes=[
            pltpu.VMEM((rows, width), jnp.bfloat16),
            pltpu.VMEM((rows, width), jnp.bfloat16),
            pltpu.SemaphoreType.DMA((2,)),
        ],
        compiler_params=params,
    )(query_proj, key_proj)
    if splits == 2:
        others = lax.ppermute(sums, "head", [(0, 1), (1, 0)])
    else:
        sums = lax.psum(sums, "head")
        others = jnp.zeros_like(sums)

    query_pack, pair_pack = pl.pallas_call(
        functools.partial(norm_kernel, width * splits),
        out_shape=(
            jax.ShapeDtypeStruct((rows + EXTRA, width), jnp.bfloat16),
            jax.ShapeDtypeStruct((2 * rows, width), jnp.bfloat16),
        ),
        in_specs=[ANY, ANY, ANY, VMEM, VMEM, VMEM, VMEM, VMEM],
        out_specs=(VMEM, VMEM),
        scratch_shapes=[
            pltpu.VMEM((rows, width), jnp.bfloat16),
            pltpu.VMEM((rows, width), jnp.bfloat16),
            pltpu.SemaphoreType.DMA((3,)),
        ],
        compiler_params=params,
    )(
        query_proj,
        key_proj,
        value_proj,
        query_gain.reshape(1, width),
        key_gain.reshape(1, width),
        far_blocks,
        sums,
        others,
    )

    pairs = {0: pair_pack}
    key_bits = [1 << bit for bit in range(3, count.bit_length() - 1)] + [1]
    for mask in key_bits:
        for held in list(pairs):
            pairs[held ^ mask] = exchange(pairs[held], mask)
    key_masks = sorted(pairs)
    queries = [query_pack] + [exchange(query_pack, mask) for mask in QUERY_MASKS[1:]]

    partial = pl.pallas_call(
        functools.partial(attention_kernel, key_masks),
        out_shape=[
            jax.ShapeDtypeStruct((rows, width), jnp.float32),
            jax.ShapeDtypeStruct((8, width), jnp.float32),
        ]
        + [jax.ShapeDtypeStruct((rows + EXTRA, width), jnp.bfloat16)] * 3,
        in_specs=[VMEM] * (len(QUERY_MASKS) + len(key_masks)),
        out_specs=[VMEM] * 5,
        compiler_params=params,
    )(*queries, *[pairs[mask] for mask in key_masks])
    own, own_logs, *packets = partial
    packets = [exchange(packet, mask) for packet, mask in zip(packets, QUERY_MASKS[1:])]

    start = lax.axis_index("tm") * rows
    steps = [frame_step[start // FRAME_TOK], frame_step[(start + rows - 1) // FRAME_TOK]]
    gates = jnp.concatenate(
        [lax.dynamic_slice_in_dim(gate_table, step, 1, axis=0) for step in steps], axis=0
    )
    return pl.pallas_call(
        merge_kernel,
        out_shape=jax.ShapeDtypeStruct((rows, width), jnp.bfloat16),
        in_specs=[VMEM] * 6,
        out_specs=VMEM,
        compiler_params=params,
    )(own, own_logs, *packets, gates)


def solution(mesh):
    return jax.shard_map(
        local,
        mesh=mesh,
        in_specs=(
            P("tm", "head"),
            P("tm", "head"),
            P("tm", "head"),
            P("head"),
            P("head"),
            P(None, "head"),
            P(),
            P("tm", None),
        ),
        out_specs=P("tm", "head"),
        check_vma=False,
    )
```

```python
import functools

import jax
import jax.numpy as jnp
from jax import lax
from jax.experimental import pallas as pl
from jax.experimental.pallas import tpu as pltpu
from jax.sharding import PartitionSpec as P

HD = 128
BLK = 64
FRAME_TOK = 1560
EPSILON = 1e-06
LOG2E = 1.4426950408889634
MASKED = -1e30
EXTRA = 16
QUERY_MASKS = (0, 2, 4, 6)
ANY = pl.BlockSpec(memory_space=pl.ANY)
VMEM = pl.BlockSpec(memory_space=pltpu.VMEM)
SMEM = pl.BlockSpec(memory_space=pltpu.SMEM)


def sums_kernel(query_hbm, key_hbm, out_ref, query_ref, key_ref, sems):
    copies = [
        pltpu.make_async_copy(query_hbm, query_ref, sems.at[0]),
        pltpu.make_async_copy(key_hbm, key_ref, sems.at[1]),
    ]
    for copy in copies:
        copy.start()
    for place, ref in enumerate((query_ref, key_ref)):
        copies[place].wait()
        wide = ref[...].astype(jnp.float32)
        square = wide * wide
        part = square[:, :HD]
        for low in range(HD, square.shape[1], HD):
            part = part + square[:, low : low + HD]
        out_ref[place : place + 1, :] = jnp.sum(part.T, axis=0, keepdims=True)


def norm_kernel(
    full_width,
    query_ref,
    key_ref,
    query_gain_ref,
    key_gain_ref,
    far_ref,
    own_ref,
    other_ref,
    query_out,
    key_out,
):
    rows, width = query_ref.shape
    factors = lax.rsqrt((own_ref[...] + other_ref[...]) / full_width + EPSILON)
    columns = [
        jnp.broadcast_to(factors[place : place + 1, :], (rows, rows)).T[:, :1]
        for place in range(2)
    ]
    far = far_ref[...].astype(jnp.float32)
    far = jnp.concatenate([far, jnp.zeros((1, HD - far.shape[1]), jnp.float32)], axis=1)
    query_out[rows:, :HD] = jnp.broadcast_to(far, (EXTRA, HD)).astype(jnp.bfloat16)
    query_out[rows:, HD:] = jnp.zeros((EXTRA, width - HD), jnp.bfloat16)
    key_out[...] = (
        key_ref[...].astype(jnp.float32) * columns[1] * key_gain_ref[...]
    ).astype(jnp.bfloat16)
    query_out[:rows, :] = (
        query_ref[...].astype(jnp.float32) * columns[0] * query_gain_ref[...]
    ).astype(jnp.bfloat16)


def masked_scores(queries, keys, key_masks, low, high, biases):
    rows = keys[0].shape[0]
    scores = lax.dot_general(
        jnp.concatenate([query[:rows, low:high] for query in queries], axis=0),
        jnp.concatenate([key[:, low:high] for key in keys], axis=0),
        (((1,), (1,)), ((), ())),
        preferred_element_type=jnp.float32,
    )
    scale = HD ** (-0.5) * LOG2E
    return [
        scores[place * rows : (place + 1) * rows] * scale + bias
        for place, bias in enumerate(biases)
    ]


def key_biases(queries, key_masks, rows):
    me = lax.axis_index("tm")
    lane = lax.broadcasted_iota(jnp.int32, (1, HD), 1)
    half = (lane >= BLK).astype(jnp.float32)
    biases = []
    for query_mask, query_ref in zip(QUERY_MASKS, queries):
        far = query_ref[rows:, :HD].astype(jnp.float32)[:1]
        parts = []
        for key_mask in key_masks:
            query_id, key_id = me ^ query_mask, me ^ key_mask
            choice = jnp.sum(jnp.where(lane == key_id, far, 0.0), axis=1, keepdims=True)
            taken = (choice == half) | (jnp.abs(query_id - key_id) <= 1)
            parts.append(jnp.where(taken, 0.0, MASKED))
        biases.append(jnp.concatenate(parts, axis=1))
    return biases


def near_kernel(key_masks, step_ref, gate_ref, *refs):
    count, held = len(QUERY_MASKS), len(key_masks)
    queries, keys = refs[:count], refs[count : count + held]
    values = refs[count + held : count + 2 * held]
    context_out, stats_out, gate_out = refs[count + 2 * held :]
    rows, width = keys[0].shape
    start = lax.axis_index("tm") * rows
    first = step_ref[start // FRAME_TOK]
    last = step_ref[(start + rows - 1) // FRAME_TOK]
    gate_out[0:1, :] = gate_ref[pl.ds(first, 1), :]
    gate_out[1:2, :] = gate_ref[pl.ds(last, 1), :]
    biases = key_biases(queries, key_masks, rows)
    lane = lax.broadcasted_iota(jnp.int32, (1, HD), 1)
    stats = [jnp.zeros((rows, HD), jnp.float32)] * count
    for head in range(width // HD):
        low, high = head * HD, (head + 1) * HD
        scores = masked_scores(queries, keys, key_masks, low, high, biases)
        rounded = []
        for place in range(count):
            top = jnp.max(scores[place], axis=1, keepdims=True)
            weights = jnp.exp2(scores[place] - top)
            total = jnp.sum(weights, axis=1, keepdims=True)
            rounded.append(weights.astype(jnp.bfloat16))
            stats[place] = jnp.where(
                lane == 2 * head,
                top,
                jnp.where(lane == 2 * head + 1, total, stats[place]),
            )
        context_out[:, low:high] = jnp.dot(
            jnp.concatenate(rounded, axis=0),
            jnp.concatenate([value[:, low:high] for value in values], axis=0),
            preferred_element_type=jnp.float32,
        )
    for place in range(count):
        stats_out[place * rows : (place + 1) * rows, :] = stats[place]


def far_kernel(key_masks, *refs):
    count, held = len(QUERY_MASKS), len(key_masks)
    queries, keys = refs[:count], refs[count : count + held]
    values = refs[count + held : count + 2 * held]
    context_ref, stats_ref, own_out, sums_out, *packets = refs[count + 2 * held :]
    rows, width = own_out.shape
    heads = width // HD
    biases = key_biases(queries, key_masks, rows)
    lane = lax.broadcasted_iota(jnp.int32, (1, HD), 1)
    logs = jnp.zeros((rows, HD), jnp.float32)
    for head in range(heads):
        low, high = head * HD, (head + 1) * HD
        scores = masked_scores(queries, keys, key_masks, low, high, biases)
        rounded, totals, fades = [], [], []
        for place in range(count):
            part = slice(place * rows, (place + 1) * rows)
            old_top = stats_ref[part, 2 * head : 2 * head + 1]
            old_total = stats_ref[part, 2 * head + 1 : 2 * head + 2]
            top = jnp.maximum(old_top, jnp.max(scores[place], axis=1, keepdims=True))
            weights = jnp.exp2(scores[place] - top)
            fade = jnp.exp2(old_top - top)
            total = old_total * fade + jnp.sum(weights, axis=1, keepdims=True)
            rounded.append(weights.astype(jnp.bfloat16))
            totals.append(total)
            fades.append(fade)
            logs = jnp.where(lane == place * heads + head, top + jnp.log2(total), logs)
        added = jnp.dot(
            jnp.concatenate(rounded, axis=0),
            jnp.concatenate([value[:, low:high] for value in values], axis=0),
            preferred_element_type=jnp.float32,
        )
        for place in range(count):
            part = slice(place * rows, (place + 1) * rows)
            context = (context_ref[part, low:high] * fades[place] + added[part]) / totals[place]
            if place == 0:
                own_out[:, low:high] = context
            else:
                packets[place - 1][:rows, low:high] = context.astype(jnp.bfloat16)
    rows_form = logs.T
    sub = lax.broadcasted_iota(jnp.int32, (EXTRA, HD), 0)
    for place in range(count):
        for head in range(heads):
            low, high = head * HD, (head + 1) * HD
            line = place * heads + head
            value = rows_form[line : line + 1, :]
            if place == 0:
                sums_out[:, low:high] = jnp.broadcast_to(value, (8, HD))
            else:
                first = value.astype(jnp.bfloat16).astype(jnp.float32)
                second = (value - first).astype(jnp.bfloat16).astype(jnp.float32)
                third = value - first - second
                packets[place - 1][rows:, low:high] = jnp.where(
                    sub == 0, first, jnp.where(sub == 1, second, third)
                ).astype(jnp.bfloat16)


def merge_kernel(own_ref, sums_ref, *refs):
    *packets, gate_ref, out_ref = refs
    rows, width = own_ref.shape
    heads = width // HD
    logs = [sums_ref[:1, :]]
    for packet in packets:
        pieces = packet[rows:, :].astype(jnp.float32)
        logs.append(pieces[0:1] + pieces[1:2] + pieces[2:3])
    top = functools.reduce(jnp.maximum, logs)
    weights = [jnp.exp2(log - top) for log in logs]
    total = sum(weights)
    weights = [weight / total for weight in weights]
    lines = [weight[:, h * HD : (h + 1) * HD] for weight in weights for h in range(heads)]
    lines += [jnp.zeros((1, HD), jnp.float32)] * (-len(lines) % 8)
    columns = jnp.concatenate(lines, axis=0).T
    start = lax.axis_index("tm") * rows
    first_rows = (start // FRAME_TOK + 1) * FRAME_TOK - start
    row_ids = lax.broadcasted_iota(jnp.int32, (rows, 1), 0)
    for head in range(heads):
        low, high = head * HD, (head + 1) * HD
        context = own_ref[:, low:high] * columns[:, head : head + 1]
        for place, packet in enumerate(packets):
            line = (place + 1) * heads + head
            context += packet[:rows, low:high].astype(jnp.float32) * columns[:, line : line + 1]
        gate = jnp.where(
            row_ids < first_rows, gate_ref[0:1, low:high], gate_ref[1:2, low:high]
        )
        out_ref[:, low:high] = (context * gate).astype(jnp.bfloat16)


def exchange(array, mask):
    count = lax.axis_size("tm")
    return lax.ppermute(array, "tm", [(i, i ^ mask) for i in range(count)])


def local(
    query_proj, key_proj, value_proj, query_gain, key_gain, gate_table, frame_step, far_blocks
):
    rows, width = query_proj.shape
    count = lax.axis_size("tm")
    splits = lax.axis_size("head")
    params = pltpu.CompilerParams(vmem_limit_bytes=(8 + count // 4) * 2**20)
    far_bits = [1 << bit for bit in range(3, count.bit_length() - 1)]

    values = {0: value_proj}
    for mask in far_bits + [1]:
        for held in list(values):
            values[held ^ mask] = exchange(values[held], mask)

    sums = pl.pallas_call(
        sums_kernel,
        out_shape=jax.ShapeDtypeStruct((2, rows), jnp.float32),
        in_specs=[ANY, ANY],
        out_specs=VMEM,
        scratch_shapes=[
            pltpu.VMEM((rows, width), jnp.bfloat16),
            pltpu.VMEM((rows, width), jnp.bfloat16),
            pltpu.SemaphoreType.DMA((2,)),
        ],
    )(query_proj, key_proj)
    if splits == 2:
        others = lax.ppermute(sums, "head", [(0, 1), (1, 0)])
    else:
        sums = lax.psum(sums, "head")
        others = jnp.zeros_like(sums)

    query_pack, key_norm = pl.pallas_call(
        functools.partial(norm_kernel, width * splits),
        out_shape=(
            jax.ShapeDtypeStruct((rows + EXTRA, width), jnp.bfloat16),
            jax.ShapeDtypeStruct((rows, width), jnp.bfloat16),
        ),
        in_specs=[VMEM] * 7,
        out_specs=(VMEM, VMEM),
        compiler_params=params,
    )(
        query_proj,
        key_proj,
        query_gain.reshape(1, width),
        key_gain.reshape(1, width),
        far_blocks,
        sums,
        others,
    )

    keys = {0: key_norm}
    for mask in far_bits + [1]:
        for held in list(keys):
            keys[held ^ mask] = exchange(keys[held], mask)
    queries = [query_pack] + [exchange(query_pack, mask) for mask in QUERY_MASKS[1:]]
    near = [0, 1]
    far = [mask for mask in sorted(keys) if mask not in near]

    stacked = len(QUERY_MASKS) * rows
    context, stats, gates = pl.pallas_call(
        functools.partial(near_kernel, near),
        out_shape=[
            jax.ShapeDtypeStruct((stacked, width), jnp.float32),
            jax.ShapeDtypeStruct((stacked, HD), jnp.float32),
            jax.ShapeDtypeStruct((8, width), jnp.float32),
        ],
        in_specs=[SMEM] + [VMEM] * (1 + len(QUERY_MASKS) + 2 * len(near)),
        out_specs=[VMEM] * 3,
        compiler_params=params,
        cost_estimate=pl.CostEstimate(
            flops=4 * stacked * len(near) * rows * width,
            bytes_accessed=8 * 2**20,
            transcendentals=0,
        ),
    )(
        frame_step,
        gate_table,
        *queries,
        *[keys[mask] for mask in near],
        *[values[mask] for mask in near],
    )

    own, own_logs, *packets = pl.pallas_call(
        functools.partial(far_kernel, far),
        out_shape=[
            jax.ShapeDtypeStruct((rows, width), jnp.float32),
            jax.ShapeDtypeStruct((8, width), jnp.float32),
        ]
        + [jax.ShapeDtypeStruct((rows + EXTRA, width), jnp.bfloat16)] * 3,
        in_specs=[VMEM] * (len(QUERY_MASKS) + 2 * len(far) + 2),
        out_specs=[VMEM] * 5,
        compiler_params=params,
    )(
        *queries,
        *[keys[mask] for mask in far],
        *[values[mask] for mask in far],
        context,
        stats,
    )
    packets = [exchange(packet, mask) for packet, mask in zip(packets, QUERY_MASKS[1:])]

    return pl.pallas_call(
        merge_kernel,
        out_shape=jax.ShapeDtypeStruct((rows, width), jnp.bfloat16),
        in_specs=[VMEM] * 6,
        out_specs=VMEM,
        compiler_params=params,
    )(own, own_logs, *packets, gates)


def solution(mesh):
    return jax.shard_map(
        local,
        mesh=mesh,
        in_specs=(
            P("tm", "head"),
            P("tm", "head"),
            P("tm", "head"),
            P("head"),
            P("head"),
            P(None, "head"),
            P(),
            P("tm", None),
        ),
        out_specs=P("tm", "head"),
        check_vma=False,
    )
```

```python
import functools

import jax
import jax.numpy as jnp
from jax import lax
from jax.experimental import pallas as pl
from jax.experimental.pallas import tpu as pltpu
from jax.sharding import PartitionSpec as P

HD = 128
BLK = 64
FRAME_TOK = 1560
EPSILON = 1e-06
LOG2E = 1.4426950408889634
SCALE = HD ** (-0.5) * LOG2E
MASKED = -1e30
EXTRA = 16
ANY = pl.BlockSpec(memory_space=pl.ANY)
VMEM = pl.BlockSpec(memory_space=pltpu.VMEM)
SMEM = pl.BlockSpec(memory_space=pltpu.SMEM)


def spread(row):
    return jnp.broadcast_to(row, (row.shape[1], row.shape[1])).T


def squares(source_ref):
    wide = source_ref[...].astype(jnp.float32)
    square = wide * wide
    part = square[:, :HD]
    for low in range(HD, square.shape[1], HD):
        part = part + square[:, low : low + HD]
    return jnp.sum(part.T, axis=0, keepdims=True)


def own_sums_kernel(query_hbm, key_hbm, out_ref, query_ref, key_ref, sems):
    copies = [
        pltpu.make_async_copy(query_hbm, query_ref, sems.at[0]),
        pltpu.make_async_copy(key_hbm, key_ref, sems.at[1]),
    ]
    for copy in copies:
        copy.start()
    out_ref[...] = jnp.zeros_like(out_ref)
    for place, ref in enumerate((query_ref, key_ref)):
        copies[place].wait()
        out_ref[place : place + 1, :] = squares(ref)


def sums_kernel(own_ref, *refs):
    *sources, out_ref = refs
    out_ref[...] = jnp.zeros_like(out_ref)
    out_ref[0:2, :] = own_ref[0:2, :]
    for place, source_ref in enumerate(sources, start=2):
        out_ref[place : place + 1, :] = squares(source_ref)


def normed(source_ref, own_ref, other_ref, line, gain_ref, full_width):
    total = own_ref[line : line + 1, :] + other_ref[line : line + 1, :]
    factor = spread(lax.rsqrt(total / full_width + EPSILON))
    parts = []
    for low in range(0, source_ref.shape[1], HD):
        wide = source_ref[:, low : low + HD].astype(jnp.float32)
        parts.append((wide * factor * gain_ref[:, low : low + HD]).astype(jnp.bfloat16))
    return jnp.concatenate(parts, axis=1)


def pack_kernel(full_width, held, gain_ref, own_ref, other_ref, *refs):
    keys, values, pack_out = refs[:held], refs[held : 2 * held], refs[2 * held]
    rows = keys[0].shape[0]
    for place, key_ref in enumerate(keys):
        pack_out[place * rows : (place + 1) * rows, :] = normed(
            key_ref, own_ref, other_ref, 1 + place + (place > 0), gain_ref, full_width
        )
    for place, value_ref in enumerate(values, start=held):
        pack_out[place * rows : (place + 1) * rows, :] = value_ref[...]


def key_bias(far_ref, query_mask, key_masks):
    me = lax.axis_index("tm")
    lane = lax.broadcasted_iota(jnp.int32, (1, HD), 1)
    half = (lane >= BLK).astype(jnp.float32)
    far = far_ref[...].astype(jnp.float32)
    far = jnp.concatenate([far, jnp.full((1, HD - far.shape[1]), -1.0)], axis=1)
    parts = []
    for key_mask in key_masks:
        query_id, key_id = me ^ query_mask, me ^ key_mask
        choice = jnp.sum(jnp.where(lane == key_id, far, 0.0), axis=1, keepdims=True)
        taken = (choice == half) | (jnp.abs(query_id - key_id) <= 1)
        parts.append(jnp.where(taken, 0.0, MASKED))
    return jnp.concatenate(parts, axis=1)


def columns_of(pack, second, low, high):
    half = pack.shape[0] // 2
    return pack[half * second : half * (second + 1), low:high]


def absorb(query, keys, values, bias, old):
    rows = query.shape[0]
    logits = (
        lax.dot_general(
            query, keys, (((1,), (1,)), ((), ())), preferred_element_type=jnp.float32
        )
        * SCALE
        + bias
    )
    top = jnp.broadcast_to(jnp.max(logits, axis=1, keepdims=True), (rows, HD))
    if old is not None:
        top = jnp.maximum(top, old[0])
    weights = [
        jnp.exp2(logits[:, left : left + HD] - top) for left in range(0, logits.shape[1], HD)
    ]
    total = jnp.sum(functools.reduce(jnp.add, weights), axis=1, keepdims=True)
    total = jnp.broadcast_to(total, (rows, HD))
    context = jnp.dot(
        jnp.concatenate([weight.astype(jnp.bfloat16) for weight in weights], axis=1),
        values,
        preferred_element_type=jnp.float32,
    )
    if old is not None:
        fade = jnp.exp2(old[0] - top)
        total = total + old[1] * fade
        context = context + old[2] * fade
    return top, total, context


def own_attention(full_width, query_masks, key_masks, gain_ref, own_ref, other_ref, *refs):
    queries, far, pack = refs[:2], refs[2:4], refs[4]
    query_out, context_out, stats_out = refs[5:]
    rows, width = queries[0].shape
    for place, mask in enumerate(query_masks):
        part = slice(place * rows, (place + 1) * rows)
        bias = key_bias(far[place], mask, key_masks)
        query = normed(queries[place], own_ref, other_ref, 2 * place, gain_ref, full_width)
        query_out[part, :] = query
        for low in range(0, width, HD):
            high, wide = low + HD, 2 * low
            top, total, context = absorb(
                query[:, low:high],
                columns_of(pack, 0, low, high),
                columns_of(pack, 1, low, high),
                bias,
                None,
            )
            context_out[part, low:high] = context
            stats_out[part, wide : wide + HD] = top
            stats_out[part, wide + HD : wide + 2 * HD] = total


def last_attention(place, query_mask, key_masks, query_ref, far_ref, *refs):
    pack, context_ref, stats_ref, *outs = refs
    rows, width = query_ref.shape[0] // 2, query_ref.shape[1]
    heads = width // HD
    part = slice(place * rows, (place + 1) * rows)
    bias = key_bias(far_ref, query_mask, key_masks)
    lane = lax.broadcasted_iota(jnp.int32, (1, HD), 1)
    logs = jnp.zeros((rows, HD), jnp.float32)
    for head in range(heads):
        low, high = head * HD, (head + 1) * HD
        wide = 2 * low
        top, total, context = absorb(
            query_ref[part, low:high],
            columns_of(pack, 0, low, high),
            columns_of(pack, 1, low, high),
            bias,
            (
                stats_ref[part, wide : wide + HD],
                stats_ref[part, wide + HD : wide + 2 * HD],
                context_ref[part, low:high],
            ),
        )
        outs[0][:rows, low:high] = (context * (1.0 / total)).astype(outs[0].dtype)
        logs = jnp.where(lane == head, top + jnp.log2(total), logs)
    lines = logs.T
    sub = lax.broadcasted_iota(jnp.int32, (EXTRA, HD), 0)
    for head in range(heads):
        low, high = head * HD, (head + 1) * HD
        value = lines[head : head + 1, :]
        if place == 0:
            outs[1][:, low:high] = jnp.broadcast_to(value, (8, HD))
        else:
            first = value.astype(jnp.bfloat16).astype(jnp.float32)
            second = (value - first).astype(jnp.bfloat16).astype(jnp.float32)
            third = value - first - second
            outs[0][rows:, low:high] = jnp.where(
                sub == 0, first, jnp.where(sub == 1, second, third)
            ).astype(jnp.bfloat16)


def gate_kernel(step_ref, table_ref, out_ref):
    rows = out_ref.shape[0] // 2
    start = lax.axis_index("tm") * HD
    first = step_ref[start // FRAME_TOK]
    last = step_ref[(start + HD - 1) // FRAME_TOK]
    out_ref[:rows, :] = jnp.broadcast_to(table_ref[pl.ds(first, 1), :], (rows, out_ref.shape[1]))
    out_ref[rows:, :] = jnp.broadcast_to(table_ref[pl.ds(last, 1), :], (rows, out_ref.shape[1]))


def merge_kernel(own_ref, logs_ref, packet_ref, gate_ref, out_ref):
    rows, width = own_ref.shape
    pieces = packet_ref[rows:, :].astype(jnp.float32)
    other = pieces[0:1] + pieces[1:2] + pieces[2:3]
    top = jnp.maximum(logs_ref[:1, :], other)
    own_weight = jnp.exp2(logs_ref[:1, :] - top)
    other_weight = jnp.exp2(other - top)
    share = own_weight / (own_weight + other_weight)
    start = lax.axis_index("tm") * rows
    first_rows = (start // FRAME_TOK + 1) * FRAME_TOK - start
    row_ids = lax.broadcasted_iota(jnp.int32, (rows, 1), 0)
    for low in range(0, width, HD):
        high = low + HD
        column = spread(share[:, low:high])
        other_part = packet_ref[:rows, low:high].astype(jnp.float32)
        context = own_ref[:, low:high] * column + other_part * (1.0 - column)
        gate = jnp.where(
            row_ids < first_rows, gate_ref[0:1, low:high], gate_ref[8:9, low:high]
        )
        out_ref[:, low:high] = (context * gate).astype(jnp.bfloat16)


def exchange(array, mask):
    count = lax.axis_size("tm")
    return lax.ppermute(array, "tm", [(i, i ^ mask) for i in range(count)])


def gathered(array, bits):
    held = {0: array}
    for bit in bits:
        for mask in list(held):
            held[mask ^ bit] = exchange(held[mask], bit)
    return held


def local(
    query_proj, key_proj, value_proj, query_gain, key_gain, gate_table, frame_step, far_blocks
):
    rows, width = query_proj.shape
    count = lax.axis_size("tm")
    splits = lax.axis_size("head")
    full_width = width * splits
    params = pltpu.CompilerParams(vmem_limit_bytes=(8 + count // 2) * 2**20)
    bits = [1 << place for place in range(1, count.bit_length() - 2)]
    query_mask = count // 2
    query_gain = query_gain.reshape(1, width)
    key_gain = key_gain.reshape(1, width)

    keys = gathered(key_proj, bits[::-1])
    values = gathered(value_proj, bits)
    queries = [query_proj, exchange(query_proj, query_mask)]
    far = [far_blocks, exchange(far_blocks, query_mask)]
    masks = sorted(keys, key=lambda mask: (mask.bit_count(), mask))

    own_sums = pl.pallas_call(
        own_sums_kernel,
        out_shape=jax.ShapeDtypeStruct((8, rows), jnp.float32),
        in_specs=[ANY, ANY],
        out_specs=VMEM,
        scratch_shapes=[
            pltpu.VMEM((rows, width), jnp.bfloat16),
            pltpu.VMEM((rows, width), jnp.bfloat16),
            pltpu.SemaphoreType.DMA((2,)),
        ],
    )(query_proj, key_proj)
    sources = queries[1:] + [keys[mask] for mask in masks[1:]]
    lines = len(sources) + 2
    sums = pl.pallas_call(
        sums_kernel,
        out_shape=jax.ShapeDtypeStruct((lines + -lines % 8, rows), jnp.float32),
        in_specs=[VMEM] * (1 + len(sources)),
        out_specs=VMEM,
        compiler_params=params,
    )(own_sums, *sources)
    if splits == 2:
        others = lax.ppermute(sums, "head", [(0, 1), (1, 0)])
    else:
        sums = lax.psum(sums, "head")
        others = jnp.zeros_like(sums)

    pack = pl.pallas_call(
        functools.partial(pack_kernel, full_width, len(masks)),
        out_shape=jax.ShapeDtypeStruct((2 * len(masks) * rows, width), jnp.bfloat16),
        in_specs=[VMEM] * (3 + 2 * len(masks)),
        out_specs=VMEM,
        compiler_params=params,
    )(
        key_gain,
        sums,
        others,
        *[keys[mask] for mask in masks],
        *[values[mask] for mask in masks],
    )
    other_pack = exchange(pack, 1)

    query_norm, context, stats = pl.pallas_call(
        functools.partial(own_attention, full_width, [0, query_mask], masks),
        out_shape=[
            jax.ShapeDtypeStruct((2 * rows, width), jnp.bfloat16),
            jax.ShapeDtypeStruct((2 * rows, width), jnp.float32),
            jax.ShapeDtypeStruct((2 * rows, 2 * width), jnp.float32),
        ],
        in_specs=[VMEM] * 8,
        out_specs=[VMEM] * 3,
        compiler_params=params,
    )(query_gain, sums, others, *queries, *far, pack)

    def last_part(place, out_shape):
        return pl.pallas_call(
            functools.partial(
                last_attention, place, place * query_mask, [mask ^ 1 for mask in masks]
            ),
            out_shape=out_shape,
            in_specs=[VMEM] * 5,
            out_specs=[VMEM] * len(out_shape),
            compiler_params=params,
        )(query_norm, far[place], other_pack, context, stats)

    (packet,) = last_part(1, [jax.ShapeDtypeStruct((rows + EXTRA, width), jnp.bfloat16)])
    own, own_logs = last_part(
        0,
        [
            jax.ShapeDtypeStruct((rows, width), jnp.float32),
            jax.ShapeDtypeStruct((8, width), jnp.float32),
        ],
    )
    gates = pl.pallas_call(
        gate_kernel,
        out_shape=jax.ShapeDtypeStruct((16, width), jnp.float32),
        in_specs=[SMEM, VMEM],
        out_specs=VMEM,
        compiler_params=params,
    )(frame_step, gate_table)
    packet = exchange(packet, query_mask)

    return pl.pallas_call(
        merge_kernel,
        out_shape=jax.ShapeDtypeStruct((rows, width), jnp.bfloat16),
        in_specs=[VMEM] * 4,
        out_specs=VMEM,
        compiler_params=params,
    )(own, own_logs, packet, gates)


def solution(mesh):
    return jax.shard_map(
        local,
        mesh=mesh,
        in_specs=(
            P("tm", "head"),
            P("tm", "head"),
            P("tm", "head"),
            P("head"),
            P("head"),
            P(None, "head"),
            P(),
            P("tm", None),
        ),
        out_specs=P("tm", "head"),
        check_vma=False,
    )
```

```python
import functools

import jax
import jax.numpy as jnp
from jax import lax
from jax.experimental import pallas as pl
from jax.experimental.pallas import tpu as pltpu
from jax.sharding import PartitionSpec as P

HD = 128
BLK = 64
FRAME_TOK = 1560
EPSILON = 1e-06
LOG2E = 1.4426950408889634
SCALE = HD ** (-0.5) * LOG2E
MASKED = -1e30
EXTRA = 16
ANY = pl.BlockSpec(memory_space=pl.ANY)
VMEM = pl.BlockSpec(memory_space=pltpu.VMEM)
SMEM = pl.BlockSpec(memory_space=pltpu.SMEM)


def spread(row):
    return jnp.broadcast_to(row, (row.shape[1], row.shape[1])).T


def squares(source_ref):
    wide = source_ref[:HD, :].astype(jnp.float32)
    square = wide * wide
    part = square[:, :HD]
    for low in range(HD, square.shape[1], HD):
        part = part + square[:, low : low + HD]
    return jnp.sum(part.T, axis=0, keepdims=True)


def own_kernel(query_hbm, key_hbm, far_ref, query_out, key_out, sums_out, query_ref, sems):
    rows, width = query_ref.shape
    copies = [
        pltpu.make_async_copy(query_hbm, query_ref, sems.at[0]),
        pltpu.make_async_copy(key_hbm, key_out, sems.at[1]),
    ]
    for copy in copies:
        copy.start()
    far = far_ref[...].astype(jnp.float32)
    far = jnp.concatenate([far, jnp.full((1, HD - far.shape[1]), -1.0)], axis=1)
    query_out[rows:, :HD] = jnp.broadcast_to(far, (EXTRA, HD)).astype(jnp.bfloat16)
    query_out[rows:, HD:] = jnp.zeros((EXTRA, width - HD), jnp.bfloat16)
    sums_out[...] = jnp.zeros_like(sums_out)
    copies[0].wait()
    query_out[:rows, :] = query_ref[...]
    sums_out[0:1, :] = squares(query_ref)
    copies[1].wait()
    sums_out[1:2, :] = squares(key_out)


def sums_kernel(own_ref, *refs):
    *sources, out_ref = refs
    out_ref[...] = jnp.zeros_like(out_ref)
    out_ref[0:2, :] = own_ref[0:2, :]
    for place, source_ref in enumerate(sources, start=2):
        out_ref[place : place + 1, :] = squares(source_ref)


def normed(source_ref, own_ref, other_ref, line, gain_ref, full_width):
    total = own_ref[line : line + 1, :] + other_ref[line : line + 1, :]
    factor = spread(lax.rsqrt(total / full_width + EPSILON))
    parts = []
    for low in range(0, source_ref.shape[1], HD):
        wide = source_ref[:HD, low : low + HD].astype(jnp.float32)
        parts.append((wide * factor * gain_ref[:, low : low + HD]).astype(jnp.bfloat16))
    return jnp.concatenate(parts, axis=1)


def pack_kernel(full_width, held, gain_ref, own_ref, other_ref, *refs):
    keys, values, pack_out = refs[:held], refs[held : 2 * held], refs[2 * held]
    rows = keys[0].shape[0]
    for place, key_ref in enumerate(keys):
        pack_out[place * rows : (place + 1) * rows, :] = normed(
            key_ref, own_ref, other_ref, 1 + place + (place > 0), gain_ref, full_width
        )
    for place, value_ref in enumerate(values, start=held):
        pack_out[place * rows : (place + 1) * rows, :] = value_ref[...]


def key_bias(query_ref, query_mask, key_masks):
    me = lax.axis_index("tm")
    lane = lax.broadcasted_iota(jnp.int32, (1, HD), 1)
    half = (lane >= BLK).astype(jnp.float32)
    far = query_ref[HD:, :HD].astype(jnp.float32)[:1]
    parts = []
    for key_mask in key_masks:
        query_id, key_id = me ^ query_mask, me ^ key_mask
        choice = jnp.sum(jnp.where(lane == key_id, far, 0.0), axis=1, keepdims=True)
        taken = (choice == half) | (jnp.abs(query_id - key_id) <= 1)
        parts.append(jnp.where(taken, 0.0, MASKED))
    return jnp.concatenate(parts, axis=1)


def columns_of(pack, second, low, high):
    half = pack.shape[0] // 2
    return pack[half * second : half * (second + 1), low:high]


def absorb(query, keys, values, bias, old):
    rows = query.shape[0]
    logits = (
        lax.dot_general(
            query, keys, (((1,), (1,)), ((), ())), preferred_element_type=jnp.float32
        )
        * SCALE
        + bias
    )
    top = jnp.broadcast_to(jnp.max(logits, axis=1, keepdims=True), (rows, HD))
    if old is not None:
        top = jnp.maximum(top, old[0])
    weights = [
        jnp.exp2(logits[:, left : left + HD] - top) for left in range(0, logits.shape[1], HD)
    ]
    total = jnp.sum(functools.reduce(jnp.add, weights), axis=1, keepdims=True)
    total = jnp.broadcast_to(total, (rows, HD))
    context = jnp.dot(
        jnp.concatenate([weight.astype(jnp.bfloat16) for weight in weights], axis=1),
        values,
        preferred_element_type=jnp.float32,
    )
    if old is not None:
        fade = jnp.exp2(old[0] - top)
        total = total + old[1] * fade
        context = context + old[2] * fade
    return top, total, context


def own_attention(full_width, query_masks, key_masks, gain_ref, own_ref, other_ref, *refs):
    queries, pack = refs[:2], refs[2]
    query_out, context_out, stats_out = refs[3:]
    rows, width = query_out.shape[0] // 2, query_out.shape[1]
    for place, mask in enumerate(query_masks):
        part = slice(place * rows, (place + 1) * rows)
        bias = key_bias(queries[place], mask, key_masks)
        query = normed(queries[place], own_ref, other_ref, 2 * place, gain_ref, full_width)
        query_out[part, :] = query
        for low in range(0, width, HD):
            high, wide = low + HD, 2 * low
            top, total, context = absorb(
                query[:, low:high],
                columns_of(pack, 0, low, high),
                columns_of(pack, 1, low, high),
                bias,
                None,
            )
            context_out[part, low:high] = context
            stats_out[part, wide : wide + HD] = top
            stats_out[part, wide + HD : wide + 2 * HD] = total


def last_attention(place, query_mask, key_masks, query_ref, raw_ref, *refs):
    pack, context_ref, stats_ref, *outs = refs
    rows, width = query_ref.shape[0] // 2, query_ref.shape[1]
    heads = width // HD
    part = slice(place * rows, (place + 1) * rows)
    bias = key_bias(raw_ref, query_mask, key_masks)
    lane = lax.broadcasted_iota(jnp.int32, (1, HD), 1)
    logs = jnp.zeros((rows, HD), jnp.float32)
    for head in range(heads):
        low, high = head * HD, (head + 1) * HD
        wide = 2 * low
        top, total, context = absorb(
            query_ref[part, low:high],
            columns_of(pack, 0, low, high),
            columns_of(pack, 1, low, high),
            bias,
            (
                stats_ref[part, wide : wide + HD],
                stats_ref[part, wide + HD : wide + 2 * HD],
                context_ref[part, low:high],
            ),
        )
        outs[0][:rows, low:high] = (context * (1.0 / total)).astype(outs[0].dtype)
        logs = jnp.where(lane == head, top + jnp.log2(total), logs)
    lines = logs.T
    sub = lax.broadcasted_iota(jnp.int32, (EXTRA, HD), 0)
    for head in range(heads):
        low, high = head * HD, (head + 1) * HD
        value = lines[head : head + 1, :]
        if place == 0:
            outs[1][:, low:high] = jnp.broadcast_to(value, (8, HD))
        else:
            first = value.astype(jnp.bfloat16).astype(jnp.float32)
            second = (value - first).astype(jnp.bfloat16).astype(jnp.float32)
            third = value - first - second
            outs[0][rows:, low:high] = jnp.where(
                sub == 0, first, jnp.where(sub == 1, second, third)
            ).astype(jnp.bfloat16)


def gate_kernel(step_ref, table_ref, out_ref):
    rows = out_ref.shape[0] // 2
    start = lax.axis_index("tm") * HD
    first = step_ref[start // FRAME_TOK]
    last = step_ref[(start + HD - 1) // FRAME_TOK]
    out_ref[:rows, :] = jnp.broadcast_to(table_ref[pl.ds(first, 1), :], (rows, out_ref.shape[1]))
    out_ref[rows:, :] = jnp.broadcast_to(table_ref[pl.ds(last, 1), :], (rows, out_ref.shape[1]))


def merge_kernel(own_ref, logs_ref, packet_ref, gate_ref, out_ref):
    rows, width = own_ref.shape
    pieces = packet_ref[rows:, :].astype(jnp.float32)
    other = pieces[0:1] + pieces[1:2] + pieces[2:3]
    top = jnp.maximum(logs_ref[:1, :], other)
    own_weight = jnp.exp2(logs_ref[:1, :] - top)
    other_weight = jnp.exp2(other - top)
    share = own_weight / (own_weight + other_weight)
    start = lax.axis_index("tm") * rows
    first_rows = (start // FRAME_TOK + 1) * FRAME_TOK - start
    row_ids = lax.broadcasted_iota(jnp.int32, (rows, 1), 0)
    for low in range(0, width, HD):
        high = low + HD
        column = spread(share[:, low:high])
        other_part = packet_ref[:rows, low:high].astype(jnp.float32)
        context = own_ref[:, low:high] * column + other_part * (1.0 - column)
        gate = jnp.where(
            row_ids < first_rows, gate_ref[0:1, low:high], gate_ref[8:9, low:high]
        )
        out_ref[:, low:high] = (context * gate).astype(jnp.bfloat16)


def exchange(array, mask):
    count = lax.axis_size("tm")
    return lax.ppermute(array, "tm", [(i, i ^ mask) for i in range(count)])


def gathered(array, bits):
    held = {0: array}
    for bit in bits:
        for mask in list(held):
            held[mask ^ bit] = exchange(held[mask], bit)
    return held


def local(
    query_proj, key_proj, value_proj, query_gain, key_gain, gate_table, frame_step, far_blocks
):
    rows, width = query_proj.shape
    count = lax.axis_size("tm")
    splits = lax.axis_size("head")
    full_width = width * splits
    params = pltpu.CompilerParams(vmem_limit_bytes=(8 + count // 2) * 2**20)
    query_mask = count // 4
    bits = [1 << place for place in range(1, count.bit_length() - 1)]
    bits = [bit for bit in bits[::-1] if bit != query_mask]
    query_gain = query_gain.reshape(1, width)
    key_gain = key_gain.reshape(1, width)

    query_packet, own_key, own_sums = pl.pallas_call(
        own_kernel,
        out_shape=[
            jax.ShapeDtypeStruct((rows + EXTRA, width), jnp.bfloat16),
            jax.ShapeDtypeStruct((rows, width), jnp.bfloat16),
            jax.ShapeDtypeStruct((8, rows), jnp.float32),
        ],
        in_specs=[ANY, ANY, VMEM],
        out_specs=[VMEM] * 3,
        scratch_shapes=[
            pltpu.VMEM((rows, width), jnp.bfloat16),
            pltpu.SemaphoreType.DMA((2,)),
        ],
    )(query_proj, key_proj, far_blocks)
    keys = gathered(key_proj, bits)
    keys[0] = own_key
    values = gathered(value_proj, bits)
    queries = [query_packet, exchange(query_packet, query_mask)]
    masks = sorted(keys, key=lambda mask: (mask.bit_count(), mask))

    sources = queries[1:] + [keys[mask] for mask in masks[1:]]
    lines = len(sources) + 2
    sums = pl.pallas_call(
        sums_kernel,
        out_shape=jax.ShapeDtypeStruct((lines + -lines % 8, rows), jnp.float32),
        in_specs=[VMEM] * (1 + len(sources)),
        out_specs=VMEM,
        compiler_params=params,
    )(own_sums, *sources)
    if splits == 2:
        others = lax.ppermute(sums, "head", [(0, 1), (1, 0)])
    else:
        sums = lax.psum(sums, "head")
        others = jnp.zeros_like(sums)

    pack = pl.pallas_call(
        functools.partial(pack_kernel, full_width, len(masks)),
        out_shape=jax.ShapeDtypeStruct((2 * len(masks) * rows, width), jnp.bfloat16),
        in_specs=[VMEM] * (3 + 2 * len(masks)),
        out_specs=VMEM,
        compiler_params=params,
    )(
        key_gain,
        sums,
        others,
        *[keys[mask] for mask in masks],
        *[values[mask] for mask in masks],
    )
    other_pack = exchange(pack, 1)

    query_norm, context, stats = pl.pallas_call(
        functools.partial(own_attention, full_width, [0, query_mask], masks),
        out_shape=[
            jax.ShapeDtypeStruct((2 * rows, width), jnp.bfloat16),
            jax.ShapeDtypeStruct((2 * rows, width), jnp.float32),
            jax.ShapeDtypeStruct((2 * rows, 2 * width), jnp.float32),
        ],
        in_specs=[VMEM] * 6,
        out_specs=[VMEM] * 3,
        compiler_params=params,
    )(query_gain, sums, others, *queries, pack)

    def last_part(place, out_shape):
        return pl.pallas_call(
            functools.partial(
                last_attention, place, place * query_mask, [mask ^ 1 for mask in masks]
            ),
            out_shape=out_shape,
            in_specs=[VMEM] * 5,
            out_specs=[VMEM] * len(out_shape),
            compiler_params=params,
        )(query_norm, queries[place], other_pack, context, stats)

    (packet,) = last_part(1, [jax.ShapeDtypeStruct((rows + EXTRA, width), jnp.bfloat16)])
    own, own_logs = last_part(
        0,
        [
            jax.ShapeDtypeStruct((rows, width), jnp.float32),
            jax.ShapeDtypeStruct((8, width), jnp.float32),
        ],
    )
    gates = pl.pallas_call(
        gate_kernel,
        out_shape=jax.ShapeDtypeStruct((16, width), jnp.float32),
        in_specs=[SMEM, VMEM],
        out_specs=VMEM,
        compiler_params=params,
    )(frame_step, gate_table)
    packet = exchange(packet, query_mask)

    return pl.pallas_call(
        merge_kernel,
        out_shape=jax.ShapeDtypeStruct((rows, width), jnp.bfloat16),
        in_specs=[VMEM] * 4,
        out_specs=VMEM,
        compiler_params=params,
    )(own, own_logs, packet, gates)


def solution(mesh):
    return jax.shard_map(
        local,
        mesh=mesh,
        in_specs=(
            P("tm", "head"),
            P("tm", "head"),
            P("tm", "head"),
            P("head"),
            P("head"),
            P(None, "head"),
            P(),
            P("tm", None),
        ),
        out_specs=P("tm", "head"),
        check_vma=False,
    )
```

```python
import functools

import jax
import jax.numpy as jnp
from jax import lax
from jax.experimental import pallas as pl
from jax.experimental.pallas import tpu as pltpu
from jax.sharding import PartitionSpec as P

HD = 128
BLK = 64
FRAME_TOK = 1560
EPSILON = 1e-06
LOG2E = 1.4426950408889634
SCALE = HD ** (-0.5) * LOG2E
MASKED = -1e30
EXTRA = 16
ANY = pl.BlockSpec(memory_space=pl.ANY)
VMEM = pl.BlockSpec(memory_space=pltpu.VMEM)
SMEM = pl.BlockSpec(memory_space=pltpu.SMEM)


def spread(row):
    return jnp.broadcast_to(row, (row.shape[1], row.shape[1])).T


def squares(source_ref):
    wide = source_ref[:HD, :].astype(jnp.float32)
    square = wide * wide
    part = square[:, :HD]
    for low in range(HD, square.shape[1], HD):
        part = part + square[:, low : low + HD]
    return jnp.sum(part.T, axis=0, keepdims=True)


def own_kernel(
    query_hbm,
    key_hbm,
    value_hbm,
    far_hbm,
    query_out,
    key_out,
    value_out,
    sums_out,
    query_ref,
    far_ref,
    sems,
):
    rows, width = query_ref.shape
    copies = [
        pltpu.make_async_copy(query_hbm, query_ref, sems.at[0]),
        pltpu.make_async_copy(key_hbm, key_out, sems.at[1]),
        pltpu.make_async_copy(far_hbm, far_ref, sems.at[2]),
        pltpu.make_async_copy(value_hbm, value_out, sems.at[3]),
    ]
    for copy in copies:
        copy.start()
    query_out[rows:, HD:] = jnp.zeros((EXTRA, width - HD), jnp.bfloat16)
    sums_out[...] = jnp.zeros_like(sums_out)
    copies[0].wait()
    query_out[:rows, :] = query_ref[...]
    sums_out[0:1, :] = squares(query_ref)
    copies[1].wait()
    sums_out[1:2, :] = squares(key_out)
    copies[2].wait()
    far = far_ref[...].astype(jnp.float32)
    far = jnp.concatenate([far, jnp.full((1, HD - far.shape[1]), -1.0)], axis=1)
    query_out[rows:, :HD] = jnp.broadcast_to(far, (EXTRA, HD)).astype(jnp.bfloat16)
    copies[3].wait()


def sums_kernel(first, before_ref, *refs):
    *sources, out_ref = refs
    out_ref[...] = before_ref[...]
    for place, source_ref in enumerate(sources, start=first):
        out_ref[place : place + 1, :] = squares(source_ref)


def normed(source_ref, own_ref, other_ref, line, gain_ref, full_width):
    total = own_ref[line : line + 1, :] + other_ref[line : line + 1, :]
    factor = spread(lax.rsqrt(total / full_width + EPSILON))
    parts = []
    for low in range(0, source_ref.shape[1], HD):
        wide = source_ref[:HD, low : low + HD].astype(jnp.float32)
        parts.append((wide * factor * gain_ref[:, low : low + HD]).astype(jnp.bfloat16))
    return jnp.concatenate(parts, axis=1)


def pack_kernel(full_width, held, gain_ref, own_ref, other_ref, *refs):
    keys, values, pack_out = refs[:held], refs[held : 2 * held], refs[2 * held]
    rows = keys[0].shape[0]
    for place, key_ref in enumerate(keys):
        pack_out[place * rows : (place + 1) * rows, :] = normed(
            key_ref, own_ref, other_ref, 1 + place + (place > 0), gain_ref, full_width
        )
    for place, value_ref in enumerate(values, start=held):
        pack_out[place * rows : (place + 1) * rows, :] = value_ref[...]


def key_bias(query_ref, query_mask, key_masks):
    me = lax.axis_index("tm")
    lane = lax.broadcasted_iota(jnp.int32, (1, HD), 1)
    half = (lane >= BLK).astype(jnp.float32)
    far = query_ref[HD:, :HD].astype(jnp.float32)[:1]
    parts = []
    for key_mask in key_masks:
        query_id, key_id = me ^ query_mask, me ^ key_mask
        choice = jnp.sum(jnp.where(lane == key_id, far, 0.0), axis=1, keepdims=True)
        taken = (choice == half) | (jnp.abs(query_id - key_id) <= 1)
        parts.append(jnp.where(taken, 0.0, MASKED))
    return jnp.concatenate(parts, axis=1)


def columns_of(pack, second, low, high):
    half = pack.shape[0] // 2
    return pack[half * second : half * (second + 1), low:high]


def absorb(query, keys, values, bias, old):
    rows = query.shape[0]
    logits = (
        lax.dot_general(
            query, keys, (((1,), (1,)), ((), ())), preferred_element_type=jnp.float32
        )
        * SCALE
        + bias
    )
    top = jnp.broadcast_to(jnp.max(logits, axis=1, keepdims=True), (rows, HD))
    if old is not None:
        top = jnp.maximum(top, old[0])
    weights = [
        jnp.exp2(logits[:, left : left + HD] - top) for left in range(0, logits.shape[1], HD)
    ]
    total = jnp.sum(functools.reduce(jnp.add, weights), axis=1, keepdims=True)
    total = jnp.broadcast_to(total, (rows, HD))
    context = jnp.dot(
        jnp.concatenate([weight.astype(jnp.bfloat16) for weight in weights], axis=1),
        values,
        preferred_element_type=jnp.float32,
    )
    if old is not None:
        fade = jnp.exp2(old[0] - top)
        total = total + old[1] * fade
        context = context + old[2] * fade
    return top, total, context


def own_attention(full_width, query_masks, key_masks, gain_ref, own_ref, other_ref, *refs):
    queries, pack = refs[:2], refs[2]
    query_out, context_out, stats_out = refs[3:]
    rows, width = query_out.shape[0] // 2, query_out.shape[1]
    for place, mask in enumerate(query_masks):
        part = slice(place * rows, (place + 1) * rows)
        bias = key_bias(queries[place], mask, key_masks)
        query = normed(queries[place], own_ref, other_ref, 2 * place, gain_ref, full_width)
        query_out[part, :] = query
        for low in range(0, width, HD):
            high, wide = low + HD, 2 * low
            top, total, context = absorb(
                query[:, low:high],
                columns_of(pack, 0, low, high),
                columns_of(pack, 1, low, high),
                bias,
                None,
            )
            context_out[part, low:high] = context
            stats_out[part, wide : wide + HD] = top
            stats_out[part, wide + HD : wide + 2 * HD] = total


def last_attention(place, query_mask, key_masks, query_ref, raw_ref, *refs):
    pack, context_ref, stats_ref, *outs = refs
    rows, width = query_ref.shape[0] // 2, query_ref.shape[1]
    heads = width // HD
    part = slice(place * rows, (place + 1) * rows)
    bias = key_bias(raw_ref, query_mask, key_masks)
    lane = lax.broadcasted_iota(jnp.int32, (1, HD), 1)
    logs = jnp.zeros((rows, HD), jnp.float32)
    for head in range(heads):
        low, high = head * HD, (head + 1) * HD
        wide = 2 * low
        top, total, context = absorb(
            query_ref[part, low:high],
            columns_of(pack, 0, low, high),
            columns_of(pack, 1, low, high),
            bias,
            (
                stats_ref[part, wide : wide + HD],
                stats_ref[part, wide + HD : wide + 2 * HD],
                context_ref[part, low:high],
            ),
        )
        outs[0][:rows, low:high] = (context * (1.0 / total)).astype(outs[0].dtype)
        logs = jnp.where(lane == head, top + jnp.log2(total), logs)
    lines = logs.T
    sub = lax.broadcasted_iota(jnp.int32, (EXTRA, HD), 0)
    for head in range(heads):
        low, high = head * HD, (head + 1) * HD
        value = lines[head : head + 1, :]
        if place == 0:
            outs[1][:, low:high] = jnp.broadcast_to(value, (8, HD))
        else:
            first = value.astype(jnp.bfloat16).astype(jnp.float32)
            second = (value - first).astype(jnp.bfloat16).astype(jnp.float32)
            third = value - first - second
            outs[0][rows:, low:high] = jnp.where(
                sub == 0, first, jnp.where(sub == 1, second, third)
            ).astype(jnp.bfloat16)


def gate_kernel(step_ref, table_ref, out_ref):
    rows = out_ref.shape[0] // 2
    start = lax.axis_index("tm") * HD
    first = step_ref[start // FRAME_TOK]
    last = step_ref[(start + HD - 1) // FRAME_TOK]
    out_ref[:rows, :] = jnp.broadcast_to(table_ref[pl.ds(first, 1), :], (rows, out_ref.shape[1]))
    out_ref[rows:, :] = jnp.broadcast_to(table_ref[pl.ds(last, 1), :], (rows, out_ref.shape[1]))


def merge_kernel(own_ref, logs_ref, packet_ref, gate_ref, out_ref):
    rows, width = own_ref.shape
    pieces = packet_ref[rows:, :].astype(jnp.float32)
    other = pieces[0:1] + pieces[1:2] + pieces[2:3]
    top = jnp.maximum(logs_ref[:1, :], other)
    own_weight = jnp.exp2(logs_ref[:1, :] - top)
    other_weight = jnp.exp2(other - top)
    share = own_weight / (own_weight + other_weight)
    start = lax.axis_index("tm") * rows
    first_rows = (start // FRAME_TOK + 1) * FRAME_TOK - start
    row_ids = lax.broadcasted_iota(jnp.int32, (rows, 1), 0)
    for low in range(0, width, HD):
        high = low + HD
        column = spread(share[:, low:high])
        other_part = packet_ref[:rows, low:high].astype(jnp.float32)
        context = own_ref[:, low:high] * column + other_part * (1.0 - column)
        gate = jnp.where(
            row_ids < first_rows, gate_ref[0:1, low:high], gate_ref[8:9, low:high]
        )
        out_ref[:, low:high] = (context * gate).astype(jnp.bfloat16)


def exchange(array, mask):
    count = lax.axis_size("tm")
    return lax.ppermute(array, "tm", [(i, i ^ mask) for i in range(count)])


def gathered(array, bits):
    held = {0: array}
    for bit in bits:
        for mask in list(held):
            held[mask ^ bit] = exchange(held[mask], bit)
    return held


def local(
    query_proj, key_proj, value_proj, query_gain, key_gain, gate_table, frame_step, far_blocks
):
    rows, width = query_proj.shape
    count = lax.axis_size("tm")
    splits = lax.axis_size("head")
    full_width = width * splits
    params = pltpu.CompilerParams(vmem_limit_bytes=(8 + count // 2) * 2**20)
    query_mask = count // 4
    bits = [1 << place for place in range(1, count.bit_length() - 1)]
    bits = [bit for bit in bits[::-1] if bit != query_mask]
    query_gain = query_gain.reshape(1, width)
    key_gain = key_gain.reshape(1, width)

    lines = 2 + 2 ** len(bits)
    lines += -lines % 8
    query_packet, own_key, own_value, own_sums = pl.pallas_call(
        own_kernel,
        out_shape=[
            jax.ShapeDtypeStruct((rows + EXTRA, width), jnp.bfloat16),
            jax.ShapeDtypeStruct((rows, width), jnp.bfloat16),
            jax.ShapeDtypeStruct((rows, width), jnp.bfloat16),
            jax.ShapeDtypeStruct((lines, rows), jnp.float32),
        ],
        in_specs=[ANY] * 4,
        out_specs=[VMEM] * 4,
        scratch_shapes=[
            pltpu.VMEM((rows, width), jnp.bfloat16),
            pltpu.VMEM(far_blocks.shape, jnp.int32),
            pltpu.SemaphoreType.DMA((4,)),
        ],
    )(query_proj, key_proj, value_proj, far_blocks)
    keys = gathered(key_proj, bits)
    keys[0] = own_key
    values = gathered(own_value, bits)
    queries = [query_packet, exchange(query_packet, query_mask)]
    masks = sorted(keys, key=lambda mask: (mask.bit_count(), mask))

    sums = own_sums
    first = 2
    near = [mask for mask in masks[1:] if mask.bit_count() == 1]
    for sources in (
        queries[1:] + [keys[mask] for mask in near],
        [keys[mask] for mask in masks[1 + len(near) :]],
    ):
        sums = pl.pallas_call(
            functools.partial(sums_kernel, first),
            out_shape=jax.ShapeDtypeStruct(own_sums.shape, jnp.float32),
            in_specs=[VMEM] * (1 + len(sources)),
            out_specs=VMEM,
            compiler_params=params,
        )(sums, *sources)
        first += len(sources)
    if splits == 2:
        others = lax.ppermute(sums, "head", [(0, 1), (1, 0)])
    else:
        sums = lax.psum(sums, "head")
        others = jnp.zeros_like(sums)

    pack = pl.pallas_call(
        functools.partial(pack_kernel, full_width, len(masks)),
        out_shape=jax.ShapeDtypeStruct((2 * len(masks) * rows, width), jnp.bfloat16),
        in_specs=[VMEM] * (3 + 2 * len(masks)),
        out_specs=VMEM,
        compiler_params=params,
    )(
        key_gain,
        sums,
        others,
        *[keys[mask] for mask in masks],
        *[values[mask] for mask in masks],
    )
    other_pack = exchange(pack, 1)

    query_norm, context, stats = pl.pallas_call(
        functools.partial(own_attention, full_width, [0, query_mask], masks),
        out_shape=[
            jax.ShapeDtypeStruct((2 * rows, width), jnp.bfloat16),
            jax.ShapeDtypeStruct((2 * rows, width), jnp.float32),
            jax.ShapeDtypeStruct((2 * rows, 2 * width), jnp.float32),
        ],
        in_specs=[VMEM] * 6,
        out_specs=[VMEM] * 3,
        compiler_params=params,
    )(query_gain, sums, others, *queries, pack)

    def last_part(place, out_shape):
        return pl.pallas_call(
            functools.partial(
                last_attention, place, place * query_mask, [mask ^ 1 for mask in masks]
            ),
            out_shape=out_shape,
            in_specs=[VMEM] * 5,
            out_specs=[VMEM] * len(out_shape),
            compiler_params=params,
        )(query_norm, queries[place], other_pack, context, stats)

    (packet,) = last_part(1, [jax.ShapeDtypeStruct((rows + EXTRA, width), jnp.bfloat16)])
    own, own_logs = last_part(
        0,
        [
            jax.ShapeDtypeStruct((rows, width), jnp.float32),
            jax.ShapeDtypeStruct((8, width), jnp.float32),
        ],
    )
    gates = pl.pallas_call(
        gate_kernel,
        out_shape=jax.ShapeDtypeStruct((16, width), jnp.float32),
        in_specs=[SMEM, VMEM],
        out_specs=VMEM,
        compiler_params=params,
    )(frame_step, gate_table)
    packet = exchange(packet, query_mask)

    return pl.pallas_call(
        merge_kernel,
        out_shape=jax.ShapeDtypeStruct((rows, width), jnp.bfloat16),
        in_specs=[VMEM] * 4,
        out_specs=VMEM,
        compiler_params=params,
    )(own, own_logs, packet, gates)


def solution(mesh):
    return jax.shard_map(
        local,
        mesh=mesh,
        in_specs=(
            P("tm", "head"),
            P("tm", "head"),
            P("tm", "head"),
            P("head"),
            P("head"),
            P(None, "head"),
            P(),
            P("tm", None),
        ),
        out_specs=P("tm", "head"),
        check_vma=False,
    )
```

```python
import functools

import jax
import jax.numpy as jnp
from jax import lax
from jax.experimental import pallas as pl
from jax.experimental.pallas import tpu as pltpu
from jax.sharding import PartitionSpec as P

HD = 128
BLK = 64
FRAME_TOK = 1560
EPSILON = 1e-06
LOG2E = 1.4426950408889634
SCALE = HD ** (-0.5) * LOG2E
MASKED = -1e30
EXTRA = 16
ANY = pl.BlockSpec(memory_space=pl.ANY)
VMEM = pl.BlockSpec(memory_space=pltpu.VMEM)
SMEM = pl.BlockSpec(memory_space=pltpu.SMEM)


def spread(row):
    return jnp.broadcast_to(row, (row.shape[1], row.shape[1])).T


def squares(source_ref):
    wide = source_ref[:HD, :].astype(jnp.float32)
    square = wide * wide
    part = square[:, :HD]
    for low in range(HD, square.shape[1], HD):
        part = part + square[:, low : low + HD]
    return jnp.sum(part.T, axis=0, keepdims=True)


def own_kernel(
    query_hbm,
    key_hbm,
    value_hbm,
    far_hbm,
    query_out,
    key_out,
    value_out,
    sums_out,
    query_ref,
    far_ref,
    sems,
):
    rows, width = query_ref.shape
    copies = [
        pltpu.make_async_copy(query_hbm, query_ref, sems.at[0]),
        pltpu.make_async_copy(key_hbm, key_out, sems.at[1]),
        pltpu.make_async_copy(far_hbm, far_ref, sems.at[2]),
        pltpu.make_async_copy(value_hbm, value_out, sems.at[3]),
    ]
    for copy in copies:
        copy.start()
    query_out[rows:, HD:] = jnp.zeros((EXTRA, width - HD), jnp.bfloat16)
    sums_out[...] = jnp.zeros_like(sums_out)
    copies[0].wait()
    query_out[:rows, :] = query_ref[...]
    sums_out[0:1, :] = squares(query_ref)
    copies[1].wait()
    sums_out[1:2, :] = squares(key_out)
    copies[2].wait()
    far = far_ref[...].astype(jnp.float32)
    far = jnp.concatenate([far, jnp.full((1, HD - far.shape[1]), -1.0)], axis=1)
    query_out[rows:, :HD] = jnp.broadcast_to(far, (EXTRA, HD)).astype(jnp.bfloat16)
    copies[3].wait()


def sums_kernel(first, before_ref, *refs):
    *sources, out_ref = refs
    out_ref[...] = before_ref[...]
    for place, source_ref in enumerate(sources, start=first):
        out_ref[place : place + 1, :] = squares(source_ref)


def normed(source_ref, own_ref, other_ref, line, gain_ref, full_width):
    total = own_ref[line : line + 1, :] + other_ref[line : line + 1, :]
    factor = spread(lax.rsqrt(total / full_width + EPSILON))
    parts = []
    for low in range(0, source_ref.shape[1], HD):
        wide = source_ref[:HD, low : low + HD].astype(jnp.float32)
        parts.append((wide * factor * gain_ref[:, low : low + HD]).astype(jnp.bfloat16))
    return jnp.concatenate(parts, axis=1)


def pack_kernel(full_width, held, gain_ref, own_ref, other_ref, *refs):
    keys, values, pack_out = refs[:held], refs[held : 2 * held], refs[2 * held]
    rows = keys[0].shape[0]
    for place, key_ref in enumerate(keys):
        pack_out[place * rows : (place + 1) * rows, :] = normed(
            key_ref, own_ref, other_ref, 1 + place + (place > 0), gain_ref, full_width
        )
    for place, value_ref in enumerate(values, start=held):
        pack_out[place * rows : (place + 1) * rows, :] = value_ref[...]


def key_bias(query_ref, query_mask, key_masks):
    me = lax.axis_index("tm")
    lane = lax.broadcasted_iota(jnp.int32, (1, HD), 1)
    half = (lane >= BLK).astype(jnp.float32)
    far = query_ref[HD:, :HD].astype(jnp.float32)[:1]
    parts = []
    for key_mask in key_masks:
        query_id, key_id = me ^ query_mask, me ^ key_mask
        choice = jnp.sum(jnp.where(lane == key_id, far, 0.0), axis=1, keepdims=True)
        taken = (choice == half) | (jnp.abs(query_id - key_id) <= 1)
        parts.append(jnp.where(taken, 0.0, MASKED))
    return jnp.concatenate(parts, axis=1)


def columns_of(pack, second, low, high):
    half = pack.shape[0] // 2
    return pack[half * second : half * (second + 1), low:high]


def absorb(query, keys, values, bias, old):
    rows = query.shape[0]
    logits = (
        lax.dot_general(
            query, keys, (((1,), (1,)), ((), ())), preferred_element_type=jnp.float32
        )
        * SCALE
        + bias
    )
    top = jnp.broadcast_to(jnp.max(logits, axis=1, keepdims=True), (rows, HD))
    if old is not None:
        top = jnp.maximum(top, old[0])
    weights = [
        jnp.exp2(logits[:, left : left + HD] - top) for left in range(0, logits.shape[1], HD)
    ]
    total = jnp.sum(functools.reduce(jnp.add, weights), axis=1, keepdims=True)
    total = jnp.broadcast_to(total, (rows, HD))
    context = jnp.dot(
        jnp.concatenate([weight.astype(jnp.bfloat16) for weight in weights], axis=1),
        values,
        preferred_element_type=jnp.float32,
    )
    if old is not None:
        fade = jnp.exp2(old[0] - top)
        total = total + old[1] * fade
        context = context + old[2] * fade
    return top, total, context


def own_attention(full_width, query_masks, key_masks, gain_ref, own_ref, other_ref, *refs):
    queries, pack = refs[:2], refs[2]
    query_out, context_out, stats_out = refs[3:]
    rows, width = query_out.shape[0] // 2, query_out.shape[1]
    for place, mask in enumerate(query_masks):
        part = slice(place * rows, (place + 1) * rows)
        bias = key_bias(queries[place], mask, key_masks)
        query = normed(queries[place], own_ref, other_ref, 2 * place, gain_ref, full_width)
        query_out[part, :] = query
        for low in range(0, width, HD):
            high, wide = low + HD, 2 * low
            top, total, context = absorb(
                query[:, low:high],
                columns_of(pack, 0, low, high),
                columns_of(pack, 1, low, high),
                bias,
                None,
            )
            context_out[part, low:high] = context
            stats_out[part, wide : wide + HD] = top
            stats_out[part, wide + HD : wide + 2 * HD] = total


def last_attention(place, query_mask, key_masks, query_ref, raw_ref, *refs):
    pack, context_ref, stats_ref, *outs = refs
    rows, width = query_ref.shape[0] // 2, query_ref.shape[1]
    heads = width // HD
    part = slice(place * rows, (place + 1) * rows)
    bias = key_bias(raw_ref, query_mask, key_masks)
    lane = lax.broadcasted_iota(jnp.int32, (1, HD), 1)
    logs = jnp.zeros((rows, HD), jnp.float32)
    for head in range(heads):
        low, high = head * HD, (head + 1) * HD
        wide = 2 * low
        top, total, context = absorb(
            query_ref[part, low:high],
            columns_of(pack, 0, low, high),
            columns_of(pack, 1, low, high),
            bias,
            (
                stats_ref[part, wide : wide + HD],
                stats_ref[part, wide + HD : wide + 2 * HD],
                context_ref[part, low:high],
            ),
        )
        outs[0][:rows, low:high] = (context * (1.0 / total)).astype(outs[0].dtype)
        logs = jnp.where(lane == head, top + jnp.log2(total), logs)
    lines = logs.T
    sub = lax.broadcasted_iota(jnp.int32, (EXTRA, HD), 0)
    for head in range(heads):
        low, high = head * HD, (head + 1) * HD
        value = lines[head : head + 1, :]
        if place == 0:
            outs[1][:, low:high] = jnp.broadcast_to(value, (8, HD))
        else:
            first = value.astype(jnp.bfloat16).astype(jnp.float32)
            second = (value - first).astype(jnp.bfloat16).astype(jnp.float32)
            third = value - first - second
            outs[0][rows:, low:high] = jnp.where(
                sub == 0, first, jnp.where(sub == 1, second, third)
            ).astype(jnp.bfloat16)


def gate_kernel(step_ref, table_ref, out_ref):
    rows = out_ref.shape[0] // 2
    start = lax.axis_index("tm") * HD
    first = step_ref[start // FRAME_TOK]
    last = step_ref[(start + HD - 1) // FRAME_TOK]
    out_ref[:rows, :] = jnp.broadcast_to(table_ref[pl.ds(first, 1), :], (rows, out_ref.shape[1]))
    out_ref[rows:, :] = jnp.broadcast_to(table_ref[pl.ds(last, 1), :], (rows, out_ref.shape[1]))


def merge_kernel(own_ref, logs_ref, packet_ref, gate_ref, out_ref):
    rows, width = own_ref.shape
    pieces = packet_ref[rows:, :].astype(jnp.float32)
    other = pieces[0:1] + pieces[1:2] + pieces[2:3]
    top = jnp.maximum(logs_ref[:1, :], other)
    own_weight = jnp.exp2(logs_ref[:1, :] - top)
    other_weight = jnp.exp2(other - top)
    share = own_weight / (own_weight + other_weight)
    start = lax.axis_index("tm") * rows
    first_rows = (start // FRAME_TOK + 1) * FRAME_TOK - start
    row_ids = lax.broadcasted_iota(jnp.int32, (rows, 1), 0)
    for low in range(0, width, HD):
        high = low + HD
        column = spread(share[:, low:high])
        other_part = packet_ref[:rows, low:high].astype(jnp.float32)
        context = own_ref[:, low:high] * column + other_part * (1.0 - column)
        gate = jnp.where(
            row_ids < first_rows, gate_ref[0:1, low:high], gate_ref[8:9, low:high]
        )
        out_ref[:, low:high] = (context * gate).astype(jnp.bfloat16)


def exchange(array, mask):
    count = lax.axis_size("tm")
    return lax.ppermute(array, "tm", [(i, i ^ mask) for i in range(count)])


def gathered(array, bits):
    held = {0: array}
    for bit in bits:
        for mask in list(held):
            held[mask ^ bit] = exchange(held[mask], bit)
    return held


def local(
    query_proj, key_proj, value_proj, query_gain, key_gain, gate_table, frame_step, far_blocks
):
    rows, width = query_proj.shape
    count = lax.axis_size("tm")
    splits = lax.axis_size("head")
    full_width = width * splits
    params = pltpu.CompilerParams(vmem_limit_bytes=(8 + count // 2) * 2**20)
    query_mask = count // 2
    bits = [1 << place for place in range(1, count.bit_length() - 2)]
    query_gain = query_gain.reshape(1, width)
    key_gain = key_gain.reshape(1, width)

    lines = 2 + 2 ** len(bits)
    lines += -lines % 8
    query_packet, own_key, own_value, own_sums = pl.pallas_call(
        own_kernel,
        out_shape=[
            jax.ShapeDtypeStruct((rows + EXTRA, width), jnp.bfloat16),
            jax.ShapeDtypeStruct((rows, width), jnp.bfloat16),
            jax.ShapeDtypeStruct((rows, width), jnp.bfloat16),
            jax.ShapeDtypeStruct((lines, rows), jnp.float32),
        ],
        in_specs=[ANY] * 4,
        out_specs=[VMEM] * 4,
        scratch_shapes=[
            pltpu.VMEM((rows, width), jnp.bfloat16),
            pltpu.VMEM(far_blocks.shape, jnp.int32),
            pltpu.SemaphoreType.DMA((4,)),
        ],
    )(query_proj, key_proj, value_proj, far_blocks)
    keys = gathered(key_proj, bits[::-1])
    keys[0] = own_key
    values = gathered(own_value, bits)
    queries = [query_packet, exchange(query_packet, query_mask)]
    masks = sorted(keys, key=lambda mask: (mask.bit_count(), mask))

    sums = own_sums
    first = 2
    near = [mask for mask in masks[1:] if mask.bit_count() == 1]
    for sources in (
        queries[1:] + [keys[mask] for mask in near],
        [keys[mask] for mask in masks[1 + len(near) :]],
    ):
        sums = pl.pallas_call(
            functools.partial(sums_kernel, first),
            out_shape=jax.ShapeDtypeStruct(own_sums.shape, jnp.float32),
            in_specs=[VMEM] * (1 + len(sources)),
            out_specs=VMEM,
            compiler_params=params,
        )(sums, *sources)
        first += len(sources)
    if splits == 2:
        others = lax.ppermute(sums, "head", [(0, 1), (1, 0)])
    else:
        sums = lax.psum(sums, "head")
        others = jnp.zeros_like(sums)

    pack = pl.pallas_call(
        functools.partial(pack_kernel, full_width, len(masks)),
        out_shape=jax.ShapeDtypeStruct((2 * len(masks) * rows, width), jnp.bfloat16),
        in_specs=[VMEM] * (3 + 2 * len(masks)),
        out_specs=VMEM,
        compiler_params=params,
    )(
        key_gain,
        sums,
        others,
        *[keys[mask] for mask in masks],
        *[values[mask] for mask in masks],
    )
    other_pack = exchange(pack, 1)

    query_norm, context, stats = pl.pallas_call(
        functools.partial(own_attention, full_width, [0, query_mask], masks),
        out_shape=[
            jax.ShapeDtypeStruct((2 * rows, width), jnp.bfloat16),
            jax.ShapeDtypeStruct((2 * rows, width), jnp.float32),
            jax.ShapeDtypeStruct((2 * rows, 2 * width), jnp.float32),
        ],
        in_specs=[VMEM] * 6,
        out_specs=[VMEM] * 3,
        compiler_params=params,
    )(query_gain, sums, others, *queries, pack)

    def last_part(place, out_shape):
        return pl.pallas_call(
            functools.partial(
                last_attention, place, place * query_mask, [mask ^ 1 for mask in masks]
            ),
            out_shape=out_shape,
            in_specs=[VMEM] * 5,
            out_specs=[VMEM] * len(out_shape),
            compiler_params=params,
        )(query_norm, queries[place], other_pack, context, stats)

    (packet,) = last_part(1, [jax.ShapeDtypeStruct((rows + EXTRA, width), jnp.bfloat16)])
    own, own_logs = last_part(
        0,
        [
            jax.ShapeDtypeStruct((rows, width), jnp.float32),
            jax.ShapeDtypeStruct((8, width), jnp.float32),
        ],
    )
    gates = pl.pallas_call(
        gate_kernel,
        out_shape=jax.ShapeDtypeStruct((16, width), jnp.float32),
        in_specs=[SMEM, VMEM],
        out_specs=VMEM,
        compiler_params=params,
    )(frame_step, gate_table)
    packet = exchange(packet, query_mask)

    return pl.pallas_call(
        merge_kernel,
        out_shape=jax.ShapeDtypeStruct((rows, width), jnp.bfloat16),
        in_specs=[VMEM] * 4,
        out_specs=VMEM,
        compiler_params=params,
    )(own, own_logs, packet, gates)


def solution(mesh):
    return jax.shard_map(
        local,
        mesh=mesh,
        in_specs=(
            P("tm", "head"),
            P("tm", "head"),
            P("tm", "head"),
            P("head"),
            P("head"),
            P(None, "head"),
            P(),
            P("tm", None),
        ),
        out_specs=P("tm", "head"),
        check_vma=False,
    )
```

```python
import functools

import jax
import jax.numpy as jnp
from jax import lax
from jax.experimental import pallas as pl
from jax.experimental.pallas import tpu as pltpu
from jax.sharding import PartitionSpec as P

HD = 128
BLK = 64
FRAME_TOK = 1560
EPSILON = 1e-06
LOG2E = 1.4426950408889634
SCALE = HD ** (-0.5) * LOG2E
MASKED = -1e30
EXTRA = 16
AHEAD = 4 * 10**9
ANY = pl.BlockSpec(memory_space=pl.ANY)
VMEM = pl.BlockSpec(memory_space=pltpu.VMEM)
SMEM = pl.BlockSpec(memory_space=pltpu.SMEM)


def spread(row):
    return jnp.broadcast_to(row, (row.shape[1], row.shape[1])).T


def squares(source_ref):
    wide = source_ref[:HD, :].astype(jnp.float32)
    square = wide * wide
    part = square[:, :HD]
    for low in range(HD, square.shape[1], HD):
        part = part + square[:, low : low + HD]
    return jnp.sum(part.T, axis=0, keepdims=True)


def own_kernel(
    query_hbm,
    key_hbm,
    value_hbm,
    far_hbm,
    query_out,
    key_out,
    value_out,
    sums_out,
    query_ref,
    far_ref,
    sems,
):
    rows, width = query_ref.shape
    copies = [
        pltpu.make_async_copy(query_hbm, query_ref, sems.at[0]),
        pltpu.make_async_copy(key_hbm, key_out, sems.at[1]),
        pltpu.make_async_copy(far_hbm, far_ref, sems.at[2]),
        pltpu.make_async_copy(value_hbm, value_out, sems.at[3]),
    ]
    for copy in copies:
        copy.start()
    query_out[rows:, HD:] = jnp.zeros((EXTRA, width - HD), jnp.bfloat16)
    sums_out[...] = jnp.zeros_like(sums_out)
    copies[0].wait()
    query_out[:rows, :] = query_ref[...]
    sums_out[0:1, :] = squares(query_ref)
    copies[1].wait()
    sums_out[1:2, :] = squares(key_out)
    copies[2].wait()
    far = far_ref[...].astype(jnp.float32)
    far = jnp.concatenate([far, jnp.full((1, HD - far.shape[1]), -1.0)], axis=1)
    query_out[rows:, :HD] = jnp.broadcast_to(far, (EXTRA, HD)).astype(jnp.bfloat16)
    copies[3].wait()


def near_sums_kernel(lines, before_ref, value_ref, *refs):
    *sources, out_ref, value_out = refs
    sums_kernel(lines, before_ref, *sources[: len(lines)], out_ref)
    value_out[...] = value_ref[...]


def sums_kernel(lines, before_ref, *refs):
    *sources, out_ref = refs
    out_ref[...] = before_ref[...]
    for line, source_ref in zip(lines, sources):
        out_ref[line : line + 1, :] = squares(source_ref)


def factor_kernel(full_width, own_ref, other_ref, out_ref):
    out_ref[...] = lax.rsqrt((own_ref[...] + other_ref[...]) / full_width + EPSILON)


def normed(source_ref, factors_ref, line, gain_ref):
    factor = spread(factors_ref[line : line + 1, :])
    parts = []
    for low in range(0, source_ref.shape[1], HD):
        wide = source_ref[:HD, low : low + HD].astype(jnp.float32)
        parts.append((wide * factor * gain_ref[:, low : low + HD]).astype(jnp.bfloat16))
    return jnp.concatenate(parts, axis=1)


def pack_kernel(held, gain_ref, factors_ref, *refs):
    keys, values, pack_out = refs[:held], refs[held : 2 * held], refs[2 * held]
    rows = keys[0].shape[0]
    for place, key_ref in enumerate(keys):
        pack_out[place * rows : (place + 1) * rows, :] = normed(
            key_ref, factors_ref, 1 + place + (place > 0), gain_ref
        )
    for place, value_ref in enumerate(values, start=held):
        pack_out[place * rows : (place + 1) * rows, :] = value_ref[...]


def key_bias(query_ref, query_mask, key_masks):
    me = lax.axis_index("tm")
    lane = lax.broadcasted_iota(jnp.int32, (1, HD), 1)
    half = (lane >= BLK).astype(jnp.float32)
    far = query_ref[HD:, :HD].astype(jnp.float32)[:1]
    parts = []
    for key_mask in key_masks:
        query_id, key_id = me ^ query_mask, me ^ key_mask
        choice = jnp.sum(jnp.where(lane == key_id, far, 0.0), axis=1, keepdims=True)
        taken = (choice == half) | (jnp.abs(query_id - key_id) <= 1)
        parts.append(jnp.where(taken, 0.0, MASKED))
    return jnp.concatenate(parts, axis=1)


def columns_of(pack, second, low, high):
    half = pack.shape[0] // 2
    return pack[half * second : half * (second + 1), low:high]


def absorb(query, keys, values, bias, old):
    rows = query.shape[0]
    logits = (
        lax.dot_general(
            query, keys, (((1,), (1,)), ((), ())), preferred_element_type=jnp.float32
        )
        * SCALE
        + bias
    )
    top = jnp.broadcast_to(jnp.max(logits, axis=1, keepdims=True), (rows, HD))
    if old is not None:
        top = jnp.maximum(top, old[0])
    weights = [
        jnp.exp2(logits[:, left : left + HD] - top) for left in range(0, logits.shape[1], HD)
    ]
    total = jnp.sum(functools.reduce(jnp.add, weights), axis=1, keepdims=True)
    total = jnp.broadcast_to(total, (rows, HD))
    context = jnp.dot(
        jnp.concatenate([weight.astype(jnp.bfloat16) for weight in weights], axis=1),
        values,
        preferred_element_type=jnp.float32,
    )
    if old is not None:
        fade = jnp.exp2(old[0] - top)
        total = total + old[1] * fade
        context = context + old[2] * fade
    return top, total, context


def own_attention(query_masks, key_masks, gain_ref, factors_ref, *refs):
    queries, pack = refs[:2], refs[2]
    query_out, context_out, stats_out = refs[3:]
    rows, width = query_out.shape[0] // 2, query_out.shape[1]
    for place, mask in enumerate(query_masks):
        part = slice(place * rows, (place + 1) * rows)
        bias = key_bias(queries[place], mask, key_masks)
        query = normed(queries[place], factors_ref, 2 * place, gain_ref)
        query_out[part, :] = query
        for low in range(0, width, HD):
            high, wide = low + HD, 2 * low
            top, total, context = absorb(
                query[:, low:high],
                columns_of(pack, 0, low, high),
                columns_of(pack, 1, low, high),
                bias,
                None,
            )
            context_out[part, low:high] = context
            stats_out[part, wide : wide + HD] = top
            stats_out[part, wide + HD : wide + 2 * HD] = total


def last_attention(place, query_mask, key_masks, query_ref, raw_ref, *refs):
    pack, context_ref, stats_ref, *outs = refs
    rows, width = query_ref.shape[0] // 2, query_ref.shape[1]
    heads = width // HD
    part = slice(place * rows, (place + 1) * rows)
    bias = key_bias(raw_ref, query_mask, key_masks)
    lane = lax.broadcasted_iota(jnp.int32, (1, HD), 1)
    logs = jnp.zeros((rows, HD), jnp.float32)
    for head in range(heads):
        low, high = head * HD, (head + 1) * HD
        wide = 2 * low
        top, total, context = absorb(
            query_ref[part, low:high],
            columns_of(pack, 0, low, high),
            columns_of(pack, 1, low, high),
            bias,
            (
                stats_ref[part, wide : wide + HD],
                stats_ref[part, wide + HD : wide + 2 * HD],
                context_ref[part, low:high],
            ),
        )
        outs[0][:rows, low:high] = (context * (1.0 / total)).astype(outs[0].dtype)
        logs = jnp.where(lane == head, top + jnp.log2(total), logs)
    lines = logs.T
    sub = lax.broadcasted_iota(jnp.int32, (EXTRA, HD), 0)
    for head in range(heads):
        low, high = head * HD, (head + 1) * HD
        value = lines[head : head + 1, :]
        if place == 0:
            outs[1][:, low:high] = jnp.broadcast_to(value, (8, HD))
        else:
            first = value.astype(jnp.bfloat16).astype(jnp.float32)
            second = (value - first).astype(jnp.bfloat16).astype(jnp.float32)
            third = value - first - second
            outs[0][rows:, low:high] = jnp.where(
                sub == 0, first, jnp.where(sub == 1, second, third)
            ).astype(jnp.bfloat16)


def gate_kernel(step_ref, table_ref, out_ref):
    rows = out_ref.shape[0] // 2
    start = lax.axis_index("tm") * HD
    first = step_ref[start // FRAME_TOK]
    last = step_ref[(start + HD - 1) // FRAME_TOK]
    out_ref[:rows, :] = jnp.broadcast_to(table_ref[pl.ds(first, 1), :], (rows, out_ref.shape[1]))
    out_ref[rows:, :] = jnp.broadcast_to(table_ref[pl.ds(last, 1), :], (rows, out_ref.shape[1]))


def merge_kernel(own_ref, logs_ref, packet_ref, gate_ref, out_ref):
    rows, width = own_ref.shape
    pieces = packet_ref[rows:, :].astype(jnp.float32)
    other = pieces[0:1] + pieces[1:2] + pieces[2:3]
    top = jnp.maximum(logs_ref[:1, :], other)
    own_weight = jnp.exp2(logs_ref[:1, :] - top)
    other_weight = jnp.exp2(other - top)
    share = own_weight / (own_weight + other_weight)
    start = lax.axis_index("tm") * rows
    first_rows = (start // FRAME_TOK + 1) * FRAME_TOK - start
    row_ids = lax.broadcasted_iota(jnp.int32, (rows, 1), 0)
    for low in range(0, width, HD):
        high = low + HD
        column = spread(share[:, low:high])
        other_part = packet_ref[:rows, low:high].astype(jnp.float32)
        context = own_ref[:, low:high] * column + other_part * (1.0 - column)
        gate = jnp.where(
            row_ids < first_rows, gate_ref[0:1, low:high], gate_ref[8:9, low:high]
        )
        out_ref[:, low:high] = (context * gate).astype(jnp.bfloat16)


def exchange(array, mask):
    count = lax.axis_size("tm")
    return lax.ppermute(array, "tm", [(i, i ^ mask) for i in range(count)])


def gathered(array, bits):
    held = {0: array}
    for bit in bits:
        for mask in list(held):
            held[mask ^ bit] = exchange(held[mask], bit)
    return held


def local(
    query_proj, key_proj, value_proj, query_gain, key_gain, gate_table, frame_step, far_blocks
):
    rows, width = query_proj.shape
    count = lax.axis_size("tm")
    splits = lax.axis_size("head")
    params = pltpu.CompilerParams(vmem_limit_bytes=(8 + count // 2) * 2**20)
    query_mask = count // 4
    bits = [1 << place for place in range(1, count.bit_length() - 1)]
    bits = [bit for bit in bits[::-1] if bit != query_mask]
    query_gain = query_gain.reshape(1, width)
    key_gain = key_gain.reshape(1, width)

    lines = 2 + 2 ** len(bits)
    lines += -lines % 8
    query_packet, own_key, own_value, own_sums = pl.pallas_call(
        own_kernel,
        out_shape=[
            jax.ShapeDtypeStruct((rows + EXTRA, width), jnp.bfloat16),
            jax.ShapeDtypeStruct((rows, width), jnp.bfloat16),
            jax.ShapeDtypeStruct((rows, width), jnp.bfloat16),
            jax.ShapeDtypeStruct((lines, rows), jnp.float32),
        ],
        in_specs=[ANY] * 4,
        out_specs=[VMEM] * 4,
        scratch_shapes=[
            pltpu.VMEM((rows, width), jnp.bfloat16),
            pltpu.VMEM(far_blocks.shape, jnp.int32),
            pltpu.SemaphoreType.DMA((4,)),
        ],
    )(query_proj, key_proj, value_proj, far_blocks)
    queries = [query_packet, exchange(query_packet, query_mask)]
    keys = gathered(key_proj, bits)
    keys[0] = own_key
    masks = sorted(keys, key=lambda mask: (mask.bit_count(), -mask))
    near = 1 + len(bits)

    def summed(sums, sources, lines, cost):
        return pl.pallas_call(
            functools.partial(sums_kernel, lines),
            out_shape=jax.ShapeDtypeStruct(own_sums.shape, jnp.float32),
            in_specs=[VMEM] * (1 + len(sources)),
            out_specs=VMEM,
            compiler_params=params,
            cost_estimate=pl.CostEstimate(flops=cost, bytes_accessed=0, transcendentals=0),
        )(sums, *sources)

    values = gathered(own_value, bits[1:])
    sums = summed(own_sums, [keys[bits[0]]], [3], AHEAD)
    sources = [queries[1]] + [keys[mask] for mask in masks[2:near]]
    sources += [values[bit] for bit in bits[1:]]
    sums, late_value = pl.pallas_call(
        functools.partial(near_sums_kernel, [2, *range(4, near + 2)]),
        out_shape=[
            jax.ShapeDtypeStruct(own_sums.shape, jnp.float32),
            jax.ShapeDtypeStruct((rows, width), jnp.bfloat16),
        ],
        in_specs=[VMEM] * (2 + len(sources)),
        out_specs=[VMEM] * 2,
        compiler_params=params,
    )(sums, own_value, *sources)
    late_values = gathered(exchange(late_value, bits[0]), bits[1:])
    values.update({mask ^ bits[0]: value for mask, value in late_values.items()})
    sums = summed(sums, [keys[mask] for mask in masks[near:]], range(near + 2, len(masks) + 2), 0)
    if splits == 2:
        others = lax.ppermute(sums, "head", [(0, 1), (1, 0)])
    else:
        sums = lax.psum(sums, "head")
        others = jnp.zeros_like(sums)

    factors = pl.pallas_call(
        functools.partial(factor_kernel, width * splits),
        out_shape=jax.ShapeDtypeStruct(sums.shape, jnp.float32),
        in_specs=[VMEM] * 2,
        out_specs=VMEM,
        compiler_params=params,
        cost_estimate=pl.CostEstimate(flops=AHEAD, bytes_accessed=0, transcendentals=0),
    )(sums, others)
    pack = pl.pallas_call(
        functools.partial(pack_kernel, len(masks)),
        out_shape=jax.ShapeDtypeStruct((2 * len(masks) * rows, width), jnp.bfloat16),
        in_specs=[VMEM] * (2 + 2 * len(masks)),
        out_specs=VMEM,
        compiler_params=params,
    )(
        key_gain,
        factors,
        *[keys[mask] for mask in masks],
        *[values[mask] for mask in masks],
    )
    other_pack = exchange(pack, 1)

    query_norm, context, stats = pl.pallas_call(
        functools.partial(own_attention, [0, query_mask], masks),
        out_shape=[
            jax.ShapeDtypeStruct((2 * rows, width), jnp.bfloat16),
            jax.ShapeDtypeStruct((2 * rows, width), jnp.float32),
            jax.ShapeDtypeStruct((2 * rows, 2 * width), jnp.float32),
        ],
        in_specs=[VMEM] * 5,
        out_specs=[VMEM] * 3,
        compiler_params=params,
    )(query_gain, factors, *queries, pack)

    def last_part(place, out_shape):
        return pl.pallas_call(
            functools.partial(
                last_attention, place, place * query_mask, [mask ^ 1 for mask in masks]
            ),
            out_shape=out_shape,
            in_specs=[VMEM] * 5,
            out_specs=[VMEM] * len(out_shape),
            compiler_params=params,
        )(query_norm, queries[place], other_pack, context, stats)

    (packet,) = last_part(1, [jax.ShapeDtypeStruct((rows + EXTRA, width), jnp.bfloat16)])
    own, own_logs = last_part(
        0,
        [
            jax.ShapeDtypeStruct((rows, width), jnp.float32),
            jax.ShapeDtypeStruct((8, width), jnp.float32),
        ],
    )
    gates = pl.pallas_call(
        gate_kernel,
        out_shape=jax.ShapeDtypeStruct((16, width), jnp.float32),
        in_specs=[SMEM, VMEM],
        out_specs=VMEM,
        compiler_params=params,
    )(frame_step, gate_table)
    packet = exchange(packet, query_mask)

    return pl.pallas_call(
        merge_kernel,
        out_shape=jax.ShapeDtypeStruct((rows, width), jnp.bfloat16),
        in_specs=[VMEM] * 4,
        out_specs=VMEM,
        compiler_params=params,
    )(own, own_logs, packet, gates)


def solution(mesh):
    return jax.shard_map(
        local,
        mesh=mesh,
        in_specs=(
            P("tm", "head"),
            P("tm", "head"),
            P("tm", "head"),
            P("head"),
            P("head"),
            P(None, "head"),
            P(),
            P("tm", None),
        ),
        out_specs=P("tm", "head"),
        check_vma=False,
    )
```

```python
import functools

import jax
import jax.numpy as jnp
from jax import lax
from jax.experimental import pallas as pl
from jax.experimental.pallas import tpu as pltpu
from jax.sharding import PartitionSpec as P

HD = 128
BLK = 64
FRAME_TOK = 1560
EPSILON = 1e-06
LOG2E = 1.4426950408889634
SCALE = HD ** (-0.5) * LOG2E
MASKED = -1e30
EXTRA = 16
AHEAD = 4 * 10**9
QUERY_MASKS = (0, 2, 4, 6)
ANY = pl.BlockSpec(memory_space=pl.ANY)
VMEM = pl.BlockSpec(memory_space=pltpu.VMEM)
SMEM = pl.BlockSpec(memory_space=pltpu.SMEM)


def spread(row):
    return jnp.broadcast_to(row, (row.shape[1], row.shape[1])).T


def squares(source_ref):
    wide = source_ref[...].astype(jnp.float32)
    square = wide * wide
    part = square[:, :HD]
    for low in range(HD, square.shape[1], HD):
        part = part + square[:, low : low + HD]
    return jnp.sum(part.T, axis=0, keepdims=True)


def sums_kernel(query_hbm, key_hbm, out_ref, query_ref, key_ref, sems):
    copies = [
        pltpu.make_async_copy(query_hbm, query_ref, sems.at[0]),
        pltpu.make_async_copy(key_hbm, key_ref, sems.at[1]),
    ]
    for copy in copies:
        copy.start()
    for place, ref in enumerate((query_ref, key_ref)):
        copies[place].wait()
        out_ref[place : place + 1, :] = squares(ref)


def normed(source_ref, factor, gain_ref):
    parts = []
    for low in range(0, source_ref.shape[1], HD):
        wide = source_ref[:, low : low + HD].astype(jnp.float32)
        parts.append((wide * factor * gain_ref[:, low : low + HD]).astype(jnp.bfloat16))
    return jnp.concatenate(parts, axis=1)


def norm_kernel(
    full_width,
    query_ref,
    key_ref,
    value_ref,
    query_gain_ref,
    key_gain_ref,
    far_ref,
    own_ref,
    other_ref,
    query_out,
    key_out,
    pack_out,
):
    rows, width = query_ref.shape
    factors = lax.rsqrt((own_ref[...] + other_ref[...]) / full_width + EPSILON)
    key = normed(key_ref, spread(factors[1:2, :]), key_gain_ref)
    key_out[...] = key
    pack_out[:rows, :] = key
    pack_out[rows:, :] = value_ref[...]
    query_out[:rows, :] = normed(query_ref, spread(factors[0:1, :]), query_gain_ref)
    far = far_ref[...].astype(jnp.float32)
    far = jnp.concatenate([far, jnp.full((1, HD - far.shape[1]), -1.0)], axis=1)
    query_out[rows:, :HD] = jnp.broadcast_to(far, (EXTRA, HD)).astype(jnp.bfloat16)
    query_out[rows:, HD:] = jnp.zeros((EXTRA, width - HD), jnp.bfloat16)


def pack_kernel(*refs):
    *sources, out_ref = refs
    rows = sources[0].shape[0]
    for place, source_ref in enumerate(sources):
        out_ref[place * rows : (place + 1) * rows, :] = source_ref[...]


def key_bias(query_ref, query_mask, key_masks):
    me = lax.axis_index("tm")
    lane = lax.broadcasted_iota(jnp.int32, (1, HD), 1)
    half = (lane >= BLK).astype(jnp.float32)
    far = query_ref[HD:, :HD].astype(jnp.float32)[:1]
    parts = []
    for key_mask in key_masks:
        query_id, key_id = me ^ query_mask, me ^ key_mask
        choice = jnp.sum(jnp.where(lane == key_id, far, 0.0), axis=1, keepdims=True)
        taken = (choice == half) | (jnp.abs(query_id - key_id) <= 1)
        parts.append(jnp.where(taken, 0.0, MASKED))
    return jnp.concatenate(parts, axis=1)


def absorb(queries, packs, biases, olds, low):
    rows, high = HD, low + HD
    halves = [pack.shape[0] // 2 for pack in packs]
    keys = [pack[:half, low:high] for pack, half in zip(packs, halves)]
    values = [pack[half:, low:high] for pack, half in zip(packs, halves)]
    scores = lax.dot_general(
        jnp.concatenate([query[:rows, low:high] for query in queries], axis=0),
        jnp.concatenate(keys, axis=0),
        (((1,), (1,)), ((), ())),
        preferred_element_type=jnp.float32,
    )
    tops, totals, rounded = [], [], []
    for place, bias in enumerate(biases):
        logits = scores[place * rows : (place + 1) * rows] * SCALE + bias
        top = jnp.broadcast_to(jnp.max(logits, axis=1, keepdims=True), (rows, HD))
        if olds is not None:
            top = jnp.maximum(top, olds[place][0])
        weights = [
            jnp.exp2(logits[:, left : left + HD] - top)
            for left in range(0, logits.shape[1], HD)
        ]
        total = jnp.sum(functools.reduce(jnp.add, weights), axis=1, keepdims=True)
        tops.append(top)
        totals.append(jnp.broadcast_to(total, (rows, HD)))
        rounded.append(
            jnp.concatenate([weight.astype(jnp.bfloat16) for weight in weights], axis=1)
        )
    added = jnp.dot(
        jnp.concatenate(rounded, axis=0),
        jnp.concatenate(values, axis=0),
        preferred_element_type=jnp.float32,
    )
    results = []
    for place in range(len(biases)):
        context = added[place * rows : (place + 1) * rows]
        total = totals[place]
        if olds is not None:
            fade = jnp.exp2(olds[place][0] - tops[place])
            total = total + olds[place][1] * fade
            context = context + olds[place][2] * fade
        results.append((tops[place], total, context))
    return results


def held_state(context_ref, stats_ref, place, low):
    part, wide = slice(place * HD, (place + 1) * HD), 2 * low
    return (
        stats_ref[part, wide : wide + HD],
        stats_ref[part, wide + HD : wide + 2 * HD],
        context_ref[part, low : low + HD],
    )


def step_kernel(key_masks, resumed, *refs):
    count = len(QUERY_MASKS)
    queries, refs = refs[:count], refs[count:]
    held = len(refs) - 2 - 2 * resumed
    packs, olds, (context_out, stats_out) = refs[:held], refs[held:-2], refs[-2:]
    biases = [key_bias(ref, mask, key_masks) for ref, mask in zip(queries, QUERY_MASKS)]
    for low in range(0, context_out.shape[1], HD):
        state = None
        if resumed:
            state = [held_state(*olds, place, low) for place in range(count)]
        for place, result in enumerate(absorb(queries, packs, biases, state, low)):
            part, wide = slice(place * HD, (place + 1) * HD), 2 * low
            top, total, context = result
            context_out[part, low : low + HD] = context
            stats_out[part, wide : wide + HD] = top
            stats_out[part, wide + HD : wide + 2 * HD] = total


def last_kernel(place, key_masks, query_ref, pack_ref, context_ref, stats_ref, *outs):
    rows, width = HD, context_ref.shape[1]
    heads = width // HD
    bias = key_bias(query_ref, QUERY_MASKS[place], key_masks)
    lane = lax.broadcasted_iota(jnp.int32, (1, HD), 1)
    logs = jnp.zeros((rows, HD), jnp.float32)
    for head in range(heads):
        low, high = head * HD, (head + 1) * HD
        old = held_state(context_ref, stats_ref, place, low)
        ((top, total, context),) = absorb([query_ref], [pack_ref], [bias], [old], low)
        outs[0][:rows, low:high] = (context * (1.0 / total)).astype(outs[0].dtype)
        logs = jnp.where(lane == head, top + jnp.log2(total), logs)
    lines = logs.T
    sub = lax.broadcasted_iota(jnp.int32, (EXTRA, HD), 0)
    for head in range(heads):
        low, high = head * HD, (head + 1) * HD
        value = lines[head : head + 1, :]
        if place == 0:
            outs[1][:, low:high] = jnp.broadcast_to(value, (8, HD))
        else:
            first = value.astype(jnp.bfloat16).astype(jnp.float32)
            second = (value - first).astype(jnp.bfloat16).astype(jnp.float32)
            third = value - first - second
            outs[0][rows:, low:high] = jnp.where(
                sub == 0, first, jnp.where(sub == 1, second, third)
            ).astype(jnp.bfloat16)


def gate_kernel(step_ref, table_ref, out_ref):
    rows = out_ref.shape[0] // 2
    start = lax.axis_index("tm") * HD
    first = step_ref[start // FRAME_TOK]
    last = step_ref[(start + HD - 1) // FRAME_TOK]
    out_ref[:rows, :] = jnp.broadcast_to(table_ref[pl.ds(first, 1), :], (rows, out_ref.shape[1]))
    out_ref[rows:, :] = jnp.broadcast_to(table_ref[pl.ds(last, 1), :], (rows, out_ref.shape[1]))


def merge_kernel(own_ref, logs_ref, *refs):
    *packets, gate_ref, out_ref = refs
    rows, width = own_ref.shape
    logs = [logs_ref[:1, :]]
    for packet in packets:
        pieces = packet[rows:, :].astype(jnp.float32)
        logs.append(pieces[0:1] + pieces[1:2] + pieces[2:3])
    top = functools.reduce(jnp.maximum, logs)
    shares = [jnp.exp2(log - top) for log in logs]
    scale = 1.0 / sum(shares)
    shares = [share * scale for share in shares]
    start = lax.axis_index("tm") * rows
    first_rows = (start // FRAME_TOK + 1) * FRAME_TOK - start
    row_ids = lax.broadcasted_iota(jnp.int32, (rows, 1), 0)
    for low in range(0, width, HD):
        high = low + HD
        context = own_ref[:, low:high] * spread(shares[0][:, low:high])
        for packet, share in zip(packets, shares[1:]):
            context += packet[:rows, low:high].astype(jnp.float32) * spread(share[:, low:high])
        gate = jnp.where(
            row_ids < first_rows, gate_ref[0:1, low:high], gate_ref[8:9, low:high]
        )
        out_ref[:, low:high] = (context * gate).astype(jnp.bfloat16)


def exchange(array, mask):
    count = lax.axis_size("tm")
    return lax.ppermute(array, "tm", [(i, i ^ mask) for i in range(count)])


def gathered(array, bits):
    held = {0: array}
    for bit in bits:
        for mask in list(held):
            held[mask ^ bit] = exchange(held[mask], bit)
    return held


def cost(flops):
    return pl.CostEstimate(flops=flops, bytes_accessed=0, transcendentals=0)


def local(
    query_proj, key_proj, value_proj, query_gain, key_gain, gate_table, frame_step, far_blocks
):
    rows, width = query_proj.shape
    count = lax.axis_size("tm")
    splits = lax.axis_size("head")
    params = pltpu.CompilerParams(vmem_limit_bytes=(8 + count // 2) * 2**20)
    far_bits = [1 << place for place in range(3, count.bit_length() - 1)]

    sums = pl.pallas_call(
        sums_kernel,
        out_shape=jax.ShapeDtypeStruct((2, rows), jnp.float32),
        in_specs=[ANY, ANY],
        out_specs=VMEM,
        scratch_shapes=[
            pltpu.VMEM((rows, width), jnp.bfloat16),
            pltpu.VMEM((rows, width), jnp.bfloat16),
            pltpu.SemaphoreType.DMA((2,)),
        ],
    )(query_proj, key_proj)
    if splits == 2:
        others = lax.ppermute(sums, "head", [(0, 1), (1, 0)])
    else:
        sums = lax.psum(sums, "head")
        others = jnp.zeros_like(sums)

    query_packet, key_norm, near_pack = pl.pallas_call(
        functools.partial(norm_kernel, width * splits),
        out_shape=(
            jax.ShapeDtypeStruct((rows + EXTRA, width), jnp.bfloat16),
            jax.ShapeDtypeStruct((rows, width), jnp.bfloat16),
            jax.ShapeDtypeStruct((2 * rows, width), jnp.bfloat16),
        ),
        in_specs=[VMEM] * 8,
        out_specs=[VMEM] * 3,
        compiler_params=params,
    )(
        query_proj,
        key_proj,
        value_proj,
        query_gain.reshape(1, width),
        key_gain.reshape(1, width),
        far_blocks,
        sums,
        others,
    )
    values = gathered(value_proj, far_bits)
    keys = gathered(key_norm, far_bits)
    queries = [query_packet] + [exchange(query_packet, mask) for mask in QUERY_MASKS[1:]]
    far = [mask for mask in keys if mask]
    far_pack = pl.pallas_call(
        pack_kernel,
        out_shape=jax.ShapeDtypeStruct((2 * len(far) * rows, width), jnp.bfloat16),
        in_specs=[VMEM] * (2 * len(far)),
        out_specs=VMEM,
        compiler_params=params,
        cost_estimate=cost(AHEAD),
    )(*[keys[mask] for mask in far], *[values[mask] for mask in far])

    def step(masks, packs, *old):
        stacked = len(QUERY_MASKS) * rows
        return pl.pallas_call(
            functools.partial(step_kernel, masks, bool(old)),
            out_shape=[
                jax.ShapeDtypeStruct((stacked, width), jnp.float32),
                jax.ShapeDtypeStruct((stacked, 2 * width), jnp.float32),
            ],
            in_specs=[VMEM] * (len(QUERY_MASKS) + len(packs) + len(old)),
            out_specs=[VMEM] * 2,
            compiler_params=params,
            cost_estimate=cost(0 if old else 2 * AHEAD),
        )(*queries, *packs, *old)

    state = step([0, 1], [near_pack, exchange(near_pack, 1)])
    last_pack = exchange(far_pack, 1)
    state = step(far, [far_pack], *state)

    def last(place, out_shape):
        return pl.pallas_call(
            functools.partial(last_kernel, place, [mask ^ 1 for mask in far]),
            out_shape=out_shape,
            in_specs=[VMEM] * 4,
            out_specs=[VMEM] * len(out_shape),
            compiler_params=params,
        )(queries[place], last_pack, *state)

    packets = {}
    for place in (3, 1, 2):
        (packet,) = last(place, [jax.ShapeDtypeStruct((rows + EXTRA, width), jnp.bfloat16)])
        packets[place] = exchange(packet, QUERY_MASKS[place])
    own, own_logs = last(
        0,
        [
            jax.ShapeDtypeStruct((rows, width), jnp.float32),
            jax.ShapeDtypeStruct((8, width), jnp.float32),
        ],
    )
    gates = pl.pallas_call(
        gate_kernel,
        out_shape=jax.ShapeDtypeStruct((16, width), jnp.float32),
        in_specs=[SMEM, VMEM],
        out_specs=VMEM,
        compiler_params=params,
    )(frame_step, gate_table)
    return pl.pallas_call(
        merge_kernel,
        out_shape=jax.ShapeDtypeStruct((rows, width), jnp.bfloat16),
        in_specs=[VMEM] * 6,
        out_specs=VMEM,
        compiler_params=params,
    )(own, own_logs, packets[1], packets[2], packets[3], gates)


def solution(mesh):
    return jax.shard_map(
        local,
        mesh=mesh,
        in_specs=(
            P("tm", "head"),
            P("tm", "head"),
            P("tm", "head"),
            P("head"),
            P("head"),
            P(None, "head"),
            P(),
            P("tm", None),
        ),
        out_specs=P("tm", "head"),
        check_vma=False,
    )
```

```python
import functools

import jax
import jax.numpy as jnp
from jax import lax
from jax.experimental import pallas as pl
from jax.experimental.pallas import tpu as pltpu
from jax.sharding import PartitionSpec as P

HD = 128
BLK = 64
FRAME_TOK = 1560
EPSILON = 1e-06
LOG2E = 1.4426950408889634
SCALE = HD ** (-0.5) * LOG2E
MASKED = -1e30
EXTRA = 16
ANY = pl.BlockSpec(memory_space=pl.ANY)
VMEM = pl.BlockSpec(memory_space=pltpu.VMEM)
SMEM = pl.BlockSpec(memory_space=pltpu.SMEM)


def spread(row):
    return jnp.broadcast_to(row, (row.shape[1], row.shape[1])).T


def squares(source_ref):
    wide = source_ref[:HD, :].astype(jnp.float32)
    square = wide * wide
    part = square[:, :HD]
    for low in range(HD, square.shape[1], HD):
        part = part + square[:, low : low + HD]
    return jnp.sum(part.T, axis=0, keepdims=True)


def own_kernel(
    query_hbm,
    key_hbm,
    value_hbm,
    far_hbm,
    query_out,
    key_out,
    value_out,
    sums_out,
    query_ref,
    far_ref,
    sems,
):
    rows, width = query_ref.shape
    copies = [
        pltpu.make_async_copy(query_hbm, query_ref, sems.at[0]),
        pltpu.make_async_copy(key_hbm, key_out, sems.at[1]),
        pltpu.make_async_copy(far_hbm, far_ref, sems.at[2]),
        pltpu.make_async_copy(value_hbm, value_out, sems.at[3]),
    ]
    for copy in copies:
        copy.start()
    query_out[rows:, HD:] = jnp.zeros((EXTRA, width - HD), jnp.bfloat16)
    sums_out[...] = jnp.zeros_like(sums_out)
    copies[0].wait()
    query_out[:rows, :] = query_ref[...]
    sums_out[0:1, :] = squares(query_ref)
    copies[1].wait()
    sums_out[1:2, :] = squares(key_out)
    copies[2].wait()
    far = far_ref[...].astype(jnp.float32)
    far = jnp.concatenate([far, jnp.full((1, HD - far.shape[1]), -1.0)], axis=1)
    query_out[rows:, :HD] = jnp.broadcast_to(far, (EXTRA, HD)).astype(jnp.bfloat16)
    copies[3].wait()


def sums_kernel(lines, before_ref, *refs):
    *sources, out_ref = refs
    out_ref[...] = before_ref[...]
    for line, source_ref in zip(lines, sources):
        out_ref[line : line + 1, :] = squares(source_ref)


def factor_of(line, full_width):
    return spread(lax.rsqrt(line / full_width + EPSILON))


def normed(source_ref, factor, gain_ref):
    parts = []
    for low in range(0, source_ref.shape[1], HD):
        wide = source_ref[:HD, low : low + HD].astype(jnp.float32)
        parts.append((wide * factor * gain_ref[:, low : low + HD]).astype(jnp.bfloat16))
    return jnp.concatenate(parts, axis=1)


def query_kernel(full_width, key_masks, gain_ref, own_ref, other_ref, *refs):
    queries, (query_out, bias_out) = refs[:2], refs[2:]
    me = lax.axis_index("tm")
    query_mask = lax.axis_size("tm") // 4
    lane = lax.broadcasted_iota(jnp.int32, (1, HD), 1)
    half = (lane >= BLK).astype(jnp.float32)
    for place, query_ref in enumerate(queries):
        line = 2 * place
        total = own_ref[line : line + 1, :] + other_ref[line : line + 1, :]
        query_out[place * HD : (place + 1) * HD, :] = normed(
            query_ref, factor_of(total, full_width), gain_ref
        )
        far = query_ref[HD:, :HD].astype(jnp.float32)[:1]
        query_id = me ^ (place * query_mask)
        for block, key_mask in enumerate(key_masks):
            key_id = me ^ key_mask
            choice = jnp.sum(jnp.where(lane == key_id, far, 0.0), axis=1, keepdims=True)
            taken = (choice == half) | (jnp.abs(query_id - key_id) <= 1)
            bias_out[8 * place : 8 * place + 8, block * HD : (block + 1) * HD] = (
                jnp.broadcast_to(jnp.where(taken, 0.0, MASKED), (8, HD))
            )


def pack_kernel(full_width, near, held, gain_ref, own_ref, other_ref, cross_ref, *refs):
    keys, values, pack_out = refs[:held], refs[held : 2 * held], refs[2 * held]
    for place, key_ref in enumerate(keys):
        line = 1 + place + (place > 0)
        if place < near:
            total = own_ref[line : line + 1, :] + other_ref[line : line + 1, :]
        else:
            total = squares(key_ref) + cross_ref[3:4, :]
        pack_out[place * HD : (place + 1) * HD, :] = normed(
            key_ref, factor_of(total, full_width), gain_ref
        )
    for place, value_ref in enumerate(values, start=held):
        pack_out[place * HD : (place + 1) * HD, :] = value_ref[...]


def absorb(query, pack_ref, biases, olds, low):
    high, half = low + HD, pack_ref.shape[0] // 2
    scores = lax.dot_general(
        query,
        pack_ref[:half, low:high],
        (((1,), (1,)), ((), ())),
        preferred_element_type=jnp.float32,
    )
    tops, totals, rounded = [], [], []
    for place, bias in enumerate(biases):
        logits = scores[place * HD : (place + 1) * HD] * SCALE + bias
        top = jnp.broadcast_to(jnp.max(logits, axis=1, keepdims=True), (HD, HD))
        if olds is not None:
            top = jnp.maximum(top, olds[place][0])
        weights = [
            jnp.exp2(logits[:, left : left + HD] - top)
            for left in range(0, logits.shape[1], HD)
        ]
        total = jnp.sum(functools.reduce(jnp.add, weights), axis=1, keepdims=True)
        tops.append(top)
        totals.append(jnp.broadcast_to(total, (HD, HD)))
        rounded.append(
            jnp.concatenate([weight.astype(jnp.bfloat16) for weight in weights], axis=1)
        )
    added = jnp.dot(
        jnp.concatenate(rounded, axis=0),
        pack_ref[half:, low:high],
        preferred_element_type=jnp.float32,
    )
    results = []
    for place in range(len(biases)):
        context = added[place * HD : (place + 1) * HD]
        total = totals[place]
        if olds is not None:
            fade = jnp.exp2(olds[place][0] - tops[place])
            total = total + olds[place][1] * fade
            context = context + olds[place][2] * fade
        results.append((tops[place], total, context))
    return results


def own_attention(query_ref, bias_ref, pack_ref, context_out, stats_out):
    keys = pack_ref.shape[0] // 2
    biases = [bias_ref[8 * place : 8 * place + 1, :keys] for place in range(2)]
    for low in range(0, query_ref.shape[1], HD):
        results = absorb(query_ref[:, low : low + HD], pack_ref, biases, None, low)
        for place, (top, total, context) in enumerate(results):
            part, wide = slice(place * HD, (place + 1) * HD), 2 * low
            context_out[part, low : low + HD] = context
            stats_out[part, wide : wide + HD] = top
            stats_out[part, wide + HD : wide + 2 * HD] = total


def last_attention(place, query_ref, bias_ref, pack_ref, context_ref, stats_ref, *outs):
    width, keys = query_ref.shape[1], pack_ref.shape[0] // 2
    part = slice(place * HD, (place + 1) * HD)
    bias = bias_ref[8 * place : 8 * place + 1, keys:]
    lane = lax.broadcasted_iota(jnp.int32, (1, HD), 1)
    columns = jnp.zeros((HD, HD), jnp.float32)
    for low in range(0, width, HD):
        wide = 2 * low
        old = (
            stats_ref[part, wide : wide + HD],
            stats_ref[part, wide + HD : wide + 2 * HD],
            context_ref[part, low : low + HD],
        )
        ((top, total, context),) = absorb(
            query_ref[part, low : low + HD], pack_ref, [bias], [old], low
        )
        outs[0][:HD, low : low + HD] = context.astype(outs[0].dtype)
        line = wide // HD
        columns = jnp.where(lane == line, top, jnp.where(lane == line + 1, total, columns))
    lines = columns.T
    sub = lax.broadcasted_iota(jnp.int32, (EXTRA, HD), 0)
    for low in range(0, width, HD):
        line = 2 * low // HD
        pair = (lines[line : line + 1, :], lines[line + 1 : line + 2, :])
        if place == 0:
            for row, value in enumerate(pair):
                outs[1][8 * row : 8 * row + 8, low : low + HD] = jnp.broadcast_to(value, (8, HD))
        else:
            piece_rows = jnp.zeros((EXTRA, HD), jnp.float32)
            for row, value in enumerate(pair):
                first = value.astype(jnp.bfloat16).astype(jnp.float32)
                second = (value - first).astype(jnp.bfloat16).astype(jnp.float32)
                for piece, part_value in enumerate((first, second, value - first - second)):
                    piece_rows = jnp.where(sub == 3 * row + piece, part_value, piece_rows)
            outs[0][HD:, low : low + HD] = piece_rows.astype(jnp.bfloat16)


def gate_kernel(step_ref, table_ref, out_ref):
    rows = out_ref.shape[0] // 2
    start = lax.axis_index("tm") * HD
    first = step_ref[start // FRAME_TOK]
    last = step_ref[(start + HD - 1) // FRAME_TOK]
    out_ref[:rows, :] = jnp.broadcast_to(table_ref[pl.ds(first, 1), :], (rows, out_ref.shape[1]))
    out_ref[rows:, :] = jnp.broadcast_to(table_ref[pl.ds(last, 1), :], (rows, out_ref.shape[1]))


def merge_kernel(own_ref, lines_ref, packet_ref, gate_ref, out_ref):
    rows, width = own_ref.shape
    pieces = packet_ref[rows:, :].astype(jnp.float32)
    own_top, own_total = lines_ref[0:1, :], lines_ref[8:9, :]
    other_top = pieces[0:1] + pieces[1:2] + pieces[2:3]
    other_total = pieces[3:4] + pieces[4:5] + pieces[5:6]
    top = jnp.maximum(own_top, other_top)
    own_share, other_share = jnp.exp2(own_top - top), jnp.exp2(other_top - top)
    scale = 1.0 / (own_total * own_share + other_total * other_share)
    own_share, other_share = own_share * scale, other_share * scale
    start = lax.axis_index("tm") * rows
    first_rows = (start // FRAME_TOK + 1) * FRAME_TOK - start
    row_ids = lax.broadcasted_iota(jnp.int32, (rows, 1), 0)
    for low in range(0, width, HD):
        high = low + HD
        context = own_ref[:, low:high] * spread(own_share[:, low:high])
        other = packet_ref[:rows, low:high].astype(jnp.float32)
        context += other * spread(other_share[:, low:high])
        gate = jnp.where(
            row_ids < first_rows, gate_ref[0:1, low:high], gate_ref[8:9, low:high]
        )
        out_ref[:, low:high] = (context * gate).astype(jnp.bfloat16)


def exchange(array, mask):
    count = lax.axis_size("tm")
    return lax.ppermute(array, "tm", [(i, i ^ mask) for i in range(count)])


def gathered(array, bits):
    held = {0: array}
    for bit in bits:
        for mask in list(held):
            held[mask ^ bit] = exchange(held[mask], bit)
    return held


def local(
    query_proj, key_proj, value_proj, query_gain, key_gain, gate_table, frame_step, far_blocks
):
    rows, width = query_proj.shape
    count = lax.axis_size("tm")
    splits = lax.axis_size("head")
    full_width = width * splits
    params = pltpu.CompilerParams(vmem_limit_bytes=(8 + count // 2) * 2**20)
    query_mask = count // 4
    bits = [1 << place for place in range(1, count.bit_length() - 1)]
    bits = [bit for bit in bits[::-1] if bit != query_mask]
    query_gain = query_gain.reshape(1, width)
    key_gain = key_gain.reshape(1, width)

    lines = 2 + 2 ** len(bits)
    lines += -lines % 8
    query_packet, own_key, own_value, own_sums = pl.pallas_call(
        own_kernel,
        out_shape=[
            jax.ShapeDtypeStruct((rows + EXTRA, width), jnp.bfloat16),
            jax.ShapeDtypeStruct((rows, width), jnp.bfloat16),
            jax.ShapeDtypeStruct((rows, width), jnp.bfloat16),
            jax.ShapeDtypeStruct((lines, rows), jnp.float32),
        ],
        in_specs=[ANY] * 4,
        out_specs=[VMEM] * 4,
        scratch_shapes=[
            pltpu.VMEM((rows, width), jnp.bfloat16),
            pltpu.VMEM(far_blocks.shape, jnp.int32),
            pltpu.SemaphoreType.DMA((4,)),
        ],
    )(query_proj, key_proj, value_proj, far_blocks)
    keys = gathered(key_proj, bits)
    keys[0] = own_key
    values = gathered(own_value, bits)
    queries = [query_packet, exchange(query_packet, query_mask)]
    masks = sorted(keys, key=lambda mask: (mask.bit_count(), -mask))
    near = 1 + len(bits)

    def summed(sums, sources, held):
        return pl.pallas_call(
            functools.partial(sums_kernel, held),
            out_shape=jax.ShapeDtypeStruct(own_sums.shape, jnp.float32),
            in_specs=[VMEM] * (1 + len(sources)),
            out_specs=VMEM,
            compiler_params=params,
        )(sums, *sources)

    sources = [queries[1]] + [keys[mask] for mask in masks[1:near]]
    sums = summed(own_sums, sources, range(2, near + 2))
    if splits == 2:
        others = lax.ppermute(sums, "head", [(0, 1), (1, 0)])
        pairs = []
        for i in range(2 * count):
            pairs.append((i, ((i // 2) ^ bits[1]) * 2 + (i % 2 ^ 1)))
        crossed = lax.ppermute(sums, ("tm", "head"), pairs)
    else:
        sources = [keys[mask] for mask in masks[near:]]
        sums = summed(sums, sources, range(near + 2, len(masks) + 2))
        sums = lax.psum(sums, "head")
        others = crossed = jnp.zeros_like(sums)

    all_masks = masks + [mask ^ 1 for mask in masks]
    query_norm, biases = pl.pallas_call(
        functools.partial(query_kernel, width * splits, all_masks),
        out_shape=[
            jax.ShapeDtypeStruct((2 * rows, width), jnp.bfloat16),
            jax.ShapeDtypeStruct((16, len(all_masks) * HD), jnp.float32),
        ],
        in_specs=[VMEM] * 5,
        out_specs=[VMEM] * 2,
        compiler_params=params,
    )(query_gain, sums, others, *queries)

    pack = pl.pallas_call(
        functools.partial(
            pack_kernel, width * splits, near if splits == 2 else len(masks), len(masks)
        ),
        out_shape=jax.ShapeDtypeStruct((2 * len(masks) * rows, width), jnp.bfloat16),
        in_specs=[VMEM] * (4 + 2 * len(masks)),
        out_specs=VMEM,
        compiler_params=params,
    )(
        key_gain,
        sums,
        others,
        crossed,
        *[keys[mask] for mask in masks],
        *[values[mask] for mask in masks],
    )
    other_pack = exchange(pack, 1)

    state = pl.pallas_call(
        own_attention,
        out_shape=[
            jax.ShapeDtypeStruct((2 * rows, width), jnp.float32),
            jax.ShapeDtypeStruct((2 * rows, 2 * width), jnp.float32),
        ],
        in_specs=[VMEM] * 3,
        out_specs=[VMEM] * 2,
        compiler_params=params,
    )(query_norm, biases, pack)

    def last(place, out_shape):
        return pl.pallas_call(
            functools.partial(last_attention, place),
            out_shape=out_shape,
            in_specs=[VMEM] * 5,
            out_specs=[VMEM] * len(out_shape),
            compiler_params=params,
        )(query_norm, biases, other_pack, *state)

    (packet,) = last(1, [jax.ShapeDtypeStruct((rows + EXTRA, width), jnp.bfloat16)])
    own, own_lines = last(
        0,
        [
            jax.ShapeDtypeStruct((rows, width), jnp.float32),
            jax.ShapeDtypeStruct((16, width), jnp.float32),
        ],
    )
    gates = pl.pallas_call(
        gate_kernel,
        out_shape=jax.ShapeDtypeStruct((16, width), jnp.float32),
        in_specs=[SMEM, VMEM],
        out_specs=VMEM,
        compiler_params=params,
    )(frame_step, gate_table)
    packet = exchange(packet, query_mask)

    return pl.pallas_call(
        merge_kernel,
        out_shape=jax.ShapeDtypeStruct((rows, width), jnp.bfloat16),
        in_specs=[VMEM] * 4,
        out_specs=VMEM,
        compiler_params=params,
    )(own, own_lines, packet, gates)


def solution(mesh):
    return jax.shard_map(
        local,
        mesh=mesh,
        in_specs=(
            P("tm", "head"),
            P("tm", "head"),
            P("tm", "head"),
            P("head"),
            P("head"),
            P(None, "head"),
            P(),
            P("tm", None),
        ),
        out_specs=P("tm", "head"),
        check_vma=False,
    )
```

```python
import functools

import jax
import jax.numpy as jnp
from jax import lax
from jax.experimental import pallas as pl
from jax.experimental.pallas import tpu as pltpu
from jax.sharding import PartitionSpec as P

HD = 128
BLK = 64
FRAME_TOK = 1560
EPSILON = 1e-06
LOG2E = 1.4426950408889634
SCALE = HD ** (-0.5) * LOG2E
MASKED = -1e30
EXTRA = 16
ANY = pl.BlockSpec(memory_space=pl.ANY)
VMEM = pl.BlockSpec(memory_space=pltpu.VMEM)
SMEM = pl.BlockSpec(memory_space=pltpu.SMEM)


def spread(row):
    return jnp.broadcast_to(row, (row.shape[1], row.shape[1])).T


def squares(source_ref):
    wide = source_ref[:HD, :].astype(jnp.float32)
    square = wide * wide
    part = square[:, :HD]
    for low in range(HD, square.shape[1], HD):
        part = part + square[:, low : low + HD]
    return jnp.sum(part.T, axis=0, keepdims=True)


def own_kernel(
    query_hbm,
    key_hbm,
    value_hbm,
    far_hbm,
    query_out,
    key_out,
    value_out,
    sums_out,
    query_ref,
    far_ref,
    sems,
):
    rows, width = query_ref.shape
    copies = [
        pltpu.make_async_copy(query_hbm, query_ref, sems.at[0]),
        pltpu.make_async_copy(key_hbm, key_out, sems.at[1]),
        pltpu.make_async_copy(far_hbm, far_ref, sems.at[2]),
        pltpu.make_async_copy(value_hbm, value_out, sems.at[3]),
    ]
    for copy in copies:
        copy.start()
    query_out[rows:, HD:] = jnp.zeros((EXTRA, width - HD), jnp.bfloat16)
    sums_out[...] = jnp.zeros_like(sums_out)
    copies[0].wait()
    query_out[:rows, :] = query_ref[...]
    sums_out[0:1, :] = squares(query_ref)
    copies[1].wait()
    sums_out[1:2, :] = squares(key_out)
    copies[2].wait()
    far = far_ref[...].astype(jnp.float32)
    far = jnp.concatenate([far, jnp.full((1, HD - far.shape[1]), -1.0)], axis=1)
    query_out[rows:, :HD] = jnp.broadcast_to(far, (EXTRA, HD)).astype(jnp.bfloat16)
    copies[3].wait()


def sums_kernel(lines, before_ref, *refs):
    *sources, out_ref = refs
    out_ref[...] = before_ref[...]
    for line, source_ref in zip(lines, sources):
        out_ref[line : line + 1, :] = squares(source_ref)


def factor_of(line, full_width):
    return spread(lax.rsqrt(line / full_width + EPSILON))


def normed(source_ref, factor, gain_ref):
    parts = []
    for low in range(0, source_ref.shape[1], HD):
        wide = source_ref[:HD, low : low + HD].astype(jnp.float32)
        parts.append((wide * factor * gain_ref[:, low : low + HD]).astype(jnp.bfloat16))
    return jnp.concatenate(parts, axis=1)


def query_kernel(full_width, key_masks, gain_ref, own_ref, other_ref, *refs):
    queries, (query_out, bias_out) = refs[:2], refs[2:]
    me = lax.axis_index("tm")
    count = lax.axis_size("tm")
    query_mask = count // 2 + count // 4
    lane = lax.broadcasted_iota(jnp.int32, (1, HD), 1)
    half = (lane >= BLK).astype(jnp.float32)
    for place, query_ref in enumerate(queries):
        line = 2 * place
        total = own_ref[line : line + 1, :] + other_ref[line : line + 1, :]
        query_out[place * HD : (place + 1) * HD, :] = normed(
            query_ref, factor_of(total, full_width), gain_ref
        )
        far = query_ref[HD:, :HD].astype(jnp.float32)[:1]
        query_id = me ^ (place * query_mask)
        for block, key_mask in enumerate(key_masks):
            key_id = me ^ key_mask
            choice = jnp.sum(jnp.where(lane == key_id, far, 0.0), axis=1, keepdims=True)
            taken = (choice == half) | (jnp.abs(query_id - key_id) <= 1)
            bias_out[8 * place : 8 * place + 8, block * HD : (block + 1) * HD] = (
                jnp.broadcast_to(jnp.where(taken, 0.0, MASKED), (8, HD))
            )


def pack_kernel(full_width, near, held, gain_ref, own_ref, other_ref, cross_ref, *refs):
    keys, values, pack_out = refs[:held], refs[held : 2 * held], refs[2 * held]
    for place, key_ref in enumerate(keys):
        line = 1 + place + (place > 0)
        if place < near:
            total = own_ref[line : line + 1, :] + other_ref[line : line + 1, :]
        else:
            total = squares(key_ref) + cross_ref[3:4, :]
        pack_out[place * HD : (place + 1) * HD, :] = normed(
            key_ref, factor_of(total, full_width), gain_ref
        )
    for place, value_ref in enumerate(values, start=held):
        pack_out[place * HD : (place + 1) * HD, :] = value_ref[...]


def absorb(query, pack_ref, biases, olds, low):
    high, half = low + HD, pack_ref.shape[0] // 2
    scores = lax.dot_general(
        query,
        pack_ref[:half, low:high],
        (((1,), (1,)), ((), ())),
        preferred_element_type=jnp.float32,
    )
    tops, totals, rounded = [], [], []
    for place, bias in enumerate(biases):
        logits = scores[place * HD : (place + 1) * HD] * SCALE + bias
        top = jnp.broadcast_to(jnp.max(logits, axis=1, keepdims=True), (HD, HD))
        if olds is not None:
            top = jnp.maximum(top, olds[place][0])
        weights = [
            jnp.exp2(logits[:, left : left + HD] - top)
            for left in range(0, logits.shape[1], HD)
        ]
        total = jnp.sum(functools.reduce(jnp.add, weights), axis=1, keepdims=True)
        tops.append(top)
        totals.append(jnp.broadcast_to(total, (HD, HD)))
        rounded.append(
            jnp.concatenate([weight.astype(jnp.bfloat16) for weight in weights], axis=1)
        )
    added = jnp.dot(
        jnp.concatenate(rounded, axis=0),
        pack_ref[half:, low:high],
        preferred_element_type=jnp.float32,
    )
    results = []
    for place in range(len(biases)):
        context = added[place * HD : (place + 1) * HD]
        total = totals[place]
        if olds is not None:
            fade = jnp.exp2(olds[place][0] - tops[place])
            total = total + olds[place][1] * fade
            context = context + olds[place][2] * fade
        results.append((tops[place], total, context))
    return results


def own_attention(query_ref, bias_ref, pack_ref, context_out, stats_out):
    keys = pack_ref.shape[0] // 2
    biases = [bias_ref[8 * place : 8 * place + 1, :keys] for place in range(2)]
    for low in range(0, query_ref.shape[1], HD):
        results = absorb(query_ref[:, low : low + HD], pack_ref, biases, None, low)
        for place, (top, total, context) in enumerate(results):
            part, wide = slice(place * HD, (place + 1) * HD), 2 * low
            context_out[part, low : low + HD] = context
            stats_out[part, wide : wide + HD] = top
            stats_out[part, wide + HD : wide + 2 * HD] = total


def last_attention(place, query_ref, bias_ref, pack_ref, context_ref, stats_ref, *outs):
    width, keys = query_ref.shape[1], pack_ref.shape[0] // 2
    part = slice(place * HD, (place + 1) * HD)
    bias = bias_ref[8 * place : 8 * place + 1, keys:]
    lane = lax.broadcasted_iota(jnp.int32, (1, HD), 1)
    columns = jnp.zeros((HD, HD), jnp.float32)
    for low in range(0, width, HD):
        wide = 2 * low
        old = (
            stats_ref[part, wide : wide + HD],
            stats_ref[part, wide + HD : wide + 2 * HD],
            context_ref[part, low : low + HD],
        )
        ((top, total, context),) = absorb(
            query_ref[part, low : low + HD], pack_ref, [bias], [old], low
        )
        outs[0][:HD, low : low + HD] = context.astype(outs[0].dtype)
        line = wide // HD
        columns = jnp.where(lane == line, top, jnp.where(lane == line + 1, total, columns))
    lines = columns.T
    sub = lax.broadcasted_iota(jnp.int32, (EXTRA, HD), 0)
    for low in range(0, width, HD):
        line = 2 * low // HD
        pair = (lines[line : line + 1, :], lines[line + 1 : line + 2, :])
        if place == 0:
            for row, value in enumerate(pair):
                outs[1][8 * row : 8 * row + 8, low : low + HD] = jnp.broadcast_to(value, (8, HD))
        else:
            piece_rows = jnp.zeros((EXTRA, HD), jnp.float32)
            for row, value in enumerate(pair):
                first = value.astype(jnp.bfloat16).astype(jnp.float32)
                second = (value - first).astype(jnp.bfloat16).astype(jnp.float32)
                for piece, part_value in enumerate((first, second, value - first - second)):
                    piece_rows = jnp.where(sub == 3 * row + piece, part_value, piece_rows)
            outs[0][HD:, low : low + HD] = piece_rows.astype(jnp.bfloat16)


def gate_kernel(step_ref, table_ref, out_ref):
    rows = out_ref.shape[0] // 2
    start = lax.axis_index("tm") * HD
    first = step_ref[start // FRAME_TOK]
    last = step_ref[(start + HD - 1) // FRAME_TOK]
    out_ref[:rows, :] = jnp.broadcast_to(table_ref[pl.ds(first, 1), :], (rows, out_ref.shape[1]))
    out_ref[rows:, :] = jnp.broadcast_to(table_ref[pl.ds(last, 1), :], (rows, out_ref.shape[1]))


def merge_kernel(own_ref, lines_ref, packet_ref, gate_ref, out_ref):
    rows, width = own_ref.shape
    pieces = packet_ref[rows:, :].astype(jnp.float32)
    own_top, own_total = lines_ref[0:1, :], lines_ref[8:9, :]
    other_top = pieces[0:1] + pieces[1:2] + pieces[2:3]
    other_total = pieces[3:4] + pieces[4:5] + pieces[5:6]
    top = jnp.maximum(own_top, other_top)
    own_share, other_share = jnp.exp2(own_top - top), jnp.exp2(other_top - top)
    scale = 1.0 / (own_total * own_share + other_total * other_share)
    own_share, other_share = own_share * scale, other_share * scale
    start = lax.axis_index("tm") * rows
    first_rows = (start // FRAME_TOK + 1) * FRAME_TOK - start
    row_ids = lax.broadcasted_iota(jnp.int32, (rows, 1), 0)
    for low in range(0, width, HD):
        high = low + HD
        context = own_ref[:, low:high] * spread(own_share[:, low:high])
        other = packet_ref[:rows, low:high].astype(jnp.float32)
        context += other * spread(other_share[:, low:high])
        gate = jnp.where(
            row_ids < first_rows, gate_ref[0:1, low:high], gate_ref[8:9, low:high]
        )
        out_ref[:, low:high] = (context * gate).astype(jnp.bfloat16)


def exchange(array, mask):
    count = lax.axis_size("tm")
    return lax.ppermute(array, "tm", [(i, i ^ mask) for i in range(count)])


def gathered(array, bits):
    held = {0: array}
    for bit in bits:
        for mask in list(held):
            held[mask ^ bit] = exchange(held[mask], bit)
    return held


def local(
    query_proj, key_proj, value_proj, query_gain, key_gain, gate_table, frame_step, far_blocks
):
    rows, width = query_proj.shape
    count = lax.axis_size("tm")
    splits = lax.axis_size("head")
    full_width = width * splits
    params = pltpu.CompilerParams(vmem_limit_bytes=(8 + count // 2) * 2**20)
    query_mask = count // 2 + count // 4
    bits = [1 << place for place in range(1, count.bit_length() - 2)][::-1]
    query_gain = query_gain.reshape(1, width)
    key_gain = key_gain.reshape(1, width)

    lines = 2 + 2 ** len(bits)
    lines += -lines % 8
    query_packet, own_key, own_value, own_sums = pl.pallas_call(
        own_kernel,
        out_shape=[
            jax.ShapeDtypeStruct((rows + EXTRA, width), jnp.bfloat16),
            jax.ShapeDtypeStruct((rows, width), jnp.bfloat16),
            jax.ShapeDtypeStruct((rows, width), jnp.bfloat16),
            jax.ShapeDtypeStruct((lines, rows), jnp.float32),
        ],
        in_specs=[ANY] * 4,
        out_specs=[VMEM] * 4,
        scratch_shapes=[
            pltpu.VMEM((rows, width), jnp.bfloat16),
            pltpu.VMEM(far_blocks.shape, jnp.int32),
            pltpu.SemaphoreType.DMA((4,)),
        ],
    )(query_proj, key_proj, value_proj, far_blocks)
    keys = gathered(key_proj, bits)
    keys[0] = own_key
    values = gathered(own_value, bits[::-1])
    queries = [query_packet, exchange(query_packet, query_mask)]
    masks = sorted(keys, key=lambda mask: (mask.bit_count(), -mask))
    near = 1 + len(bits)

    def summed(sums, sources, held):
        return pl.pallas_call(
            functools.partial(sums_kernel, held),
            out_shape=jax.ShapeDtypeStruct(own_sums.shape, jnp.float32),
            in_specs=[VMEM] * (1 + len(sources)),
            out_specs=VMEM,
            compiler_params=params,
        )(sums, *sources)

    sources = [queries[1]] + [keys[mask] for mask in masks[1:near]]
    sums = summed(own_sums, sources, range(2, near + 2))
    if splits == 2:
        others = lax.ppermute(sums, "head", [(0, 1), (1, 0)])
        pairs = []
        for i in range(2 * count):
            pairs.append((i, ((i // 2) ^ bits[1]) * 2 + (i % 2 ^ 1)))
        crossed = lax.ppermute(sums, ("tm", "head"), pairs)
    else:
        sources = [keys[mask] for mask in masks[near:]]
        sums = summed(sums, sources, range(near + 2, len(masks) + 2))
        sums = lax.psum(sums, "head")
        others = crossed = jnp.zeros_like(sums)

    all_masks = masks + [mask ^ 1 for mask in masks]
    query_norm, biases = pl.pallas_call(
        functools.partial(query_kernel, width * splits, all_masks),
        out_shape=[
            jax.ShapeDtypeStruct((2 * rows, width), jnp.bfloat16),
            jax.ShapeDtypeStruct((16, len(all_masks) * HD), jnp.float32),
        ],
        in_specs=[VMEM] * 5,
        out_specs=[VMEM] * 2,
        compiler_params=params,
    )(query_gain, sums, others, *queries)

    pack = pl.pallas_call(
        functools.partial(
            pack_kernel, width * splits, near if splits == 2 else len(masks), len(masks)
        ),
        out_shape=jax.ShapeDtypeStruct((2 * len(masks) * rows, width), jnp.bfloat16),
        in_specs=[VMEM] * (4 + 2 * len(masks)),
        out_specs=VMEM,
        compiler_params=params,
    )(
        key_gain,
        sums,
        others,
        crossed,
        *[keys[mask] for mask in masks],
        *[values[mask] for mask in masks],
    )
    other_pack = exchange(pack, 1)

    state = pl.pallas_call(
        own_attention,
        out_shape=[
            jax.ShapeDtypeStruct((2 * rows, width), jnp.float32),
            jax.ShapeDtypeStruct((2 * rows, 2 * width), jnp.float32),
        ],
        in_specs=[VMEM] * 3,
        out_specs=[VMEM] * 2,
        compiler_params=params,
    )(query_norm, biases, pack)

    def last(place, out_shape):
        return pl.pallas_call(
            functools.partial(last_attention, place),
            out_shape=out_shape,
            in_specs=[VMEM] * 5,
            out_specs=[VMEM] * len(out_shape),
            compiler_params=params,
        )(query_norm, biases, other_pack, *state)

    (packet,) = last(1, [jax.ShapeDtypeStruct((rows + EXTRA, width), jnp.bfloat16)])
    own, own_lines = last(
        0,
        [
            jax.ShapeDtypeStruct((rows, width), jnp.float32),
            jax.ShapeDtypeStruct((16, width), jnp.float32),
        ],
    )
    gates = pl.pallas_call(
        gate_kernel,
        out_shape=jax.ShapeDtypeStruct((16, width), jnp.float32),
        in_specs=[SMEM, VMEM],
        out_specs=VMEM,
        compiler_params=params,
    )(frame_step, gate_table)
    packet = exchange(packet, query_mask)

    return pl.pallas_call(
        merge_kernel,
        out_shape=jax.ShapeDtypeStruct((rows, width), jnp.bfloat16),
        in_specs=[VMEM] * 4,
        out_specs=VMEM,
        compiler_params=params,
    )(own, own_lines, packet, gates)


def solution(mesh):
    return jax.shard_map(
        local,
        mesh=mesh,
        in_specs=(
            P("tm", "head"),
            P("tm", "head"),
            P("tm", "head"),
            P("head"),
            P("head"),
            P(None, "head"),
            P(),
            P("tm", None),
        ),
        out_specs=P("tm", "head"),
        check_vma=False,
    )
```

```python
import functools

import jax
import jax.numpy as jnp
from jax import lax
from jax.experimental import pallas as pl
from jax.experimental.pallas import tpu as pltpu
from jax.sharding import PartitionSpec as P

HD = 128
BLK = 64
FRAME_TOK = 1560
EPSILON = 1e-06
LOG2E = 1.4426950408889634
SCALE = HD ** (-0.5) * LOG2E
MASKED = -1e30
EXTRA = 16
ANY = pl.BlockSpec(memory_space=pl.ANY)
VMEM = pl.BlockSpec(memory_space=pltpu.VMEM)
SMEM = pl.BlockSpec(memory_space=pltpu.SMEM)


def spread(row):
    return jnp.broadcast_to(row, (row.shape[1], row.shape[1])).T


def squares(source_ref):
    wide = source_ref[:HD, :].astype(jnp.float32)
    square = wide * wide
    part = square[:, :HD]
    for low in range(HD, square.shape[1], HD):
        part = part + square[:, low : low + HD]
    return jnp.sum(part.T, axis=0, keepdims=True)


def own_kernel(
    query_hbm, key_hbm, value_hbm, far_hbm, query_out, pair_out, sums_out, query_ref, far_ref, sems
):
    rows, width = query_ref.shape
    copies = [
        pltpu.make_async_copy(key_hbm, pair_out.at[:rows, :], sems.at[0]),
        pltpu.make_async_copy(value_hbm, pair_out.at[rows:, :], sems.at[1]),
        pltpu.make_async_copy(query_hbm, query_ref, sems.at[2]),
        pltpu.make_async_copy(far_hbm, far_ref, sems.at[3]),
    ]
    for copy in copies:
        copy.start()
    query_out[rows:, HD:] = jnp.zeros((EXTRA, width - HD), jnp.bfloat16)
    sums_out[...] = jnp.zeros_like(sums_out)
    copies[0].wait()
    sums_out[1:2, :] = squares(pair_out)
    copies[2].wait()
    query_out[:rows, :] = query_ref[...]
    sums_out[0:1, :] = squares(query_ref)
    copies[3].wait()
    far = far_ref[...].astype(jnp.float32)
    far = jnp.concatenate([far, jnp.full((1, HD - far.shape[1]), -1.0)], axis=1)
    query_out[rows:, :HD] = jnp.broadcast_to(far, (EXTRA, HD)).astype(jnp.bfloat16)
    copies[1].wait()


def sums_kernel(lines, before_ref, *refs):
    *sources, out_ref = refs
    out_ref[...] = before_ref[...]
    for line, source_ref in zip(lines, sources):
        out_ref[line : line + 1, :] = squares(source_ref)


def factor_of(line, full_width):
    return spread(lax.rsqrt(line / full_width + EPSILON))


def normed(source_ref, factor, gain_ref):
    parts = []
    for low in range(0, source_ref.shape[1], HD):
        wide = source_ref[:HD, low : low + HD].astype(jnp.float32)
        parts.append((wide * factor * gain_ref[:, low : low + HD]).astype(jnp.bfloat16))
    return jnp.concatenate(parts, axis=1)


def query_kernel(full_width, key_masks, gain_ref, own_ref, other_ref, *refs):
    queries, (query_out, bias_out) = refs[:2], refs[2:]
    me = lax.axis_index("tm")
    count = lax.axis_size("tm")
    query_mask = count // 2 + count // 4
    lane = lax.broadcasted_iota(jnp.int32, (1, HD), 1)
    half = (lane >= BLK).astype(jnp.float32)
    for place, query_ref in enumerate(queries):
        line = 2 * place
        total = own_ref[line : line + 1, :] + other_ref[line : line + 1, :]
        query_out[place * HD : (place + 1) * HD, :] = normed(
            query_ref, factor_of(total, full_width), gain_ref
        )
        far = query_ref[HD:, :HD].astype(jnp.float32)[:1]
        query_id = me ^ (place * query_mask)
        for block, key_mask in enumerate(key_masks):
            key_id = me ^ key_mask
            choice = jnp.sum(jnp.where(lane == key_id, far, 0.0), axis=1, keepdims=True)
            taken = (choice == half) | (jnp.abs(query_id - key_id) <= 1)
            bias_out[8 * place : 8 * place + 8, block * HD : (block + 1) * HD] = (
                jnp.broadcast_to(jnp.where(taken, 0.0, MASKED), (8, HD))
            )


def pack_kernel(full_width, near, gain_ref, own_ref, other_ref, cross_ref, *refs):
    *pairs, pack_out = refs
    held = len(pairs)
    for place, pair_ref in enumerate(pairs):
        line = 1 + place + (place > 0)
        if place < near:
            total = own_ref[line : line + 1, :] + other_ref[line : line + 1, :]
        else:
            total = squares(pair_ref) + cross_ref[3:4, :]
        pack_out[place * HD : (place + 1) * HD, :] = normed(
            pair_ref, factor_of(total, full_width), gain_ref
        )
        pack_out[(held + place) * HD : (held + place + 1) * HD, :] = pair_ref[HD:, :]


def absorb(query, pack_ref, biases, olds, low):
    high, half = low + HD, pack_ref.shape[0] // 2
    scores = lax.dot_general(
        query,
        pack_ref[:half, low:high],
        (((1,), (1,)), ((), ())),
        preferred_element_type=jnp.float32,
    )
    tops, totals, rounded = [], [], []
    for place, bias in enumerate(biases):
        logits = scores[place * HD : (place + 1) * HD] * SCALE + bias
        top = jnp.broadcast_to(jnp.max(logits, axis=1, keepdims=True), (HD, HD))
        if olds is not None:
            top = jnp.maximum(top, olds[place][0])
        weights = [
            jnp.exp2(logits[:, left : left + HD] - top)
            for left in range(0, logits.shape[1], HD)
        ]
        total = jnp.sum(functools.reduce(jnp.add, weights), axis=1, keepdims=True)
        tops.append(top)
        totals.append(jnp.broadcast_to(total, (HD, HD)))
        rounded.append(
            jnp.concatenate([weight.astype(jnp.bfloat16) for weight in weights], axis=1)
        )
    added = jnp.dot(
        jnp.concatenate(rounded, axis=0),
        pack_ref[half:, low:high],
        preferred_element_type=jnp.float32,
    )
    results = []
    for place in range(len(biases)):
        context = added[place * HD : (place + 1) * HD]
        total = totals[place]
        if olds is not None:
            fade = jnp.exp2(olds[place][0] - tops[place])
            total = total + olds[place][1] * fade
            context = context + olds[place][2] * fade
        results.append((tops[place], total, context))
    return results


def own_attention(query_ref, bias_ref, pack_ref, context_out, stats_out):
    keys = pack_ref.shape[0] // 2
    biases = [bias_ref[8 * place : 8 * place + 1, :keys] for place in range(2)]
    for low in range(0, query_ref.shape[1], HD):
        results = absorb(query_ref[:, low : low + HD], pack_ref, biases, None, low)
        for place, (top, total, context) in enumerate(results):
            part, wide = slice(place * HD, (place + 1) * HD), 2 * low
            context_out[part, low : low + HD] = context
            stats_out[part, wide : wide + HD] = top
            stats_out[part, wide + HD : wide + 2 * HD] = total


def last_attention(place, query_ref, bias_ref, pack_ref, context_ref, stats_ref, *outs):
    width, keys = query_ref.shape[1], pack_ref.shape[0] // 2
    part = slice(place * HD, (place + 1) * HD)
    bias = bias_ref[8 * place : 8 * place + 1, keys:]
    lane = lax.broadcasted_iota(jnp.int32, (1, HD), 1)
    columns = jnp.zeros((HD, HD), jnp.float32)
    for low in range(0, width, HD):
        wide = 2 * low
        old = (
            stats_ref[part, wide : wide + HD],
            stats_ref[part, wide + HD : wide + 2 * HD],
            context_ref[part, low : low + HD],
        )
        ((top, total, context),) = absorb(
            query_ref[part, low : low + HD], pack_ref, [bias], [old], low
        )
        outs[0][:HD, low : low + HD] = context.astype(outs[0].dtype)
        line = wide // HD
        columns = jnp.where(lane == line, top, jnp.where(lane == line + 1, total, columns))
    lines = columns.T
    sub = lax.broadcasted_iota(jnp.int32, (EXTRA, HD), 0)
    for low in range(0, width, HD):
        line = 2 * low // HD
        pair = (lines[line : line + 1, :], lines[line + 1 : line + 2, :])
        if place == 0:
            for row, value in enumerate(pair):
                outs[1][8 * row : 8 * row + 8, low : low + HD] = jnp.broadcast_to(value, (8, HD))
        else:
            piece_rows = jnp.zeros((EXTRA, HD), jnp.float32)
            for row, value in enumerate(pair):
                first = value.astype(jnp.bfloat16).astype(jnp.float32)
                second = (value - first).astype(jnp.bfloat16).astype(jnp.float32)
                for piece, part_value in enumerate((first, second, value - first - second)):
                    piece_rows = jnp.where(sub == 3 * row + piece, part_value, piece_rows)
            outs[0][HD:, low : low + HD] = piece_rows.astype(jnp.bfloat16)


def gate_kernel(step_ref, table_ref, out_ref):
    rows = out_ref.shape[0] // 2
    start = lax.axis_index("tm") * HD
    first = step_ref[start // FRAME_TOK]
    last = step_ref[(start + HD - 1) // FRAME_TOK]
    out_ref[:rows, :] = jnp.broadcast_to(table_ref[pl.ds(first, 1), :], (rows, out_ref.shape[1]))
    out_ref[rows:, :] = jnp.broadcast_to(table_ref[pl.ds(last, 1), :], (rows, out_ref.shape[1]))


def merge_kernel(own_ref, lines_ref, packet_ref, gate_ref, out_ref):
    rows, width = own_ref.shape
    pieces = packet_ref[rows:, :].astype(jnp.float32)
    own_top, own_total = lines_ref[0:1, :], lines_ref[8:9, :]
    other_top = pieces[0:1] + pieces[1:2] + pieces[2:3]
    other_total = pieces[3:4] + pieces[4:5] + pieces[5:6]
    top = jnp.maximum(own_top, other_top)
    own_share, other_share = jnp.exp2(own_top - top), jnp.exp2(other_top - top)
    scale = 1.0 / (own_total * own_share + other_total * other_share)
    own_share, other_share = own_share * scale, other_share * scale
    start = lax.axis_index("tm") * rows
    first_rows = (start // FRAME_TOK + 1) * FRAME_TOK - start
    row_ids = lax.broadcasted_iota(jnp.int32, (rows, 1), 0)
    for low in range(0, width, HD):
        high = low + HD
        context = own_ref[:, low:high] * spread(own_share[:, low:high])
        other = packet_ref[:rows, low:high].astype(jnp.float32)
        context += other * spread(other_share[:, low:high])
        gate = jnp.where(
            row_ids < first_rows, gate_ref[0:1, low:high], gate_ref[8:9, low:high]
        )
        out_ref[:, low:high] = (context * gate).astype(jnp.bfloat16)


def exchange(array, mask):
    count = lax.axis_size("tm")
    return lax.ppermute(array, "tm", [(i, i ^ mask) for i in range(count)])


def gathered(array, bits):
    held = {0: array}
    for bit in bits:
        for mask in list(held):
            held[mask ^ bit] = exchange(held[mask], bit)
    return held


def cost(flops):
    return pl.CostEstimate(flops=flops, bytes_accessed=0, transcendentals=0)


def local(
    query_proj, key_proj, value_proj, query_gain, key_gain, gate_table, frame_step, far_blocks
):
    rows, width = query_proj.shape
    count = lax.axis_size("tm")
    splits = lax.axis_size("head")
    full_width = width * splits
    params = pltpu.CompilerParams(vmem_limit_bytes=(8 + count // 2) * 2**20)
    query_mask = count // 2 + count // 4
    bits = [1 << place for place in range(1, count.bit_length() - 2)][::-1]
    query_gain = query_gain.reshape(1, width)
    key_gain = key_gain.reshape(1, width)

    lines = 2 + 2 ** len(bits)
    lines += -lines % 8
    query_packet, own_pair, own_sums = pl.pallas_call(
        own_kernel,
        out_shape=[
            jax.ShapeDtypeStruct((rows + EXTRA, width), jnp.bfloat16),
            jax.ShapeDtypeStruct((2 * rows, width), jnp.bfloat16),
            jax.ShapeDtypeStruct((lines, rows), jnp.float32),
        ],
        in_specs=[ANY] * 4,
        out_specs=[VMEM] * 3,
        scratch_shapes=[
            pltpu.VMEM((rows, width), jnp.bfloat16),
            pltpu.VMEM(far_blocks.shape, jnp.int32),
            pltpu.SemaphoreType.DMA((4,)),
        ],
    )(query_proj, key_proj, value_proj, far_blocks)
    blocks = gathered(own_pair, bits)
    queries = [query_packet, exchange(query_packet, query_mask)]
    masks = sorted(blocks, key=lambda mask: (mask.bit_count(), -mask))
    near = 1 + len(bits)

    def summed(sums, sources, held):
        return pl.pallas_call(
            functools.partial(sums_kernel, held),
            out_shape=jax.ShapeDtypeStruct(own_sums.shape, jnp.float32),
            in_specs=[VMEM] * (1 + len(sources)),
            out_specs=VMEM,
            compiler_params=params,
            cost_estimate=cost(4 * 10**9),
        )(sums, *sources)

    sources = [queries[1]] + [blocks[mask] for mask in masks[1:near]]
    sums = summed(own_sums, sources, range(2, near + 2))
    if splits == 2:
        others = lax.ppermute(sums, "head", [(0, 1), (1, 0)])
        pairs = []
        for i in range(2 * count):
            pairs.append((i, ((i // 2) ^ bits[1]) * 2 + (i % 2 ^ 1)))
        crossed = lax.ppermute(sums, ("tm", "head"), pairs)
    else:
        sources = [blocks[mask] for mask in masks[near:]]
        sums = summed(sums, sources, range(near + 2, len(masks) + 2))
        sums = lax.psum(sums, "head")
        others = crossed = jnp.zeros_like(sums)

    all_masks = masks + [mask ^ 1 for mask in masks]
    query_norm, biases = pl.pallas_call(
        functools.partial(query_kernel, width * splits, all_masks),
        out_shape=[
            jax.ShapeDtypeStruct((2 * rows, width), jnp.bfloat16),
            jax.ShapeDtypeStruct((16, len(all_masks) * HD), jnp.float32),
        ],
        in_specs=[VMEM] * 5,
        out_specs=[VMEM] * 2,
        compiler_params=params,
    )(query_gain, sums, others, *queries)

    pack = pl.pallas_call(
        functools.partial(pack_kernel, width * splits, near if splits == 2 else len(masks)),
        out_shape=jax.ShapeDtypeStruct((2 * len(masks) * rows, width), jnp.bfloat16),
        in_specs=[VMEM] * (4 + len(masks)),
        out_specs=VMEM,
        compiler_params=params,
    )(
        key_gain,
        sums,
        others,
        crossed,
        *[blocks[mask] for mask in masks],
    )
    other_pack = exchange(pack, 1)

    state = pl.pallas_call(
        own_attention,
        out_shape=[
            jax.ShapeDtypeStruct((2 * rows, width), jnp.float32),
            jax.ShapeDtypeStruct((2 * rows, 2 * width), jnp.float32),
        ],
        in_specs=[VMEM] * 3,
        out_specs=[VMEM] * 2,
        compiler_params=params,
    )(query_norm, biases, pack)

    def last(place, out_shape):
        return pl.pallas_call(
            functools.partial(last_attention, place),
            out_shape=out_shape,
            in_specs=[VMEM] * 5,
            out_specs=[VMEM] * len(out_shape),
            compiler_params=params,
        )(query_norm, biases, other_pack, *state)

    (packet,) = last(1, [jax.ShapeDtypeStruct((rows + EXTRA, width), jnp.bfloat16)])
    own, own_lines = last(
        0,
        [
            jax.ShapeDtypeStruct((rows, width), jnp.float32),
            jax.ShapeDtypeStruct((16, width), jnp.float32),
        ],
    )
    gates = pl.pallas_call(
        gate_kernel,
        out_shape=jax.ShapeDtypeStruct((16, width), jnp.float32),
        in_specs=[SMEM, VMEM],
        out_specs=VMEM,
        compiler_params=params,
    )(frame_step, gate_table)
    packet = exchange(packet, query_mask)

    return pl.pallas_call(
        merge_kernel,
        out_shape=jax.ShapeDtypeStruct((rows, width), jnp.bfloat16),
        in_specs=[VMEM] * 4,
        out_specs=VMEM,
        compiler_params=params,
    )(own, own_lines, packet, gates)


def solution(mesh):
    return jax.shard_map(
        local,
        mesh=mesh,
        in_specs=(
            P("tm", "head"),
            P("tm", "head"),
            P("tm", "head"),
            P("head"),
            P("head"),
            P(None, "head"),
            P(),
            P("tm", None),
        ),
        out_specs=P("tm", "head"),
        check_vma=False,
    )
```

```python
import functools

import jax
import jax.numpy as jnp
from jax import lax
from jax.experimental import pallas as pl
from jax.experimental.pallas import tpu as pltpu
from jax.sharding import PartitionSpec as P

HD = 128
BLK = 64
FRAME_TOK = 1560
EPSILON = 1e-06
LOG2E = 1.4426950408889634
SCALE = HD ** (-0.5) * LOG2E
MASKED = -1e30
EXTRA = 16
AHEAD = 4 * 10**9
ANY = pl.BlockSpec(memory_space=pl.ANY)
VMEM = pl.BlockSpec(memory_space=pltpu.VMEM)
SMEM = pl.BlockSpec(memory_space=pltpu.SMEM)


def spread(row):
    return jnp.broadcast_to(row, (row.shape[1], row.shape[1])).T


def squares(source_ref):
    wide = source_ref[:HD, :].astype(jnp.float32)
    square = wide * wide
    part = square[:, :HD]
    for low in range(HD, square.shape[1], HD):
        part = part + square[:, low : low + HD]
    return jnp.sum(part.T, axis=0, keepdims=True)


def own_kernel(
    query_hbm, key_hbm, value_hbm, far_hbm, query_out, pair_out, sums_out, query_ref, far_ref, sems
):
    rows, width = query_ref.shape
    copies = [
        pltpu.make_async_copy(key_hbm, pair_out.at[:rows, :], sems.at[0]),
        pltpu.make_async_copy(value_hbm, pair_out.at[rows:, :], sems.at[1]),
        pltpu.make_async_copy(query_hbm, query_ref, sems.at[2]),
        pltpu.make_async_copy(far_hbm, far_ref, sems.at[3]),
    ]
    for copy in copies:
        copy.start()
    query_out[rows:, HD:] = jnp.zeros((EXTRA, width - HD), jnp.bfloat16)
    sums_out[...] = jnp.zeros_like(sums_out)
    copies[0].wait()
    sums_out[1:2, :] = squares(pair_out)
    copies[2].wait()
    query_out[:rows, :] = query_ref[...]
    sums_out[0:1, :] = squares(query_ref)
    copies[3].wait()
    far = far_ref[...].astype(jnp.float32)
    far = jnp.concatenate([far, jnp.full((1, HD - far.shape[1]), -1.0)], axis=1)
    query_out[rows:, :HD] = jnp.broadcast_to(far, (EXTRA, HD)).astype(jnp.bfloat16)
    copies[1].wait()


def sums_kernel(lines, before_ref, *refs):
    *sources, out_ref = refs
    out_ref[...] = before_ref[...]
    for line, source_ref in zip(lines, sources):
        out_ref[line : line + 1, :] = squares(source_ref)


def factor_of(line, full_width):
    return spread(lax.rsqrt(line / full_width + EPSILON))


def normed(source_ref, factor, gain_ref):
    parts = []
    for low in range(0, source_ref.shape[1], HD):
        wide = source_ref[:HD, low : low + HD].astype(jnp.float32)
        parts.append((wide * factor * gain_ref[:, low : low + HD]).astype(jnp.bfloat16))
    return jnp.concatenate(parts, axis=1)


def query_kernel(full_width, key_masks, gain_ref, own_ref, other_ref, *refs):
    queries, (query_out, bias_out) = refs[:2], refs[2:]
    me = lax.axis_index("tm")
    query_mask = lax.axis_size("tm") // 4
    lane = lax.broadcasted_iota(jnp.int32, (1, HD), 1)
    half = (lane >= BLK).astype(jnp.float32)
    for place, query_ref in enumerate(queries):
        line = 2 * place
        total = own_ref[line : line + 1, :] + other_ref[line : line + 1, :]
        query_out[place * HD : (place + 1) * HD, :] = normed(
            query_ref, factor_of(total, full_width), gain_ref
        )
        far = query_ref[HD:, :HD].astype(jnp.float32)[:1]
        query_id = me ^ (place * query_mask)
        for block, key_mask in enumerate(key_masks):
            key_id = me ^ key_mask
            choice = jnp.sum(jnp.where(lane == key_id, far, 0.0), axis=1, keepdims=True)
            taken = (choice == half) | (jnp.abs(query_id - key_id) <= 1)
            bias_out[8 * place : 8 * place + 8, block * HD : (block + 1) * HD] = (
                jnp.broadcast_to(jnp.where(taken, 0.0, MASKED), (8, HD))
            )


def early_kernel(full_width, gain_ref, own_ref, other_ref, key_ref, value_ref, *refs):
    *pairs, pack_out = refs
    held = 1 + len(pairs)
    sources = [(pairs[0], pairs[0]), (key_ref, value_ref)] + [(pair, pair) for pair in pairs[1:]]
    for place, (key, value) in enumerate(sources):
        line = 1 + place + (place > 0)
        total = own_ref[line : line + 1, :] + other_ref[line : line + 1, :]
        pack_out[place * HD : (place + 1) * HD, :] = normed(
            key, factor_of(total, full_width), gain_ref
        )
        low = 0 if value is value_ref else HD
        pack_out[(held + place) * HD : (held + place + 1) * HD, :] = value[low : low + HD, :]


def late_kernel(full_width, lines, gain_ref, own_ref, other_ref, cross_ref, *refs):
    *pairs, _, pack_out = refs
    held = len(pairs) // 2
    for place, (key, value) in enumerate(zip(pairs[:held], pairs[held:])):
        if lines is None:
            total = squares(key) + cross_ref[3:4, :]
        else:
            line = lines[place]
            total = own_ref[line : line + 1, :] + other_ref[line : line + 1, :]
        pack_out[place * HD : (place + 1) * HD, :] = normed(
            key, factor_of(total, full_width), gain_ref
        )
        pack_out[(held + place) * HD : (held + place + 1) * HD, :] = value[...]


def absorb(queries, pack_ref, biases, olds):
    half = pack_ref.shape[0] // 2
    heads, count = len(queries), len(biases)
    scores = []
    for head, query in enumerate(queries):
        scores.append(
            lax.dot_general(
                query,
                pack_ref[:half, head * HD : (head + 1) * HD],
                (((1,), (1,)), ((), ())),
                preferred_element_type=jnp.float32,
            )
        )
    spots = [(head, place) for head in range(heads) for place in range(count)]
    logits, tops, weights, totals = {}, {}, {}, {}
    for head, place in spots:
        part = scores[head][place * HD : (place + 1) * HD]
        logits[head, place] = part * SCALE + biases[place]
    for spot in spots:
        top = jnp.broadcast_to(jnp.max(logits[spot], axis=1, keepdims=True), (HD, HD))
        tops[spot] = top if olds is None else jnp.maximum(top, olds[spot][0])
    for spot in spots:
        weights[spot] = [
            jnp.exp2(logits[spot][:, left : left + HD] - tops[spot])
            for left in range(0, half, HD)
        ]
    added = []
    for head in range(heads):
        rounded = [
            jnp.concatenate([w.astype(jnp.bfloat16) for w in weights[head, place]], axis=1)
            for place in range(count)
        ]
        added.append(
            jnp.dot(
                jnp.concatenate(rounded, axis=0),
                pack_ref[half:, head * HD : (head + 1) * HD],
                preferred_element_type=jnp.float32,
            )
        )
    for spot in spots:
        total = jnp.sum(functools.reduce(jnp.add, weights[spot]), axis=1, keepdims=True)
        totals[spot] = jnp.broadcast_to(total, (HD, HD))
    results = {}
    for head, place in spots:
        spot = (head, place)
        context, total = added[head][place * HD : (place + 1) * HD], totals[spot]
        if olds is not None:
            fade = jnp.exp2(olds[spot][0] - tops[spot])
            total = total + olds[spot][1] * fade
            context = context + olds[spot][2] * fade
        results[spot] = (tops[spot], total, context)
    return results


def held_state(context_ref, stats_ref, head, place):
    part, low, wide = slice(place * HD, (place + 1) * HD), head * HD, 2 * head * HD
    return (
        stats_ref[part, wide : wide + HD],
        stats_ref[part, wide + HD : wide + 2 * HD],
        context_ref[part, low : low + HD],
    )


def step_kernel(first, query_ref, bias_ref, pack_ref, *refs):
    olds, (context_out, stats_out) = refs[:-2], refs[-2:]
    heads, keys = query_ref.shape[1] // HD, pack_ref.shape[0] // 2
    left = first * HD
    biases = [bias_ref[8 * place : 8 * place + 1, left : left + keys] for place in range(2)]
    state = None
    if olds:
        state = {
            (head, place): held_state(*olds, head, place)
            for head in range(heads)
            for place in range(2)
        }
    queries = [query_ref[:, head * HD : (head + 1) * HD] for head in range(heads)]
    for (head, place), result in absorb(queries, pack_ref, biases, state).items():
        part, low, wide = slice(place * HD, (place + 1) * HD), head * HD, 2 * head * HD
        top, total, context = result
        context_out[part, low : low + HD] = context
        stats_out[part, wide : wide + HD] = top
        stats_out[part, wide + HD : wide + 2 * HD] = total


def last_attention(place, query_ref, bias_ref, pack_ref, context_ref, stats_ref, *outs):
    heads, keys = query_ref.shape[1] // HD, pack_ref.shape[0] // 2
    part = slice(place * HD, (place + 1) * HD)
    bias = bias_ref[8 * place : 8 * place + 1, bias_ref.shape[1] - keys :]
    lane = lax.broadcasted_iota(jnp.int32, (1, HD), 1)
    state = {(h, 0): held_state(context_ref, stats_ref, h, place) for h in range(heads)}
    queries = [query_ref[part, head * HD : (head + 1) * HD] for head in range(heads)]
    results = absorb(queries, pack_ref, [bias], state)
    columns = jnp.zeros((HD, HD), jnp.float32)
    for head in range(heads):
        top, total, context = results[head, 0]
        outs[0][:HD, head * HD : (head + 1) * HD] = context.astype(outs[0].dtype)
        line = 2 * head
        columns = jnp.where(lane == line, top, jnp.where(lane == line + 1, total, columns))
    lines = columns.T
    sub = lax.broadcasted_iota(jnp.int32, (EXTRA, HD), 0)
    for head in range(heads):
        low = head * HD
        pair = (lines[2 * head : 2 * head + 1, :], lines[2 * head + 1 : 2 * head + 2, :])
        if place == 0:
            for row, value in enumerate(pair):
                outs[1][8 * row : 8 * row + 8, low : low + HD] = jnp.broadcast_to(value, (8, HD))
        else:
            piece_rows = jnp.zeros((EXTRA, HD), jnp.float32)
            for row, value in enumerate(pair):
                first = value.astype(jnp.bfloat16).astype(jnp.float32)
                second = (value - first).astype(jnp.bfloat16).astype(jnp.float32)
                for piece, part_value in enumerate((first, second, value - first - second)):
                    piece_rows = jnp.where(sub == 3 * row + piece, part_value, piece_rows)
            outs[0][HD:, low : low + HD] = piece_rows.astype(jnp.bfloat16)


def gate_kernel(step_ref, table_ref, out_ref):
    rows = out_ref.shape[0] // 2
    start = lax.axis_index("tm") * HD
    first = step_ref[start // FRAME_TOK]
    last = step_ref[(start + HD - 1) // FRAME_TOK]
    out_ref[:rows, :] = jnp.broadcast_to(table_ref[pl.ds(first, 1), :], (rows, out_ref.shape[1]))
    out_ref[rows:, :] = jnp.broadcast_to(table_ref[pl.ds(last, 1), :], (rows, out_ref.shape[1]))


def merge_kernel(own_ref, lines_ref, packet_ref, gate_ref, out_ref):
    rows, width = own_ref.shape
    pieces = packet_ref[rows:, :].astype(jnp.float32)
    own_top, own_total = lines_ref[0:1, :], lines_ref[8:9, :]
    other_top = pieces[0:1] + pieces[1:2] + pieces[2:3]
    other_total = pieces[3:4] + pieces[4:5] + pieces[5:6]
    top = jnp.maximum(own_top, other_top)
    own_share, other_share = jnp.exp2(own_top - top), jnp.exp2(other_top - top)
    scale = 1.0 / (own_total * own_share + other_total * other_share)
    own_share, other_share = own_share * scale, other_share * scale
    start = lax.axis_index("tm") * rows
    first_rows = (start // FRAME_TOK + 1) * FRAME_TOK - start
    row_ids = lax.broadcasted_iota(jnp.int32, (rows, 1), 0)
    for low in range(0, width, HD):
        high = low + HD
        context = own_ref[:, low:high] * spread(own_share[:, low:high])
        other = packet_ref[:rows, low:high].astype(jnp.float32)
        context += other * spread(other_share[:, low:high])
        gate = jnp.where(
            row_ids < first_rows, gate_ref[0:1, low:high], gate_ref[8:9, low:high]
        )
        out_ref[:, low:high] = (context * gate).astype(jnp.bfloat16)


def exchange(array, mask):
    count = lax.axis_size("tm")
    return lax.ppermute(array, "tm", [(i, i ^ mask) for i in range(count)])


def gathered(array, bits):
    held = {0: array}
    for bit in bits:
        for mask in list(held):
            held[mask ^ bit] = exchange(held[mask], bit)
    return held


def cost(flops):
    return pl.CostEstimate(flops=flops, bytes_accessed=0, transcendentals=0)


def local(
    query_proj, key_proj, value_proj, query_gain, key_gain, gate_table, frame_step, far_blocks
):
    rows, width = query_proj.shape
    count = lax.axis_size("tm")
    splits = lax.axis_size("head")
    full_width = width * splits
    params = pltpu.CompilerParams(vmem_limit_bytes=(8 + count // 2) * 2**20)
    query_mask = count // 4
    bits = [1 << place for place in range(1, count.bit_length() - 1)]
    bits = [bit for bit in bits[::-1] if bit != query_mask]
    query_gain = query_gain.reshape(1, width)
    key_gain = key_gain.reshape(1, width)

    lines = 2 + 2 ** len(bits)
    lines += -lines % 8
    query_packet, own_pair, own_sums = pl.pallas_call(
        own_kernel,
        out_shape=[
            jax.ShapeDtypeStruct((rows + EXTRA, width), jnp.bfloat16),
            jax.ShapeDtypeStruct((2 * rows, width), jnp.bfloat16),
            jax.ShapeDtypeStruct((lines, rows), jnp.float32),
        ],
        in_specs=[ANY] * 4,
        out_specs=[VMEM] * 3,
        scratch_shapes=[
            pltpu.VMEM((rows, width), jnp.bfloat16),
            pltpu.VMEM(far_blocks.shape, jnp.int32),
            pltpu.SemaphoreType.DMA((4,)),
        ],
    )(query_proj, key_proj, value_proj, far_blocks)
    far = bits[0]
    far_key, far_value = exchange(key_proj, far), exchange(value_proj, far)
    pairs = gathered(own_pair, bits[1:])
    late_keys, late_values = gathered(far_key, bits[1:]), gathered(far_value, bits[1:])
    queries = [query_packet, exchange(query_packet, query_mask)]
    early = [0, far] + sorted(mask for mask in pairs if mask)
    late = sorted(mask ^ far for mask in late_keys if mask)
    late_lines = range(2 + len(early), 2 + len(early) + len(late))

    def summed(sums, sources, held, flops=0):
        return pl.pallas_call(
            functools.partial(sums_kernel, held),
            out_shape=jax.ShapeDtypeStruct(own_sums.shape, jnp.float32),
            in_specs=[VMEM] * (1 + len(sources)),
            out_specs=VMEM,
            compiler_params=params,
            cost_estimate=cost(flops),
        )(sums, *sources)

    sums = summed(own_sums, [far_key], [3], 2 * AHEAD)
    sources = [queries[1]] + [pairs[mask] for mask in early[2:]]
    sums = summed(sums, sources, [2, *range(4, 3 + len(sources))])
    if splits == 2:
        others = lax.ppermute(sums, "head", [(0, 1), (1, 0)])
        flips = []
        for i in range(2 * count):
            flips.append((i, ((i // 2) ^ bits[1]) * 2 + (i % 2 ^ 1)))
        crossed = lax.ppermute(sums, ("tm", "head"), flips)
        late_lines = None
    else:
        sums = summed(sums, [late_keys[mask ^ far] for mask in late], late_lines)
        sums = lax.psum(sums, "head")
        others = crossed = jnp.zeros_like(sums)

    early_masks = early + [mask ^ 1 for mask in early]
    all_masks = early_masks + late + [mask ^ 1 for mask in late]
    query_norm, biases = pl.pallas_call(
        functools.partial(query_kernel, width * splits, all_masks),
        out_shape=[
            jax.ShapeDtypeStruct((2 * rows, width), jnp.bfloat16),
            jax.ShapeDtypeStruct((16, len(all_masks) * HD), jnp.float32),
        ],
        in_specs=[VMEM] * 5,
        out_specs=[VMEM] * 2,
        compiler_params=params,
    )(query_gain, sums, others, *queries)

    def packed(kernel, masks, operands, flops):
        return pl.pallas_call(
            kernel,
            out_shape=jax.ShapeDtypeStruct((2 * len(masks) * rows, width), jnp.bfloat16),
            in_specs=[VMEM] * (1 + len(operands)),
            out_specs=VMEM,
            compiler_params=params,
            cost_estimate=cost(flops),
        )(key_gain, *operands)

    early_pack = packed(
        functools.partial(early_kernel, width * splits),
        early,
        [sums, others, far_key, far_value, own_pair] + [pairs[mask] for mask in early[2:]],
        AHEAD,
    )
    def step(first, pack, *state):
        return pl.pallas_call(
            functools.partial(step_kernel, first),
            out_shape=[
                jax.ShapeDtypeStruct((2 * rows, width), jnp.float32),
                jax.ShapeDtypeStruct((2 * rows, 2 * width), jnp.float32),
            ],
            in_specs=[VMEM] * (3 + len(state)),
            out_specs=[VMEM] * 2,
            compiler_params=params,
        )(query_norm, biases, pack, *state)

    state = step(0, early_pack)
    late_pack = packed(
        functools.partial(late_kernel, width * splits, late_lines),
        late,
        [sums, others, crossed]
        + [late_keys[mask ^ far] for mask in late]
        + [late_values[mask ^ far] for mask in late]
        + [state[1]],
        3 * AHEAD,
    )
    state = step(len(early), exchange(early_pack, 1), *state)
    state = step(2 * len(early), late_pack, *state)
    last_pack = exchange(late_pack, 1)

    def last(place, out_shape):
        return pl.pallas_call(
            functools.partial(last_attention, place),
            out_shape=out_shape,
            in_specs=[VMEM] * 5,
            out_specs=[VMEM] * len(out_shape),
            compiler_params=params,
        )(query_norm, biases, last_pack, *state)

    (packet,) = last(1, [jax.ShapeDtypeStruct((rows + EXTRA, width), jnp.bfloat16)])
    own, own_lines = last(
        0,
        [
            jax.ShapeDtypeStruct((rows, width), jnp.float32),
            jax.ShapeDtypeStruct((16, width), jnp.float32),
        ],
    )
    gates = pl.pallas_call(
        gate_kernel,
        out_shape=jax.ShapeDtypeStruct((16, width), jnp.float32),
        in_specs=[SMEM, VMEM],
        out_specs=VMEM,
        compiler_params=params,
    )(frame_step, gate_table)
    packet = exchange(packet, query_mask)

    return pl.pallas_call(
        merge_kernel,
        out_shape=jax.ShapeDtypeStruct((rows, width), jnp.bfloat16),
        in_specs=[VMEM] * 4,
        out_specs=VMEM,
        compiler_params=params,
    )(own, own_lines, packet, gates)


def solution(mesh):
    return jax.shard_map(
        local,
        mesh=mesh,
        in_specs=(
            P("tm", "head"),
            P("tm", "head"),
            P("tm", "head"),
            P("head"),
            P("head"),
            P(None, "head"),
            P(),
            P("tm", None),
        ),
        out_specs=P("tm", "head"),
        check_vma=False,
    )
```

```python
import functools

import jax
import jax.numpy as jnp
from jax import lax
from jax.experimental import pallas as pl
from jax.experimental.pallas import tpu as pltpu
from jax.sharding import PartitionSpec as P

HD = 128
BLK = 64
FRAME_TOK = 1560
EPSILON = 1e-06
LOG2E = 1.4426950408889634
SCALE = HD ** (-0.5) * LOG2E
MASKED = -1e30
EXTRA = 16
AHEAD = 4 * 10**9
ANY = pl.BlockSpec(memory_space=pl.ANY)
VMEM = pl.BlockSpec(memory_space=pltpu.VMEM)
SMEM = pl.BlockSpec(memory_space=pltpu.SMEM)


def spread(row):
    return jnp.broadcast_to(row, (row.shape[1], row.shape[1])).T


def squares(source_ref):
    wide = source_ref[:HD, :].astype(jnp.float32)
    square = wide * wide
    part = square[:, :HD]
    for low in range(HD, square.shape[1], HD):
        part = part + square[:, low : low + HD]
    return jnp.sum(part.T, axis=0, keepdims=True)


def own_kernel(query_hbm, key_hbm, value_hbm, pair_out, sums_out, query_ref, sems):
    rows = query_ref.shape[0]
    copies = [
        pltpu.make_async_copy(key_hbm, pair_out.at[:rows, :], sems.at[0]),
        pltpu.make_async_copy(value_hbm, pair_out.at[rows:, :], sems.at[1]),
        pltpu.make_async_copy(query_hbm, query_ref, sems.at[2]),
    ]
    for copy in copies:
        copy.start()
    sums_out[...] = jnp.zeros_like(sums_out)
    copies[0].wait()
    sums_out[1:2, :] = squares(pair_out)
    copies[2].wait()
    sums_out[0:1, :] = squares(query_ref)
    copies[1].wait()


def sums_kernel(lines, before_ref, *refs):
    *sources, out_ref = refs
    out_ref[...] = before_ref[...]
    for line, source_ref in zip(lines, sources):
        out_ref[line : line + 1, :] = squares(source_ref)


def factor_of(line, full_width):
    return spread(lax.rsqrt(line / full_width + EPSILON))


def normed(source_ref, factor, gain_ref):
    parts = []
    for low in range(0, source_ref.shape[1], HD):
        wide = source_ref[:HD, low : low + HD].astype(jnp.float32)
        parts.append((wide * factor * gain_ref[:, low : low + HD]).astype(jnp.bfloat16))
    return jnp.concatenate(parts, axis=1)


def query_kernel(full_width, query_ref, far_ref, gain_ref, own_ref, other_ref, out_ref):
    total = own_ref[0:1, :] + other_ref[0:1, :]
    out_ref[:HD, :] = normed(query_ref, factor_of(total, full_width), gain_ref)
    far = far_ref[...].astype(jnp.float32)
    far = jnp.concatenate([far, jnp.full((1, HD - far.shape[1]), -1.0)], axis=1)
    out_ref[HD:, :HD] = jnp.broadcast_to(far, (EXTRA, HD)).astype(jnp.bfloat16)
    out_ref[HD:, HD:] = jnp.zeros((EXTRA, out_ref.shape[1] - HD), jnp.bfloat16)


def bias_kernel(key_masks, own_ref, remote_ref, bias_out):
    me = lax.axis_index("tm")
    query_mask = lax.axis_size("tm") // 4
    lane = lax.broadcasted_iota(jnp.int32, (1, HD), 1)
    half = (lane >= BLK).astype(jnp.float32)
    for place, query_ref in enumerate((own_ref, remote_ref)):
        far = query_ref[HD:, :HD].astype(jnp.float32)[:1]
        query_id = me ^ (place * query_mask)
        for block, key_mask in enumerate(key_masks):
            key_id = me ^ key_mask
            choice = jnp.sum(jnp.where(lane == key_id, far, 0.0), axis=1, keepdims=True)
            taken = (choice == half) | (jnp.abs(query_id - key_id) <= 1)
            bias_out[8 * place : 8 * place + 8, block * HD : (block + 1) * HD] = (
                jnp.broadcast_to(jnp.where(taken, 0.0, MASKED), (8, HD))
            )


def early_kernel(full_width, gain_ref, own_ref, other_ref, key_ref, value_ref, *refs):
    *pairs, pack_out = refs
    held = 1 + len(pairs)
    sources = [(pairs[0], pairs[0]), (key_ref, value_ref)] + [(pair, pair) for pair in pairs[1:]]
    for place, (key, value) in enumerate(sources):
        line = 1 + place + (place > 0)
        total = own_ref[line : line + 1, :] + other_ref[line : line + 1, :]
        pack_out[place * HD : (place + 1) * HD, :] = normed(
            key, factor_of(total, full_width), gain_ref
        )
        low = 0 if value is value_ref else HD
        pack_out[(held + place) * HD : (held + place + 1) * HD, :] = value[low : low + HD, :]


def late_kernel(full_width, lines, gain_ref, own_ref, other_ref, cross_ref, *refs):
    *pairs, _, pack_out = refs
    held = len(pairs) // 2
    for place, (key, value) in enumerate(zip(pairs[:held], pairs[held:])):
        if lines is None:
            total = squares(key) + cross_ref[3:4, :]
        else:
            line = lines[place]
            total = own_ref[line : line + 1, :] + other_ref[line : line + 1, :]
        pack_out[place * HD : (place + 1) * HD, :] = normed(
            key, factor_of(total, full_width), gain_ref
        )
        pack_out[(held + place) * HD : (held + place + 1) * HD, :] = value[...]


def absorb(queries, pack_ref, biases, olds):
    half = pack_ref.shape[0] // 2
    heads, count = len(queries), len(biases)
    scores = []
    for head, query in enumerate(queries):
        scores.append(
            lax.dot_general(
                query,
                pack_ref[:half, head * HD : (head + 1) * HD],
                (((1,), (1,)), ((), ())),
                preferred_element_type=jnp.float32,
            )
        )
    spots = [(head, place) for head in range(heads) for place in range(count)]
    logits, tops, weights, totals = {}, {}, {}, {}
    for head, place in spots:
        part = scores[head][place * HD : (place + 1) * HD]
        logits[head, place] = part * SCALE + biases[place]
    for spot in spots:
        top = jnp.broadcast_to(jnp.max(logits[spot], axis=1, keepdims=True), (HD, HD))
        tops[spot] = top if olds is None else jnp.maximum(top, olds[spot][0])
    for spot in spots:
        weights[spot] = [
            jnp.exp2(logits[spot][:, left : left + HD] - tops[spot])
            for left in range(0, half, HD)
        ]
    added = []
    for head in range(heads):
        rounded = [
            jnp.concatenate([w.astype(jnp.bfloat16) for w in weights[head, place]], axis=1)
            for place in range(count)
        ]
        added.append(
            jnp.dot(
                jnp.concatenate(rounded, axis=0),
                pack_ref[half:, head * HD : (head + 1) * HD],
                preferred_element_type=jnp.float32,
            )
        )
    for spot in spots:
        total = jnp.sum(functools.reduce(jnp.add, weights[spot]), axis=1, keepdims=True)
        totals[spot] = jnp.broadcast_to(total, (HD, HD))
    results = {}
    for head, place in spots:
        spot = (head, place)
        context, total = added[head][place * HD : (place + 1) * HD], totals[spot]
        if olds is not None:
            fade = jnp.exp2(olds[spot][0] - tops[spot])
            total = total + olds[spot][1] * fade
            context = context + olds[spot][2] * fade
        results[spot] = (tops[spot], total, context)
    return results


def held_state(context_ref, stats_ref, head, place):
    part, low, wide = slice(place * HD, (place + 1) * HD), head * HD, 2 * head * HD
    return (
        stats_ref[part, wide : wide + HD],
        stats_ref[part, wide + HD : wide + 2 * HD],
        context_ref[part, low : low + HD],
    )


def step_kernel(first, own_ref, remote_ref, bias_ref, pack_ref, *refs):
    olds, (context_out, stats_out) = refs[:-2], refs[-2:]
    heads, keys = own_ref.shape[1] // HD, pack_ref.shape[0] // 2
    left = first * HD
    biases = [bias_ref[8 * place : 8 * place + 1, left : left + keys] for place in range(2)]
    state = None
    if olds:
        state = {
            (head, place): held_state(*olds, head, place)
            for head in range(heads)
            for place in range(2)
        }
    queries = [
        jnp.concatenate([ref[:HD, head * HD : (head + 1) * HD] for ref in (own_ref, remote_ref)])
        for head in range(heads)
    ]
    for (head, place), result in absorb(queries, pack_ref, biases, state).items():
        part, low, wide = slice(place * HD, (place + 1) * HD), head * HD, 2 * head * HD
        top, total, context = result
        context_out[part, low : low + HD] = context
        stats_out[part, wide : wide + HD] = top
        stats_out[part, wide + HD : wide + 2 * HD] = total


def last_attention(place, query_ref, bias_ref, pack_ref, context_ref, stats_ref, *outs):
    heads, keys = query_ref.shape[1] // HD, pack_ref.shape[0] // 2
    part = slice(place * HD, (place + 1) * HD)
    bias = bias_ref[8 * place : 8 * place + 1, bias_ref.shape[1] - keys :]
    lane = lax.broadcasted_iota(jnp.int32, (1, HD), 1)
    state = {(h, 0): held_state(context_ref, stats_ref, h, place) for h in range(heads)}
    queries = [query_ref[:HD, head * HD : (head + 1) * HD] for head in range(heads)]
    results = absorb(queries, pack_ref, [bias], state)
    columns = jnp.zeros((HD, HD), jnp.float32)
    for head in range(heads):
        top, total, context = results[head, 0]
        outs[0][:HD, head * HD : (head + 1) * HD] = context.astype(outs[0].dtype)
        line = 2 * head
        columns = jnp.where(lane == line, top, jnp.where(lane == line + 1, total, columns))
    lines = columns.T
    sub = lax.broadcasted_iota(jnp.int32, (EXTRA, HD), 0)
    for head in range(heads):
        low = head * HD
        pair = (lines[2 * head : 2 * head + 1, :], lines[2 * head + 1 : 2 * head + 2, :])
        if place == 0:
            for row, value in enumerate(pair):
                outs[1][8 * row : 8 * row + 8, low : low + HD] = jnp.broadcast_to(value, (8, HD))
        else:
            piece_rows = jnp.zeros((EXTRA, HD), jnp.float32)
            for row, value in enumerate(pair):
                first = value.astype(jnp.bfloat16).astype(jnp.float32)
                second = (value - first).astype(jnp.bfloat16).astype(jnp.float32)
                for piece, part_value in enumerate((first, second, value - first - second)):
                    piece_rows = jnp.where(sub == 3 * row + piece, part_value, piece_rows)
            outs[0][HD:, low : low + HD] = piece_rows.astype(jnp.bfloat16)


def gate_kernel(step_ref, table_ref, out_ref):
    rows = out_ref.shape[0] // 2
    start = lax.axis_index("tm") * HD
    first = step_ref[start // FRAME_TOK]
    last = step_ref[(start + HD - 1) // FRAME_TOK]
    out_ref[:rows, :] = jnp.broadcast_to(table_ref[pl.ds(first, 1), :], (rows, out_ref.shape[1]))
    out_ref[rows:, :] = jnp.broadcast_to(table_ref[pl.ds(last, 1), :], (rows, out_ref.shape[1]))


def merge_kernel(own_ref, lines_ref, packet_ref, gate_ref, out_ref):
    rows, width = own_ref.shape
    pieces = packet_ref[rows:, :].astype(jnp.float32)
    own_top, own_total = lines_ref[0:1, :], lines_ref[8:9, :]
    other_top = pieces[0:1] + pieces[1:2] + pieces[2:3]
    other_total = pieces[3:4] + pieces[4:5] + pieces[5:6]
    top = jnp.maximum(own_top, other_top)
    own_share, other_share = jnp.exp2(own_top - top), jnp.exp2(other_top - top)
    scale = 1.0 / (own_total * own_share + other_total * other_share)
    own_share, other_share = own_share * scale, other_share * scale
    start = lax.axis_index("tm") * rows
    first_rows = (start // FRAME_TOK + 1) * FRAME_TOK - start
    row_ids = lax.broadcasted_iota(jnp.int32, (rows, 1), 0)
    for low in range(0, width, HD):
        high = low + HD
        context = own_ref[:, low:high] * spread(own_share[:, low:high])
        other = packet_ref[:rows, low:high].astype(jnp.float32)
        context += other * spread(other_share[:, low:high])
        gate = jnp.where(
            row_ids < first_rows, gate_ref[0:1, low:high], gate_ref[8:9, low:high]
        )
        out_ref[:, low:high] = (context * gate).astype(jnp.bfloat16)


def exchange(array, mask):
    count = lax.axis_size("tm")
    return lax.ppermute(array, "tm", [(i, i ^ mask) for i in range(count)])


def gathered(array, bits):
    held = {0: array}
    for bit in bits:
        for mask in list(held):
            held[mask ^ bit] = exchange(held[mask], bit)
    return held


def cost(flops):
    return pl.CostEstimate(flops=flops, bytes_accessed=0, transcendentals=0)


def local(
    query_proj, key_proj, value_proj, query_gain, key_gain, gate_table, frame_step, far_blocks
):
    rows, width = query_proj.shape
    count = lax.axis_size("tm")
    splits = lax.axis_size("head")
    full_width = width * splits
    params = pltpu.CompilerParams(vmem_limit_bytes=(8 + count // 2) * 2**20)
    query_mask = count // 4
    bits = [1 << place for place in range(1, count.bit_length() - 1)]
    bits = [bit for bit in bits[::-1] if bit != query_mask]
    query_gain = query_gain.reshape(1, width)
    key_gain = key_gain.reshape(1, width)

    lines = 2 + 2 ** len(bits)
    lines += -lines % 8
    own_pair, own_sums = pl.pallas_call(
        own_kernel,
        out_shape=[
            jax.ShapeDtypeStruct((2 * rows, width), jnp.bfloat16),
            jax.ShapeDtypeStruct((lines, rows), jnp.float32),
        ],
        in_specs=[ANY] * 3,
        out_specs=[VMEM] * 2,
        scratch_shapes=[
            pltpu.VMEM((rows, width), jnp.bfloat16),
            pltpu.SemaphoreType.DMA((3,)),
        ],
    )(query_proj, key_proj, value_proj)
    far = bits[0]
    far_key, far_value = exchange(key_proj, far), exchange(value_proj, far)
    pairs = gathered(own_pair, bits[1:])
    late_keys, late_values = gathered(far_key, bits[1:]), gathered(far_value, bits[1:])
    early = [0, far] + sorted(mask for mask in pairs if mask)
    late = sorted(mask ^ far for mask in late_keys if mask)
    late_lines = range(2 + len(early), 2 + len(early) + len(late))

    def summed(sums, sources, held, flops=0):
        return pl.pallas_call(
            functools.partial(sums_kernel, held),
            out_shape=jax.ShapeDtypeStruct(own_sums.shape, jnp.float32),
            in_specs=[VMEM] * (1 + len(sources)),
            out_specs=VMEM,
            compiler_params=params,
            cost_estimate=cost(flops),
        )(sums, *sources)

    sums = summed(own_sums, [far_key], [3], 2 * AHEAD)
    sources = [pairs[mask] for mask in early[2:]]
    sums = summed(sums, sources, range(4, 4 + len(sources)))
    if splits == 2:
        others = lax.ppermute(sums, "head", [(0, 1), (1, 0)])
        flips = []
        for i in range(2 * count):
            flips.append((i, ((i // 2) ^ bits[1]) * 2 + (i % 2 ^ 1)))
        crossed = lax.ppermute(sums, ("tm", "head"), flips)
        late_lines = None
    else:
        sums = summed(sums, [late_keys[mask ^ far] for mask in late], late_lines)
        sums = lax.psum(sums, "head")
        others = crossed = jnp.zeros_like(sums)

    early_masks = early + [mask ^ 1 for mask in early]
    all_masks = early_masks + late + [mask ^ 1 for mask in late]
    query_packet = pl.pallas_call(
        functools.partial(query_kernel, width * splits),
        out_shape=jax.ShapeDtypeStruct((rows + EXTRA, width), jnp.bfloat16),
        in_specs=[VMEM] * 5,
        out_specs=VMEM,
        compiler_params=params,
    )(query_proj, far_blocks, query_gain, sums, others)
    queries = [query_packet, exchange(query_packet, query_mask)]
    biases = pl.pallas_call(
        functools.partial(bias_kernel, all_masks),
        out_shape=jax.ShapeDtypeStruct((16, len(all_masks) * HD), jnp.float32),
        in_specs=[VMEM] * 2,
        out_specs=VMEM,
        compiler_params=params,
    )(*queries)

    def packed(kernel, masks, operands, flops):
        return pl.pallas_call(
            kernel,
            out_shape=jax.ShapeDtypeStruct((2 * len(masks) * rows, width), jnp.bfloat16),
            in_specs=[VMEM] * (1 + len(operands)),
            out_specs=VMEM,
            compiler_params=params,
            cost_estimate=cost(flops),
        )(key_gain, *operands)

    early_pack = packed(
        functools.partial(early_kernel, width * splits),
        early,
        [sums, others, far_key, far_value, own_pair] + [pairs[mask] for mask in early[2:]],
        AHEAD,
    )
    def step(first, pack, *state):
        return pl.pallas_call(
            functools.partial(step_kernel, first),
            out_shape=[
                jax.ShapeDtypeStruct((2 * rows, width), jnp.float32),
                jax.ShapeDtypeStruct((2 * rows, 2 * width), jnp.float32),
            ],
            in_specs=[VMEM] * (4 + len(state)),
            out_specs=[VMEM] * 2,
            compiler_params=params,
        )(*queries, biases, pack, *state)

    state = step(0, early_pack)
    late_pack = packed(
        functools.partial(late_kernel, width * splits, late_lines),
        late,
        [sums, others, crossed]
        + [late_keys[mask ^ far] for mask in late]
        + [late_values[mask ^ far] for mask in late]
        + [state[1]],
        3 * AHEAD,
    )
    state = step(len(early), exchange(early_pack, 1), *state)
    state = step(2 * len(early), late_pack, *state)
    last_pack = exchange(late_pack, 1)

    def last(place, out_shape):
        return pl.pallas_call(
            functools.partial(last_attention, place),
            out_shape=out_shape,
            in_specs=[VMEM] * 5,
            out_specs=[VMEM] * len(out_shape),
            compiler_params=params,
        )(queries[place], biases, last_pack, *state)

    (packet,) = last(1, [jax.ShapeDtypeStruct((rows + EXTRA, width), jnp.bfloat16)])
    own, own_lines = last(
        0,
        [
            jax.ShapeDtypeStruct((rows, width), jnp.float32),
            jax.ShapeDtypeStruct((16, width), jnp.float32),
        ],
    )
    gates = pl.pallas_call(
        gate_kernel,
        out_shape=jax.ShapeDtypeStruct((16, width), jnp.float32),
        in_specs=[SMEM, VMEM],
        out_specs=VMEM,
        compiler_params=params,
    )(frame_step, gate_table)
    packet = exchange(packet, query_mask)

    return pl.pallas_call(
        merge_kernel,
        out_shape=jax.ShapeDtypeStruct((rows, width), jnp.bfloat16),
        in_specs=[VMEM] * 4,
        out_specs=VMEM,
        compiler_params=params,
    )(own, own_lines, packet, gates)


def solution(mesh):
    return jax.shard_map(
        local,
        mesh=mesh,
        in_specs=(
            P("tm", "head"),
            P("tm", "head"),
            P("tm", "head"),
            P("head"),
            P("head"),
            P(None, "head"),
            P(),
            P("tm", None),
        ),
        out_specs=P("tm", "head"),
        check_vma=False,
    )
```

```python
import functools

import jax
import jax.numpy as jnp
from jax import lax
from jax.experimental import pallas as pl
from jax.experimental.pallas import tpu as pltpu
from jax.sharding import PartitionSpec as P

HD = 128
BLK = 64
FRAME_TOK = 1560
EPSILON = 1e-06
LOG2E = 1.4426950408889634
SCALE = HD ** (-0.5) * LOG2E
MASKED = -1e30
EXTRA = 16
UNIT = 10**9
ANY = pl.BlockSpec(memory_space=pl.ANY)
VMEM = pl.BlockSpec(memory_space=pltpu.VMEM)
SMEM = pl.BlockSpec(memory_space=pltpu.SMEM)


def spread(row):
    return jnp.broadcast_to(row, (row.shape[1], row.shape[1])).T


def squares(source_ref):
    wide = source_ref[:HD, :].astype(jnp.float32)
    square = wide * wide
    part = square[:, :HD]
    for low in range(HD, square.shape[1], HD):
        part = part + square[:, low : low + HD]
    return jnp.sum(part.T, axis=0, keepdims=True)


def own_kernel(
    query_hbm, key_hbm, value_hbm, far_hbm, query_out, pair_out, sums_out, query_ref, far_ref, sems
):
    rows, width = query_ref.shape
    copies = [
        pltpu.make_async_copy(key_hbm, pair_out.at[:rows, :], sems.at[0]),
        pltpu.make_async_copy(value_hbm, pair_out.at[rows:, :], sems.at[1]),
        pltpu.make_async_copy(query_hbm, query_ref, sems.at[2]),
        pltpu.make_async_copy(far_hbm, far_ref, sems.at[3]),
    ]
    for copy in copies:
        copy.start()
    query_out[rows:, HD:] = jnp.zeros((EXTRA, width - HD), jnp.bfloat16)
    sums_out[...] = jnp.zeros_like(sums_out)
    copies[0].wait()
    sums_out[1:2, :] = squares(pair_out)
    copies[2].wait()
    query_out[:rows, :] = query_ref[...]
    sums_out[0:1, :] = squares(query_ref)
    copies[3].wait()
    far = far_ref[...].astype(jnp.float32)
    far = jnp.concatenate([far, jnp.full((1, HD - far.shape[1]), -1.0)], axis=1)
    query_out[rows:, :HD] = jnp.broadcast_to(far, (EXTRA, HD)).astype(jnp.bfloat16)
    copies[1].wait()


def relay_kernel(own_ref, cross_ref, out_ref):
    out_ref[...] = jnp.zeros_like(out_ref)
    out_ref[0:1, :] = own_ref[1:2, :]
    out_ref[1:2, :] = cross_ref[1:2, :]


def squares_kernel(*refs):
    *sources, out_ref = refs
    out_ref[...] = jnp.zeros_like(out_ref)
    for place, source_ref in enumerate(sources):
        out_ref[place : place + 1, :] = squares(source_ref)


def factor_of(line, full_width):
    return spread(lax.rsqrt(line / full_width + EPSILON))


def normed(source_ref, factor, gain_ref):
    parts = []
    for low in range(0, source_ref.shape[1], HD):
        wide = source_ref[:HD, low : low + HD].astype(jnp.float32)
        parts.append((wide * factor * gain_ref[:, low : low + HD]).astype(jnp.bfloat16))
    return jnp.concatenate(parts, axis=1)


def query_kernel(full_width, key_masks, rows, gain_ref, *refs):
    queries, others, (query_out, bias_out) = refs[:2], refs[2:4], refs[4:]
    me = lax.axis_index("tm")
    query_mask = lax.axis_size("tm") // 4
    lane = lax.broadcasted_iota(jnp.int32, (1, HD), 1)
    half = (lane >= BLK).astype(jnp.float32)
    for place, query_ref in enumerate(queries):
        total = squares(query_ref) + others[place][rows[place] : rows[place] + 1, :]
        query_out[place * HD : (place + 1) * HD, :] = normed(
            query_ref, factor_of(total, full_width), gain_ref
        )
        far = query_ref[HD:, :HD].astype(jnp.float32)[:1]
        query_id = me ^ (place * query_mask)
        for block, key_mask in enumerate(key_masks):
            key_id = me ^ key_mask
            choice = jnp.sum(jnp.where(lane == key_id, far, 0.0), axis=1, keepdims=True)
            taken = (choice == half) | (jnp.abs(query_id - key_id) <= 1)
            bias_out[8 * place : 8 * place + 8, block * HD : (block + 1) * HD] = (
                jnp.broadcast_to(jnp.where(taken, 0.0, MASKED), (8, HD))
            )


def pack_kernel(full_width, held, rows, gain_ref, *refs):
    keys, values, others = refs[:held], refs[held : 2 * held], refs[2 * held : 3 * held]
    pack_out = refs[-1]
    for place, (key, value) in enumerate(zip(keys, values)):
        total = squares(key) + others[place][rows[place] : rows[place] + 1, :]
        pack_out[place * HD : (place + 1) * HD, :] = normed(
            key, factor_of(total, full_width), gain_ref
        )
        low = value.shape[0] - HD
        pack_out[(held + place) * HD : (held + place + 1) * HD, :] = value[low : low + HD, :]


def absorb(queries, pack_ref, biases, olds):
    half = pack_ref.shape[0] // 2
    heads, count = len(queries), len(biases)
    scores = []
    for head, query in enumerate(queries):
        scores.append(
            lax.dot_general(
                query,
                pack_ref[:half, head * HD : (head + 1) * HD],
                (((1,), (1,)), ((), ())),
                preferred_element_type=jnp.float32,
            )
        )
    spots = [(head, place) for head in range(heads) for place in range(count)]
    logits, tops, weights, totals = {}, {}, {}, {}
    for head, place in spots:
        part = scores[head][place * HD : (place + 1) * HD]
        logits[head, place] = part * SCALE + biases[place]
    for spot in spots:
        top = jnp.broadcast_to(jnp.max(logits[spot], axis=1, keepdims=True), (HD, HD))
        tops[spot] = top if olds is None else jnp.maximum(top, olds[spot][0])
    for spot in spots:
        weights[spot] = [
            jnp.exp2(logits[spot][:, left : left + HD] - tops[spot])
            for left in range(0, half, HD)
        ]
    added = []
    for head in range(heads):
        rounded = [
            jnp.concatenate([w.astype(jnp.bfloat16) for w in weights[head, place]], axis=1)
            for place in range(count)
        ]
        added.append(
            jnp.dot(
                jnp.concatenate(rounded, axis=0),
                pack_ref[half:, head * HD : (head + 1) * HD],
                preferred_element_type=jnp.float32,
            )
        )
    for spot in spots:
        total = jnp.sum(functools.reduce(jnp.add, weights[spot]), axis=1, keepdims=True)
        totals[spot] = jnp.broadcast_to(total, (HD, HD))
    results = {}
    for head, place in spots:
        spot = (head, place)
        context, total = added[head][place * HD : (place + 1) * HD], totals[spot]
        if olds is not None:
            fade = jnp.exp2(olds[spot][0] - tops[spot])
            total = total + olds[spot][1] * fade
            context = context + olds[spot][2] * fade
        results[spot] = (tops[spot], total, context)
    return results


def held_state(context_ref, stats_ref, head, place):
    part, low, wide = slice(place * HD, (place + 1) * HD), head * HD, 2 * head * HD
    return (
        stats_ref[part, wide : wide + HD],
        stats_ref[part, wide + HD : wide + 2 * HD],
        context_ref[part, low : low + HD],
    )


def step_kernel(first, query_ref, bias_ref, pack_ref, *refs):
    olds, (context_out, stats_out) = refs[:-2], refs[-2:]
    heads, keys = query_ref.shape[1] // HD, pack_ref.shape[0] // 2
    left = first * HD
    biases = [bias_ref[8 * place : 8 * place + 1, left : left + keys] for place in range(2)]
    state = None
    if olds:
        state = {
            (head, place): held_state(*olds, head, place)
            for head in range(heads)
            for place in range(2)
        }
    queries = [query_ref[:, head * HD : (head + 1) * HD] for head in range(heads)]
    for (head, place), result in absorb(queries, pack_ref, biases, state).items():
        part, low, wide = slice(place * HD, (place + 1) * HD), head * HD, 2 * head * HD
        top, total, context = result
        context_out[part, low : low + HD] = context
        stats_out[part, wide : wide + HD] = top
        stats_out[part, wide + HD : wide + 2 * HD] = total


def last_attention(place, query_ref, bias_ref, pack_ref, context_ref, stats_ref, *outs):
    heads, keys = query_ref.shape[1] // HD, pack_ref.shape[0] // 2
    part = slice(place * HD, (place + 1) * HD)
    bias = bias_ref[8 * place : 8 * place + 1, bias_ref.shape[1] - keys :]
    lane = lax.broadcasted_iota(jnp.int32, (1, HD), 1)
    state = {(h, 0): held_state(context_ref, stats_ref, h, place) for h in range(heads)}
    queries = [query_ref[part, head * HD : (head + 1) * HD] for head in range(heads)]
    results = absorb(queries, pack_ref, [bias], state)
    columns = jnp.zeros((HD, HD), jnp.float32)
    for head in range(heads):
        top, total, context = results[head, 0]
        outs[0][:HD, head * HD : (head + 1) * HD] = context.astype(outs[0].dtype)
        line = 2 * head
        columns = jnp.where(lane == line, top, jnp.where(lane == line + 1, total, columns))
    lines = columns.T
    sub = lax.broadcasted_iota(jnp.int32, (EXTRA, HD), 0)
    for head in range(heads):
        low = head * HD
        pair = (lines[2 * head : 2 * head + 1, :], lines[2 * head + 1 : 2 * head + 2, :])
        if place == 0:
            for row, value in enumerate(pair):
                outs[1][8 * row : 8 * row + 8, low : low + HD] = jnp.broadcast_to(value, (8, HD))
        else:
            piece_rows = jnp.zeros((EXTRA, HD), jnp.float32)
            for row, value in enumerate(pair):
                first = value.astype(jnp.bfloat16).astype(jnp.float32)
                second = (value - first).astype(jnp.bfloat16).astype(jnp.float32)
                for piece, part_value in enumerate((first, second, value - first - second)):
                    piece_rows = jnp.where(sub == 3 * row + piece, part_value, piece_rows)
            outs[0][HD:, low : low + HD] = piece_rows.astype(jnp.bfloat16)


def gate_kernel(step_ref, table_ref, out_ref):
    rows = out_ref.shape[0] // 2
    start = lax.axis_index("tm") * HD
    first = step_ref[start // FRAME_TOK]
    last = step_ref[(start + HD - 1) // FRAME_TOK]
    out_ref[:rows, :] = jnp.broadcast_to(table_ref[pl.ds(first, 1), :], (rows, out_ref.shape[1]))
    out_ref[rows:, :] = jnp.broadcast_to(table_ref[pl.ds(last, 1), :], (rows, out_ref.shape[1]))


def merge_kernel(own_ref, lines_ref, packet_ref, gate_ref, out_ref):
    rows, width = own_ref.shape
    pieces = packet_ref[rows:, :].astype(jnp.float32)
    own_top, own_total = lines_ref[0:1, :], lines_ref[8:9, :]
    other_top = pieces[0:1] + pieces[1:2] + pieces[2:3]
    other_total = pieces[3:4] + pieces[4:5] + pieces[5:6]
    top = jnp.maximum(own_top, other_top)
    own_share, other_share = jnp.exp2(own_top - top), jnp.exp2(other_top - top)
    scale = 1.0 / (own_total * own_share + other_total * other_share)
    own_share, other_share = own_share * scale, other_share * scale
    start = lax.axis_index("tm") * rows
    first_rows = (start // FRAME_TOK + 1) * FRAME_TOK - start
    row_ids = lax.broadcasted_iota(jnp.int32, (rows, 1), 0)
    for low in range(0, width, HD):
        high = low + HD
        context = own_ref[:, low:high] * spread(own_share[:, low:high])
        other = packet_ref[:rows, low:high].astype(jnp.float32)
        context += other * spread(other_share[:, low:high])
        gate = jnp.where(
            row_ids < first_rows, gate_ref[0:1, low:high], gate_ref[8:9, low:high]
        )
        out_ref[:, low:high] = (context * gate).astype(jnp.bfloat16)


def exchange(array, mask):
    count = lax.axis_size("tm")
    return lax.ppermute(array, "tm", [(i, i ^ mask) for i in range(count)])


def gathered(array, bits):
    held = {0: array}
    for bit in bits:
        for mask in list(held):
            held[mask ^ bit] = exchange(held[mask], bit)
    return held


def cost(flops):
    return pl.CostEstimate(flops=flops, bytes_accessed=0, transcendentals=0)


def local(
    query_proj, key_proj, value_proj, query_gain, key_gain, gate_table, frame_step, far_blocks
):
    rows, width = query_proj.shape
    count = lax.axis_size("tm")
    splits = lax.axis_size("head")
    full_width = width * splits
    params = pltpu.CompilerParams(vmem_limit_bytes=(8 + count // 2) * 2**20)
    query_mask = count // 4
    bits = [1 << place for place in range(1, count.bit_length() - 1)]
    bits = [bit for bit in bits[::-1] if bit != query_mask]
    query_gain = query_gain.reshape(1, width)
    key_gain = key_gain.reshape(1, width)

    query_packet, own_pair, own_sums = pl.pallas_call(
        own_kernel,
        out_shape=[
            jax.ShapeDtypeStruct((rows + EXTRA, width), jnp.bfloat16),
            jax.ShapeDtypeStruct((2 * rows, width), jnp.bfloat16),
            jax.ShapeDtypeStruct((8, rows), jnp.float32),
        ],
        in_specs=[ANY] * 4,
        out_specs=[VMEM] * 3,
        scratch_shapes=[
            pltpu.VMEM((rows, width), jnp.bfloat16),
            pltpu.VMEM(far_blocks.shape, jnp.int32),
            pltpu.SemaphoreType.DMA((4,)),
        ],
    )(query_proj, key_proj, value_proj, far_blocks)
    far = bits[0]
    far_key, far_value = exchange(key_proj, far), exchange(value_proj, far)
    pairs = gathered(own_pair, bits[1:])
    late_keys, late_values = gathered(far_key, bits[1:]), gathered(far_value, bits[1:])
    queries = [query_packet, exchange(query_packet, query_mask)]
    early = [0, far] + sorted(mask for mask in pairs if mask)
    late = sorted(mask ^ far for mask in late_keys if mask)
    if splits == 2:
        flipped = [query_mask, bits[1]]
        others = lax.ppermute(own_sums, "head", [(0, 1), (1, 0)])
        across = []
        for mask in flipped:
            flips = []
            for i in range(2 * count):
                flips.append((i, ((i // 2) ^ mask) * 2 + (i % 2 ^ 1)))
            across.append(lax.ppermute(own_sums, ("tm", "head"), flips))
        relay = pl.pallas_call(
            relay_kernel,
            out_shape=jax.ShapeDtypeStruct((8, rows), jnp.float32),
            in_specs=[VMEM] * 2,
            out_specs=VMEM,
            compiler_params=params,
            cost_estimate=cost(UNIT),
        )(others, across[1])
        relayed = exchange(relay, far)
        query_others = [(others, 0), (across[0], 0)]
        early_others = [(others, 1), (relayed, 0), (across[1], 1)]
        late_others = [(relayed, 1)]
    else:
        sources = queries + [far_key] + [pairs[mask] for mask in early if mask != far]
        sources += [late_keys[mask ^ far] for mask in late]
        lines = len(sources) + -len(sources) % 8
        own_rows = pl.pallas_call(
            squares_kernel,
            out_shape=jax.ShapeDtypeStruct((lines, rows), jnp.float32),
            in_specs=[VMEM] * len(sources),
            out_specs=VMEM,
            compiler_params=params,
        )(*sources)
        rest = lax.psum(own_rows, "head") - own_rows
        query_others = [(rest, 0), (rest, 1)]
        early_others = [(rest, 3), (rest, 2)] + [(rest, 4 + i) for i in range(len(early) - 2)]
        late_others = [(rest, 2 + len(early) + i) for i in range(len(late))]

    early_masks = early + [mask ^ 1 for mask in early]
    all_masks = early_masks + late + [mask ^ 1 for mask in late]
    query_norm, biases = pl.pallas_call(
        functools.partial(
            query_kernel, width * splits, all_masks, [row for _, row in query_others]
        ),
        out_shape=[
            jax.ShapeDtypeStruct((2 * rows, width), jnp.bfloat16),
            jax.ShapeDtypeStruct((16, len(all_masks) * HD), jnp.float32),
        ],
        in_specs=[VMEM] * 5,
        out_specs=[VMEM] * 2,
        compiler_params=params,
    )(query_gain, *queries, *[rest for rest, _ in query_others])

    def packed(keys, values, other_rows, flops, *after):
        held = len(keys)
        return pl.pallas_call(
            functools.partial(pack_kernel, width * splits, held, [row for _, row in other_rows]),
            out_shape=jax.ShapeDtypeStruct((2 * held * rows, width), jnp.bfloat16),
            in_specs=[VMEM] * (1 + 3 * held + len(after)),
            out_specs=VMEM,
            compiler_params=params,
            cost_estimate=cost(flops),
        )(key_gain, *keys, *values, *[rest for rest, _ in other_rows], *after)

    far_rows = pl.pallas_call(
        squares_kernel,
        out_shape=jax.ShapeDtypeStruct((8, rows), jnp.float32),
        in_specs=[VMEM],
        out_specs=VMEM,
        compiler_params=params,
        cost_estimate=cost(8 * UNIT),
    )(far_key)
    near = [pairs[mask] for mask in early if mask != far]
    early_pack = packed(
        [near[0], far_key, *near[1:]],
        [near[0], far_value, *near[1:]],
        early_others,
        4 * UNIT,
        far_rows,
    )

    def step(first, pack, *state):
        return pl.pallas_call(
            functools.partial(step_kernel, first),
            out_shape=[
                jax.ShapeDtypeStruct((2 * rows, width), jnp.float32),
                jax.ShapeDtypeStruct((2 * rows, 2 * width), jnp.float32),
            ],
            in_specs=[VMEM] * (3 + len(state)),
            out_specs=[VMEM] * 2,
            compiler_params=params,
        )(query_norm, biases, pack, *state)

    state = step(0, early_pack)
    late_pack = packed(
        [late_keys[mask ^ far] for mask in late],
        [late_values[mask ^ far] for mask in late],
        late_others,
        12 * UNIT,
        state[1],
    )
    state = step(len(early), exchange(early_pack, 1), *state)
    state = step(2 * len(early), late_pack, *state)
    last_pack = exchange(late_pack, 1)

    def last(place, out_shape):
        return pl.pallas_call(
            functools.partial(last_attention, place),
            out_shape=out_shape,
            in_specs=[VMEM] * 5,
            out_specs=[VMEM] * len(out_shape),
            compiler_params=params,
        )(query_norm, biases, last_pack, *state)

    (packet,) = last(1, [jax.ShapeDtypeStruct((rows + EXTRA, width), jnp.bfloat16)])
    own, own_lines = last(
        0,
        [
            jax.ShapeDtypeStruct((rows, width), jnp.float32),
            jax.ShapeDtypeStruct((16, width), jnp.float32),
        ],
    )
    gates = pl.pallas_call(
        gate_kernel,
        out_shape=jax.ShapeDtypeStruct((16, width), jnp.float32),
        in_specs=[SMEM, VMEM],
        out_specs=VMEM,
        compiler_params=params,
    )(frame_step, gate_table)
    packet = exchange(packet, query_mask)

    return pl.pallas_call(
        merge_kernel,
        out_shape=jax.ShapeDtypeStruct((rows, width), jnp.bfloat16),
        in_specs=[VMEM] * 4,
        out_specs=VMEM,
        compiler_params=params,
    )(own, own_lines, packet, gates)


def solution(mesh):
    return jax.shard_map(
        local,
        mesh=mesh,
        in_specs=(
            P("tm", "head"),
            P("tm", "head"),
            P("tm", "head"),
            P("head"),
            P("head"),
            P(None, "head"),
            P(),
            P("tm", None),
        ),
        out_specs=P("tm", "head"),
        check_vma=False,
    )
```

```python
import functools

import jax
import jax.numpy as jnp
from jax import lax
from jax.experimental import pallas as pl
from jax.experimental.pallas import tpu as pltpu
from jax.sharding import PartitionSpec as P

HD = 128
BLK = 64
FRAME_TOK = 1560
EPSILON = 1e-06
LOG2E = 1.4426950408889634
SCALE = HD ** (-0.5) * LOG2E
MASKED = -1e30
EXTRA = 16
UNIT = 10**9
ANY = pl.BlockSpec(memory_space=pl.ANY)
VMEM = pl.BlockSpec(memory_space=pltpu.VMEM)
SMEM = pl.BlockSpec(memory_space=pltpu.SMEM)


def spread(row):
    return jnp.broadcast_to(row, (row.shape[1], row.shape[1])).T


def squares(source_ref):
    wide = source_ref[:HD, :].astype(jnp.float32)
    square = wide * wide
    part = square[:, :HD]
    for low in range(HD, square.shape[1], HD):
        part = part + square[:, low : low + HD]
    return jnp.sum(part.T, axis=0, keepdims=True)


def sums_kernel(query_ref, key_ref, out_ref):
    out_ref[...] = jnp.zeros_like(out_ref)
    out_ref[0:1, :] = squares(query_ref)
    out_ref[1:2, :] = squares(key_ref)


def factor_of(line, full_width):
    return spread(lax.rsqrt(line / full_width + EPSILON))


def normed(source_ref, factor, gain_ref):
    parts = []
    for low in range(0, source_ref.shape[1], HD):
        wide = source_ref[:HD, low : low + HD].astype(jnp.float32)
        parts.append((wide * factor * gain_ref[:, low : low + HD]).astype(jnp.bfloat16))
    return jnp.concatenate(parts, axis=1)


def key_kernel(full_width, key_ref, gain_ref, own_ref, other_ref, out_ref):
    total = own_ref[1:2, :] + other_ref[1:2, :]
    out_ref[...] = normed(key_ref, factor_of(total, full_width), gain_ref)


def query_kernel(
    full_width,
    query_ref,
    key_ref,
    value_ref,
    gain_ref,
    far_ref,
    own_ref,
    other_ref,
    query_out,
    pair_out,
):
    pair_out[:HD, :] = key_ref[...]
    pair_out[HD:, :] = value_ref[...]
    total = own_ref[0:1, :] + other_ref[0:1, :]
    query_out[:HD, :] = normed(query_ref, factor_of(total, full_width), gain_ref)
    far = far_ref[...].astype(jnp.float32)
    far = jnp.concatenate([far, jnp.full((1, HD - far.shape[1]), -1.0)], axis=1)
    query_out[HD:, :HD] = jnp.broadcast_to(far, (EXTRA, HD)).astype(jnp.bfloat16)
    query_out[HD:, HD:] = jnp.zeros((EXTRA, query_out.shape[1] - HD), jnp.bfloat16)


def bias_kernel(key_masks, own_ref, remote_ref, bias_out):
    me = lax.axis_index("tm")
    query_mask = lax.axis_size("tm") // 4
    lane = lax.broadcasted_iota(jnp.int32, (1, HD), 1)
    half = (lane >= BLK).astype(jnp.float32)
    for place, query_ref in enumerate((own_ref, remote_ref)):
        far = query_ref[HD:, :HD].astype(jnp.float32)[:1]
        query_id = me ^ (place * query_mask)
        for block, key_mask in enumerate(key_masks):
            key_id = me ^ key_mask
            choice = jnp.sum(jnp.where(lane == key_id, far, 0.0), axis=1, keepdims=True)
            taken = (choice == half) | (jnp.abs(query_id - key_id) <= 1)
            bias_out[8 * place : 8 * place + 8, block * HD : (block + 1) * HD] = (
                jnp.broadcast_to(jnp.where(taken, 0.0, MASKED), (8, HD))
            )


def copy_kernel(source_ref, out_ref):
    out_ref[...] = source_ref[...]


def pack_kernel(held, *refs):
    keys, values, pack_out = refs[:held], refs[held : 2 * held], refs[-1]
    for place, key_ref in enumerate(keys):
        pack_out[place * HD : (place + 1) * HD, :] = key_ref[:HD, :]
    for place, value_ref in enumerate(values, start=held):
        low = value_ref.shape[0] - HD
        pack_out[place * HD : (place + 1) * HD, :] = value_ref[low:, :]


def absorb(queries, pack_ref, biases, olds):
    half = pack_ref.shape[0] // 2
    heads, count = len(queries), len(biases)
    scores = []
    for head, query in enumerate(queries):
        scores.append(
            lax.dot_general(
                query,
                pack_ref[:half, head * HD : (head + 1) * HD],
                (((1,), (1,)), ((), ())),
                preferred_element_type=jnp.float32,
            )
        )
    spots = [(head, place) for head in range(heads) for place in range(count)]
    logits, tops, weights, totals = {}, {}, {}, {}
    for head, place in spots:
        part = scores[head][place * HD : (place + 1) * HD]
        logits[head, place] = part * SCALE + biases[place]
    for spot in spots:
        top = jnp.broadcast_to(jnp.max(logits[spot], axis=1, keepdims=True), (HD, HD))
        tops[spot] = top if olds is None else jnp.maximum(top, olds[spot][0])
    for spot in spots:
        weights[spot] = [
            jnp.exp2(logits[spot][:, left : left + HD] - tops[spot])
            for left in range(0, half, HD)
        ]
    added = []
    for head in range(heads):
        rounded = [
            jnp.concatenate([w.astype(jnp.bfloat16) for w in weights[head, place]], axis=1)
            for place in range(count)
        ]
        added.append(
            jnp.dot(
                jnp.concatenate(rounded, axis=0),
                pack_ref[half:, head * HD : (head + 1) * HD],
                preferred_element_type=jnp.float32,
            )
        )
    for spot in spots:
        total = jnp.sum(functools.reduce(jnp.add, weights[spot]), axis=1, keepdims=True)
        totals[spot] = jnp.broadcast_to(total, (HD, HD))
    results = {}
    for head, place in spots:
        spot = (head, place)
        context, total = added[head][place * HD : (place + 1) * HD], totals[spot]
        if olds is not None:
            fade = jnp.exp2(olds[spot][0] - tops[spot])
            total = total + olds[spot][1] * fade
            context = context + olds[spot][2] * fade
        results[spot] = (tops[spot], total, context)
    return results


def held_state(context_ref, stats_ref, head, place):
    part, low, wide = slice(place * HD, (place + 1) * HD), head * HD, 2 * head * HD
    return (
        stats_ref[part, wide : wide + HD],
        stats_ref[part, wide + HD : wide + 2 * HD],
        context_ref[part, low : low + HD],
    )


def step_kernel(first, own_ref, remote_ref, bias_ref, pack_ref, *refs):
    olds, (context_out, stats_out) = refs[:-2], refs[-2:]
    heads, keys = own_ref.shape[1] // HD, pack_ref.shape[0] // 2
    left = first * HD
    biases = [bias_ref[8 * place : 8 * place + 1, left : left + keys] for place in range(2)]
    state = None
    if olds:
        state = {
            (head, place): held_state(*olds, head, place)
            for head in range(heads)
            for place in range(2)
        }
    queries = [
        jnp.concatenate([ref[:HD, head * HD : (head + 1) * HD] for ref in (own_ref, remote_ref)])
        for head in range(heads)
    ]
    for (head, place), result in absorb(queries, pack_ref, biases, state).items():
        part, low, wide = slice(place * HD, (place + 1) * HD), head * HD, 2 * head * HD
        top, total, context = result
        context_out[part, low : low + HD] = context
        stats_out[part, wide : wide + HD] = top
        stats_out[part, wide + HD : wide + 2 * HD] = total


def last_attention(place, query_ref, bias_ref, pack_ref, context_ref, stats_ref, *outs):
    heads, keys = query_ref.shape[1] // HD, pack_ref.shape[0] // 2
    part = slice(place * HD, (place + 1) * HD)
    bias = bias_ref[8 * place : 8 * place + 1, bias_ref.shape[1] - keys :]
    lane = lax.broadcasted_iota(jnp.int32, (1, HD), 1)
    state = {(h, 0): held_state(context_ref, stats_ref, h, place) for h in range(heads)}
    queries = [query_ref[:HD, head * HD : (head + 1) * HD] for head in range(heads)]
    results = absorb(queries, pack_ref, [bias], state)
    columns = jnp.zeros((HD, HD), jnp.float32)
    for head in range(heads):
        top, total, context = results[head, 0]
        outs[0][:HD, head * HD : (head + 1) * HD] = context.astype(outs[0].dtype)
        line = 2 * head
        columns = jnp.where(lane == line, top, jnp.where(lane == line + 1, total, columns))
    lines = columns.T
    sub = lax.broadcasted_iota(jnp.int32, (EXTRA, HD), 0)
    for head in range(heads):
        low = head * HD
        pair = (lines[2 * head : 2 * head + 1, :], lines[2 * head + 1 : 2 * head + 2, :])
        if place == 0:
            for row, value in enumerate(pair):
                outs[1][8 * row : 8 * row + 8, low : low + HD] = jnp.broadcast_to(value, (8, HD))
        else:
            piece_rows = jnp.zeros((EXTRA, HD), jnp.float32)
            for row, value in enumerate(pair):
                first = value.astype(jnp.bfloat16).astype(jnp.float32)
                second = (value - first).astype(jnp.bfloat16).astype(jnp.float32)
                for piece, part_value in enumerate((first, second, value - first - second)):
                    piece_rows = jnp.where(sub == 3 * row + piece, part_value, piece_rows)
            outs[0][HD:, low : low + HD] = piece_rows.astype(jnp.bfloat16)


def gate_kernel(step_ref, table_ref, out_ref):
    rows = out_ref.shape[0] // 2
    start = lax.axis_index("tm") * HD
    first = step_ref[start // FRAME_TOK]
    last = step_ref[(start + HD - 1) // FRAME_TOK]
    out_ref[:rows, :] = jnp.broadcast_to(table_ref[pl.ds(first, 1), :], (rows, out_ref.shape[1]))
    out_ref[rows:, :] = jnp.broadcast_to(table_ref[pl.ds(last, 1), :], (rows, out_ref.shape[1]))


def merge_kernel(own_ref, lines_ref, packet_ref, gate_ref, out_ref):
    rows, width = own_ref.shape
    pieces = packet_ref[rows:, :].astype(jnp.float32)
    own_top, own_total = lines_ref[0:1, :], lines_ref[8:9, :]
    other_top = pieces[0:1] + pieces[1:2] + pieces[2:3]
    other_total = pieces[3:4] + pieces[4:5] + pieces[5:6]
    top = jnp.maximum(own_top, other_top)
    own_share, other_share = jnp.exp2(own_top - top), jnp.exp2(other_top - top)
    scale = 1.0 / (own_total * own_share + other_total * other_share)
    own_share, other_share = own_share * scale, other_share * scale
    start = lax.axis_index("tm") * rows
    first_rows = (start // FRAME_TOK + 1) * FRAME_TOK - start
    row_ids = lax.broadcasted_iota(jnp.int32, (rows, 1), 0)
    for low in range(0, width, HD):
        high = low + HD
        context = own_ref[:, low:high] * spread(own_share[:, low:high])
        other = packet_ref[:rows, low:high].astype(jnp.float32)
        context += other * spread(other_share[:, low:high])
        gate = jnp.where(
            row_ids < first_rows, gate_ref[0:1, low:high], gate_ref[8:9, low:high]
        )
        out_ref[:, low:high] = (context * gate).astype(jnp.bfloat16)


def exchange(array, mask):
    count = lax.axis_size("tm")
    return lax.ppermute(array, "tm", [(i, i ^ mask) for i in range(count)])


def gathered(array, bits):
    held = {0: array}
    for bit in bits:
        for mask in list(held):
            held[mask ^ bit] = exchange(held[mask], bit)
    return held


def cost(flops):
    return pl.CostEstimate(flops=flops, bytes_accessed=0, transcendentals=0)


def local(
    query_proj, key_proj, value_proj, query_gain, key_gain, gate_table, frame_step, far_blocks
):
    rows, width = query_proj.shape
    count = lax.axis_size("tm")
    splits = lax.axis_size("head")
    full_width = width * splits
    params = pltpu.CompilerParams(vmem_limit_bytes=(8 + count // 2) * 2**20)
    query_mask = count // 4
    bits = [1 << place for place in range(1, count.bit_length() - 1)]
    bits = [bit for bit in bits[::-1] if bit != query_mask]
    query_gain = query_gain.reshape(1, width)
    key_gain = key_gain.reshape(1, width)

    far = bits[0]
    far_value = exchange(value_proj, far)
    sums = pl.pallas_call(
        sums_kernel,
        out_shape=jax.ShapeDtypeStruct((8, rows), jnp.float32),
        in_specs=[VMEM] * 2,
        out_specs=VMEM,
        compiler_params=params,
    )(query_proj, key_proj)
    if splits == 2:
        others = lax.ppermute(sums, "head", [(0, 1), (1, 0)])
    else:
        sums = lax.psum(sums, "head")
        others = jnp.zeros_like(sums)
    own_key = pl.pallas_call(
        functools.partial(key_kernel, width * splits),
        out_shape=jax.ShapeDtypeStruct((rows, width), jnp.bfloat16),
        in_specs=[VMEM] * 4,
        out_specs=VMEM,
        compiler_params=params,
    )(key_proj, key_gain, sums, others)
    query_packet, own_pair = pl.pallas_call(
        functools.partial(query_kernel, width * splits),
        out_shape=[
            jax.ShapeDtypeStruct((rows + EXTRA, width), jnp.bfloat16),
            jax.ShapeDtypeStruct((2 * rows, width), jnp.bfloat16),
        ],
        in_specs=[VMEM] * 7,
        out_specs=[VMEM] * 2,
        compiler_params=params,
    )(query_proj, own_key, value_proj, query_gain, far_blocks, sums, others)
    far_key = exchange(own_key, far)
    pairs = gathered(own_pair, bits[1:])
    queries = [query_packet, exchange(query_packet, query_mask)]
    far_value = pl.pallas_call(
        copy_kernel,
        out_shape=jax.ShapeDtypeStruct((rows, width), jnp.bfloat16),
        in_specs=[VMEM],
        out_specs=VMEM,
        compiler_params=params,
        cost_estimate=cost(4 * UNIT),
    )(far_value)
    late_keys, late_values = gathered(far_key, bits[1:]), gathered(far_value, bits[1:])
    early = [0, far] + sorted(mask for mask in pairs if mask)
    late = sorted(mask ^ far for mask in late_keys if mask)
    early_masks = early + [mask ^ 1 for mask in early]
    all_masks = early_masks + late + [mask ^ 1 for mask in late]
    biases = pl.pallas_call(
        functools.partial(bias_kernel, all_masks),
        out_shape=jax.ShapeDtypeStruct((16, len(all_masks) * HD), jnp.float32),
        in_specs=[VMEM] * 2,
        out_specs=VMEM,
        compiler_params=params,
    )(*queries)

    def packed(keys, values, flops, *after):
        held = len(keys)
        return pl.pallas_call(
            functools.partial(pack_kernel, held),
            out_shape=jax.ShapeDtypeStruct((2 * held * rows, width), jnp.bfloat16),
            in_specs=[VMEM] * (2 * held + len(after)),
            out_specs=VMEM,
            compiler_params=params,
            cost_estimate=cost(flops),
        )(*keys, *values, *after)

    near = [pairs[mask] for mask in early if mask != far]
    early_pack = packed([near[0], far_key, *near[1:]], [near[0], far_value, *near[1:]], 0)

    def step(first, pack, *state):
        return pl.pallas_call(
            functools.partial(step_kernel, first),
            out_shape=[
                jax.ShapeDtypeStruct((2 * rows, width), jnp.float32),
                jax.ShapeDtypeStruct((2 * rows, 2 * width), jnp.float32),
            ],
            in_specs=[VMEM] * (4 + len(state)),
            out_specs=[VMEM] * 2,
            compiler_params=params,
        )(*queries, biases, pack, *state)

    state = step(0, early_pack)
    late_pack = packed(
        [late_keys[mask ^ far] for mask in late],
        [late_values[mask ^ far] for mask in late],
        12 * UNIT,
        state[1],
    )
    state = step(len(early), exchange(early_pack, 1), *state)
    state = step(2 * len(early), late_pack, *state)
    last_pack = exchange(late_pack, 1)

    def last(place, out_shape):
        return pl.pallas_call(
            functools.partial(last_attention, place),
            out_shape=out_shape,
            in_specs=[VMEM] * 5,
            out_specs=[VMEM] * len(out_shape),
            compiler_params=params,
        )(queries[place], biases, last_pack, *state)

    (packet,) = last(1, [jax.ShapeDtypeStruct((rows + EXTRA, width), jnp.bfloat16)])
    own, own_lines = last(
        0,
        [
            jax.ShapeDtypeStruct((rows, width), jnp.float32),
            jax.ShapeDtypeStruct((16, width), jnp.float32),
        ],
    )
    gates = pl.pallas_call(
        gate_kernel,
        out_shape=jax.ShapeDtypeStruct((16, width), jnp.float32),
        in_specs=[SMEM, VMEM],
        out_specs=VMEM,
        compiler_params=params,
    )(frame_step, gate_table)
    packet = exchange(packet, query_mask)

    return pl.pallas_call(
        merge_kernel,
        out_shape=jax.ShapeDtypeStruct((rows, width), jnp.bfloat16),
        in_specs=[VMEM] * 4,
        out_specs=VMEM,
        compiler_params=params,
    )(own, own_lines, packet, gates)


def solution(mesh):
    return jax.shard_map(
        local,
        mesh=mesh,
        in_specs=(
            P("tm", "head"),
            P("tm", "head"),
            P("tm", "head"),
            P("head"),
            P("head"),
            P(None, "head"),
            P(),
            P("tm", None),
        ),
        out_specs=P("tm", "head"),
        check_vma=False,
    )
```

```python
import functools

import jax
import jax.numpy as jnp
from jax import lax
from jax.experimental import pallas as pl
from jax.experimental.pallas import tpu as pltpu
from jax.sharding import PartitionSpec as P

HD = 128
BLK = 64
FRAME_TOK = 1560
EPSILON = 1e-06
LOG2E = 1.4426950408889634
SCALE = HD ** (-0.5) * LOG2E
MASKED = -1e30
EXTRA = 16
UNIT = 10**9
ANY = pl.BlockSpec(memory_space=pl.ANY)
VMEM = pl.BlockSpec(memory_space=pltpu.VMEM)
SMEM = pl.BlockSpec(memory_space=pltpu.SMEM)


def spread(row):
    return jnp.broadcast_to(row, (row.shape[1], row.shape[1])).T


def squares(source_ref):
    wide = source_ref[:HD, :].astype(jnp.float32)
    square = wide * wide
    part = square[:, :HD]
    for low in range(HD, square.shape[1], HD):
        part = part + square[:, low : low + HD]
    return jnp.sum(part.T, axis=0, keepdims=True)


def sums_kernel(query_ref, key_ref, out_ref):
    out_ref[...] = jnp.zeros_like(out_ref)
    out_ref[0:1, :] = squares(query_ref)
    out_ref[1:2, :] = squares(key_ref)


def factor_of(line, full_width):
    return spread(lax.rsqrt(line / full_width + EPSILON))


def normed(source_ref, factor, gain_ref):
    parts = []
    for low in range(0, source_ref.shape[1], HD):
        wide = source_ref[:HD, low : low + HD].astype(jnp.float32)
        parts.append((wide * factor * gain_ref[:, low : low + HD]).astype(jnp.bfloat16))
    return jnp.concatenate(parts, axis=1)


def key_kernel(full_width, key_ref, gain_ref, own_ref, other_ref, out_ref):
    total = own_ref[1:2, :] + other_ref[1:2, :]
    out_ref[...] = normed(key_ref, factor_of(total, full_width), gain_ref)


def query_kernel(
    full_width,
    query_ref,
    gain_ref,
    far_ref,
    own_ref,
    other_ref,
    query_out,
):
    total = own_ref[0:1, :] + other_ref[0:1, :]
    query_out[:HD, :] = normed(query_ref, factor_of(total, full_width), gain_ref)
    far = far_ref[...].astype(jnp.float32)
    far = jnp.concatenate([far, jnp.full((1, HD - far.shape[1]), -1.0)], axis=1)
    query_out[HD:, :HD] = jnp.broadcast_to(far, (EXTRA, HD)).astype(jnp.bfloat16)
    query_out[HD:, HD:] = jnp.zeros((EXTRA, query_out.shape[1] - HD), jnp.bfloat16)


def bias_kernel(key_masks, own_ref, remote_ref, bias_out):
    me = lax.axis_index("tm")
    query_mask = lax.axis_size("tm") // 4
    lane = lax.broadcasted_iota(jnp.int32, (1, HD), 1)
    half = (lane >= BLK).astype(jnp.float32)
    for place, query_ref in enumerate((own_ref, remote_ref)):
        far = query_ref[HD:, :HD].astype(jnp.float32)[:1]
        query_id = me ^ (place * query_mask)
        for block, key_mask in enumerate(key_masks):
            key_id = me ^ key_mask
            choice = jnp.sum(jnp.where(lane == key_id, far, 0.0), axis=1, keepdims=True)
            taken = (choice == half) | (jnp.abs(query_id - key_id) <= 1)
            bias_out[8 * place : 8 * place + 8, block * HD : (block + 1) * HD] = (
                jnp.broadcast_to(jnp.where(taken, 0.0, MASKED), (8, HD))
            )


def copy_kernel(source_ref, out_ref):
    out_ref[...] = source_ref[...]


def pack_kernel(held, *refs):
    for place, source_ref in enumerate(refs[: 2 * held]):
        refs[-1][place * HD : (place + 1) * HD, :] = source_ref[...]


def absorb(queries, pack_ref, biases, olds):
    half = pack_ref.shape[0] // 2
    heads, count = len(queries), len(biases)
    scores = []
    for head, query in enumerate(queries):
        scores.append(
            lax.dot_general(
                query,
                pack_ref[:half, head * HD : (head + 1) * HD],
                (((1,), (1,)), ((), ())),
                preferred_element_type=jnp.float32,
            )
        )
    spots = [(head, place) for head in range(heads) for place in range(count)]
    logits, tops, weights, totals = {}, {}, {}, {}
    for head, place in spots:
        part = scores[head][place * HD : (place + 1) * HD]
        logits[head, place] = part * SCALE + biases[place]
    for spot in spots:
        top = jnp.broadcast_to(jnp.max(logits[spot], axis=1, keepdims=True), (HD, HD))
        tops[spot] = top if olds is None else jnp.maximum(top, olds[spot][0])
    for spot in spots:
        weights[spot] = [
            jnp.exp2(logits[spot][:, left : left + HD] - tops[spot])
            for left in range(0, half, HD)
        ]
    added = []
    for head in range(heads):
        rounded = [
            jnp.concatenate([w.astype(jnp.bfloat16) for w in weights[head, place]], axis=1)
            for place in range(count)
        ]
        added.append(
            jnp.dot(
                jnp.concatenate(rounded, axis=0),
                pack_ref[half:, head * HD : (head + 1) * HD],
                preferred_element_type=jnp.float32,
            )
        )
    for spot in spots:
        total = jnp.sum(functools.reduce(jnp.add, weights[spot]), axis=1, keepdims=True)
        totals[spot] = jnp.broadcast_to(total, (HD, HD))
    results = {}
    for head, place in spots:
        spot = (head, place)
        context, total = added[head][place * HD : (place + 1) * HD], totals[spot]
        if olds is not None:
            fade = jnp.exp2(olds[spot][0] - tops[spot])
            total = total + olds[spot][1] * fade
            context = context + olds[spot][2] * fade
        results[spot] = (tops[spot], total, context)
    return results


def held_state(context_ref, stats_ref, head, place):
    part, low, wide = slice(place * HD, (place + 1) * HD), head * HD, 2 * head * HD
    return (
        stats_ref[part, wide : wide + HD],
        stats_ref[part, wide + HD : wide + 2 * HD],
        context_ref[part, low : low + HD],
    )


def step_kernel(first, own_ref, remote_ref, bias_ref, pack_ref, *refs):
    olds, (context_out, stats_out) = refs[:-2], refs[-2:]
    heads, keys = own_ref.shape[1] // HD, pack_ref.shape[0] // 2
    left = first * HD
    biases = [bias_ref[8 * place : 8 * place + 1, left : left + keys] for place in range(2)]
    state = None
    if olds:
        state = {
            (head, place): held_state(*olds, head, place)
            for head in range(heads)
            for place in range(2)
        }
    queries = [
        jnp.concatenate([ref[:HD, head * HD : (head + 1) * HD] for ref in (own_ref, remote_ref)])
        for head in range(heads)
    ]
    for (head, place), result in absorb(queries, pack_ref, biases, state).items():
        part, low, wide = slice(place * HD, (place + 1) * HD), head * HD, 2 * head * HD
        top, total, context = result
        context_out[part, low : low + HD] = context
        stats_out[part, wide : wide + HD] = top
        stats_out[part, wide + HD : wide + 2 * HD] = total


def last_attention(place, query_ref, bias_ref, pack_ref, context_ref, stats_ref, *outs):
    heads, keys = query_ref.shape[1] // HD, pack_ref.shape[0] // 2
    part = slice(place * HD, (place + 1) * HD)
    bias = bias_ref[8 * place : 8 * place + 1, bias_ref.shape[1] - keys :]
    lane = lax.broadcasted_iota(jnp.int32, (1, HD), 1)
    state = {(h, 0): held_state(context_ref, stats_ref, h, place) for h in range(heads)}
    queries = [query_ref[:HD, head * HD : (head + 1) * HD] for head in range(heads)]
    results = absorb(queries, pack_ref, [bias], state)
    columns = jnp.zeros((HD, HD), jnp.float32)
    for head in range(heads):
        top, total, context = results[head, 0]
        outs[0][:HD, head * HD : (head + 1) * HD] = context.astype(outs[0].dtype)
        line = 2 * head
        columns = jnp.where(lane == line, top, jnp.where(lane == line + 1, total, columns))
    lines = columns.T
    sub = lax.broadcasted_iota(jnp.int32, (EXTRA, HD), 0)
    for head in range(heads):
        low = head * HD
        pair = (lines[2 * head : 2 * head + 1, :], lines[2 * head + 1 : 2 * head + 2, :])
        if place == 0:
            for row, value in enumerate(pair):
                outs[1][8 * row : 8 * row + 8, low : low + HD] = jnp.broadcast_to(value, (8, HD))
        else:
            piece_rows = jnp.zeros((EXTRA, HD), jnp.float32)
            for row, value in enumerate(pair):
                first = value.astype(jnp.bfloat16).astype(jnp.float32)
                second = (value - first).astype(jnp.bfloat16).astype(jnp.float32)
                for piece, part_value in enumerate((first, second, value - first - second)):
                    piece_rows = jnp.where(sub == 3 * row + piece, part_value, piece_rows)
            outs[0][HD:, low : low + HD] = piece_rows.astype(jnp.bfloat16)


def gate_kernel(step_ref, table_ref, out_ref):
    rows = out_ref.shape[0] // 2
    start = lax.axis_index("tm") * HD
    first = step_ref[start // FRAME_TOK]
    last = step_ref[(start + HD - 1) // FRAME_TOK]
    out_ref[:rows, :] = jnp.broadcast_to(table_ref[pl.ds(first, 1), :], (rows, out_ref.shape[1]))
    out_ref[rows:, :] = jnp.broadcast_to(table_ref[pl.ds(last, 1), :], (rows, out_ref.shape[1]))


def merge_kernel(own_ref, lines_ref, packet_ref, gate_ref, out_ref):
    rows, width = own_ref.shape
    pieces = packet_ref[rows:, :].astype(jnp.float32)
    own_top, own_total = lines_ref[0:1, :], lines_ref[8:9, :]
    other_top = pieces[0:1] + pieces[1:2] + pieces[2:3]
    other_total = pieces[3:4] + pieces[4:5] + pieces[5:6]
    top = jnp.maximum(own_top, other_top)
    own_share, other_share = jnp.exp2(own_top - top), jnp.exp2(other_top - top)
    scale = 1.0 / (own_total * own_share + other_total * other_share)
    own_share, other_share = own_share * scale, other_share * scale
    start = lax.axis_index("tm") * rows
    first_rows = (start // FRAME_TOK + 1) * FRAME_TOK - start
    row_ids = lax.broadcasted_iota(jnp.int32, (rows, 1), 0)
    for low in range(0, width, HD):
        high = low + HD
        context = own_ref[:, low:high] * spread(own_share[:, low:high])
        other = packet_ref[:rows, low:high].astype(jnp.float32)
        context += other * spread(other_share[:, low:high])
        gate = jnp.where(
            row_ids < first_rows, gate_ref[0:1, low:high], gate_ref[8:9, low:high]
        )
        out_ref[:, low:high] = (context * gate).astype(jnp.bfloat16)


def exchange(array, mask):
    count = lax.axis_size("tm")
    return lax.ppermute(array, "tm", [(i, i ^ mask) for i in range(count)])


def gathered(array, bits):
    held = {0: array}
    for bit in bits:
        for mask in list(held):
            held[mask ^ bit] = exchange(held[mask], bit)
    return held


def cost(flops):
    return pl.CostEstimate(flops=flops, bytes_accessed=0, transcendentals=0)


def local(
    query_proj, key_proj, value_proj, query_gain, key_gain, gate_table, frame_step, far_blocks
):
    rows, width = query_proj.shape
    count = lax.axis_size("tm")
    splits = lax.axis_size("head")
    full_width = width * splits
    params = pltpu.CompilerParams(vmem_limit_bytes=(8 + count // 2) * 2**20)
    query_mask = count // 4
    bits = [1 << place for place in range(1, count.bit_length() - 1)]
    bits = [bit for bit in bits[::-1] if bit != query_mask]
    query_gain = query_gain.reshape(1, width)
    key_gain = key_gain.reshape(1, width)

    far = bits[0]
    far_value = exchange(value_proj, far)
    sums = pl.pallas_call(
        sums_kernel,
        out_shape=jax.ShapeDtypeStruct((8, rows), jnp.float32),
        in_specs=[VMEM] * 2,
        out_specs=VMEM,
        compiler_params=params,
    )(query_proj, key_proj)
    if splits == 2:
        others = lax.ppermute(sums, "head", [(0, 1), (1, 0)])
    else:
        sums = lax.psum(sums, "head")
        others = jnp.zeros_like(sums)
    own_key = pl.pallas_call(
        functools.partial(key_kernel, width * splits),
        out_shape=jax.ShapeDtypeStruct((rows, width), jnp.bfloat16),
        in_specs=[VMEM] * 4,
        out_specs=VMEM,
        compiler_params=params,
    )(key_proj, key_gain, sums, others)
    near_values = gathered(value_proj, bits[1:])
    near_keys = gathered(own_key, bits[1:])
    query_packet = pl.pallas_call(
        functools.partial(query_kernel, width * splits),
        out_shape=jax.ShapeDtypeStruct((rows + EXTRA, width), jnp.bfloat16),
        in_specs=[VMEM] * 5,
        out_specs=VMEM,
        compiler_params=params,
    )(query_proj, query_gain, far_blocks, sums, others)
    far_key = exchange(own_key, far)
    queries = [query_packet, exchange(query_packet, query_mask)]
    far_value = pl.pallas_call(
        copy_kernel,
        out_shape=jax.ShapeDtypeStruct((rows, width), jnp.bfloat16),
        in_specs=[VMEM],
        out_specs=VMEM,
        compiler_params=params,
        cost_estimate=cost(4 * UNIT),
    )(far_value)
    late_keys, late_values = gathered(far_key, bits[1:]), gathered(far_value, bits[1:])
    early = [0, far] + sorted(mask for mask in near_keys if mask)
    late = sorted(mask ^ far for mask in late_keys if mask)
    early_masks = early + [mask ^ 1 for mask in early]
    all_masks = early_masks + late + [mask ^ 1 for mask in late]
    biases = pl.pallas_call(
        functools.partial(bias_kernel, all_masks),
        out_shape=jax.ShapeDtypeStruct((16, len(all_masks) * HD), jnp.float32),
        in_specs=[VMEM] * 2,
        out_specs=VMEM,
        compiler_params=params,
    )(*queries)

    def packed(keys, values, flops, *after):
        held = len(keys)
        return pl.pallas_call(
            functools.partial(pack_kernel, held),
            out_shape=jax.ShapeDtypeStruct((2 * held * rows, width), jnp.bfloat16),
            in_specs=[VMEM] * (2 * held + len(after)),
            out_specs=VMEM,
            compiler_params=params,
            cost_estimate=cost(flops),
        )(*keys, *values, *after)

    near_keys[far], near_values[far] = far_key, far_value
    early_pack = packed(
        [near_keys[mask] for mask in early], [near_values[mask] for mask in early], 0
    )

    def step(first, pack, *state):
        return pl.pallas_call(
            functools.partial(step_kernel, first),
            out_shape=[
                jax.ShapeDtypeStruct((2 * rows, width), jnp.float32),
                jax.ShapeDtypeStruct((2 * rows, 2 * width), jnp.float32),
            ],
            in_specs=[VMEM] * (4 + len(state)),
            out_specs=[VMEM] * 2,
            compiler_params=params,
        )(*queries, biases, pack, *state)

    state = step(0, early_pack)
    late_pack = packed(
        [late_keys[mask ^ far] for mask in late],
        [late_values[mask ^ far] for mask in late],
        12 * UNIT,
        state[1],
    )
    state = step(len(early), exchange(early_pack, 1), *state)
    state = step(2 * len(early), late_pack, *state)
    last_pack = exchange(late_pack, 1)

    def last(place, out_shape):
        return pl.pallas_call(
            functools.partial(last_attention, place),
            out_shape=out_shape,
            in_specs=[VMEM] * 5,
            out_specs=[VMEM] * len(out_shape),
            compiler_params=params,
        )(queries[place], biases, last_pack, *state)

    (packet,) = last(1, [jax.ShapeDtypeStruct((rows + EXTRA, width), jnp.bfloat16)])
    own, own_lines = last(
        0,
        [
            jax.ShapeDtypeStruct((rows, width), jnp.float32),
            jax.ShapeDtypeStruct((16, width), jnp.float32),
        ],
    )
    gates = pl.pallas_call(
        gate_kernel,
        out_shape=jax.ShapeDtypeStruct((16, width), jnp.float32),
        in_specs=[SMEM, VMEM],
        out_specs=VMEM,
        compiler_params=params,
    )(frame_step, gate_table)
    packet = exchange(packet, query_mask)

    return pl.pallas_call(
        merge_kernel,
        out_shape=jax.ShapeDtypeStruct((rows, width), jnp.bfloat16),
        in_specs=[VMEM] * 4,
        out_specs=VMEM,
        compiler_params=params,
    )(own, own_lines, packet, gates)


def solution(mesh):
    return jax.shard_map(
        local,
        mesh=mesh,
        in_specs=(
            P("tm", "head"),
            P("tm", "head"),
            P("tm", "head"),
            P("head"),
            P("head"),
            P(None, "head"),
            P(),
            P("tm", None),
        ),
        out_specs=P("tm", "head"),
        check_vma=False,
    )
```

```python
import functools

import jax
import jax.numpy as jnp
from jax import lax
from jax.experimental import pallas as pl
from jax.experimental.pallas import tpu as pltpu
from jax.sharding import PartitionSpec as P

HD = 128
BLK = 64
FRAME_TOK = 1560
EPSILON = 1e-06
LOG2E = 1.4426950408889634
SCALE = HD ** (-0.5) * LOG2E
MASKED = -1e30
EXTRA = 16
UNIT = 10**9
ANY = pl.BlockSpec(memory_space=pl.ANY)
VMEM = pl.BlockSpec(memory_space=pltpu.VMEM)
SMEM = pl.BlockSpec(memory_space=pltpu.SMEM)


def spread(row):
    return jnp.broadcast_to(row, (row.shape[1], row.shape[1])).T


def squares(source_ref):
    wide = source_ref[:HD, :].astype(jnp.float32)
    square = wide * wide
    part = square[:, :HD]
    for low in range(HD, square.shape[1], HD):
        part = part + square[:, low : low + HD]
    return jnp.sum(part.T, axis=0, keepdims=True)


def sums_kernel(query_ref, key_ref, out_ref):
    out_ref[...] = jnp.zeros_like(out_ref)
    out_ref[0:1, :] = squares(query_ref)
    out_ref[1:2, :] = squares(key_ref)


def factor_of(line, full_width):
    return spread(lax.rsqrt(line / full_width + EPSILON))


def normed(source_ref, factor, gain_ref):
    parts = []
    for low in range(0, source_ref.shape[1], HD):
        wide = source_ref[:HD, low : low + HD].astype(jnp.float32)
        parts.append((wide * factor * gain_ref[:, low : low + HD]).astype(jnp.bfloat16))
    return jnp.concatenate(parts, axis=1)


def key_kernel(full_width, key_ref, gain_ref, own_ref, other_ref, out_ref):
    total = own_ref[1:2, :] + other_ref[1:2, :]
    out_ref[...] = normed(key_ref, factor_of(total, full_width), gain_ref)


def query_kernel(
    full_width,
    query_ref,
    gain_ref,
    far_ref,
    own_ref,
    other_ref,
    query_out,
):
    total = own_ref[0:1, :] + other_ref[0:1, :]
    query_out[:HD, :] = normed(query_ref, factor_of(total, full_width), gain_ref)
    far = far_ref[...].astype(jnp.float32)
    far = jnp.concatenate([far, jnp.full((1, HD - far.shape[1]), -1.0)], axis=1)
    query_out[HD:, :HD] = jnp.broadcast_to(far, (EXTRA, HD)).astype(jnp.bfloat16)
    query_out[HD:, HD:] = jnp.zeros((EXTRA, query_out.shape[1] - HD), jnp.bfloat16)


def bias_kernel(key_masks, own_ref, remote_ref, bias_out):
    me = lax.axis_index("tm")
    query_mask = lax.axis_size("tm") // 4
    lane = lax.broadcasted_iota(jnp.int32, (1, HD), 1)
    half = (lane >= BLK).astype(jnp.float32)
    for place, query_ref in enumerate((own_ref, remote_ref)):
        far = query_ref[HD:, :HD].astype(jnp.float32)[:1]
        query_id = me ^ (place * query_mask)
        for block, key_mask in enumerate(key_masks):
            key_id = me ^ key_mask
            choice = jnp.sum(jnp.where(lane == key_id, far, 0.0), axis=1, keepdims=True)
            taken = (choice == half) | (jnp.abs(query_id - key_id) <= 1)
            bias_out[8 * place : 8 * place + 8, block * HD : (block + 1) * HD] = (
                jnp.broadcast_to(jnp.where(taken, 0.0, MASKED), (8, HD))
            )


def copy_kernel(source_ref, out_ref):
    out_ref[...] = source_ref[...]


def pack_kernel(held, *refs):
    for place, source_ref in enumerate(refs[: 2 * held]):
        refs[-1][place * HD : (place + 1) * HD, :] = source_ref[...]


def absorb(queries, pack_ref, biases, olds):
    half = pack_ref.shape[0] // 2
    heads, count = len(queries), len(biases)
    scores = []
    for head, query in enumerate(queries):
        scores.append(
            lax.dot_general(
                query,
                pack_ref[:half, head * HD : (head + 1) * HD],
                (((1,), (1,)), ((), ())),
                preferred_element_type=jnp.float32,
            )
        )
    spots = [(head, place) for head in range(heads) for place in range(count)]
    logits, tops, weights, totals = {}, {}, {}, {}
    for head, place in spots:
        part = scores[head][place * HD : (place + 1) * HD]
        logits[head, place] = part * SCALE + biases[place]
    for spot in spots:
        top = jnp.broadcast_to(jnp.max(logits[spot], axis=1, keepdims=True), (HD, HD))
        tops[spot] = top if olds is None else jnp.maximum(top, olds[spot][0])
    for spot in spots:
        weights[spot] = [
            jnp.exp2(logits[spot][:, left : left + HD] - tops[spot])
            for left in range(0, half, HD)
        ]
    added = []
    for head in range(heads):
        rounded = [
            jnp.concatenate([w.astype(jnp.bfloat16) for w in weights[head, place]], axis=1)
            for place in range(count)
        ]
        added.append(
            jnp.dot(
                jnp.concatenate(rounded, axis=0),
                pack_ref[half:, head * HD : (head + 1) * HD],
                preferred_element_type=jnp.float32,
            )
        )
    for spot in spots:
        total = jnp.sum(functools.reduce(jnp.add, weights[spot]), axis=1, keepdims=True)
        totals[spot] = jnp.broadcast_to(total, (HD, HD))
    results = {}
    for head, place in spots:
        spot = (head, place)
        context, total = added[head][place * HD : (place + 1) * HD], totals[spot]
        if olds is not None:
            fade = jnp.exp2(olds[spot][0] - tops[spot])
            total = total + olds[spot][1] * fade
            context = context + olds[spot][2] * fade
        results[spot] = (tops[spot], total, context)
    return results


def held_state(context_ref, stats_ref, head, place):
    part, low, wide = slice(place * HD, (place + 1) * HD), head * HD, 2 * head * HD
    return (
        stats_ref[part, wide : wide + HD],
        stats_ref[part, wide + HD : wide + 2 * HD],
        context_ref[part, low : low + HD],
    )


def step_kernel(first, own_ref, remote_ref, bias_ref, pack_ref, *refs):
    olds, (context_out, stats_out) = refs[:-2], refs[-2:]
    heads, keys = own_ref.shape[1] // HD, pack_ref.shape[0] // 2
    left = first * HD
    biases = [bias_ref[8 * place : 8 * place + 1, left : left + keys] for place in range(2)]
    state = None
    if olds:
        state = {
            (head, place): held_state(*olds, head, place)
            for head in range(heads)
            for place in range(2)
        }
    queries = [
        jnp.concatenate([ref[:HD, head * HD : (head + 1) * HD] for ref in (own_ref, remote_ref)])
        for head in range(heads)
    ]
    for (head, place), result in absorb(queries, pack_ref, biases, state).items():
        part, low, wide = slice(place * HD, (place + 1) * HD), head * HD, 2 * head * HD
        top, total, context = result
        context_out[part, low : low + HD] = context
        stats_out[part, wide : wide + HD] = top
        stats_out[part, wide + HD : wide + 2 * HD] = total


def last_attention(place, query_ref, bias_ref, pack_ref, context_ref, stats_ref, *outs):
    heads, keys = query_ref.shape[1] // HD, pack_ref.shape[0] // 2
    part = slice(place * HD, (place + 1) * HD)
    bias = bias_ref[8 * place : 8 * place + 1, bias_ref.shape[1] - keys :]
    lane = lax.broadcasted_iota(jnp.int32, (1, HD), 1)
    state = {(h, 0): held_state(context_ref, stats_ref, h, place) for h in range(heads)}
    queries = [query_ref[:HD, head * HD : (head + 1) * HD] for head in range(heads)]
    results = absorb(queries, pack_ref, [bias], state)
    columns = jnp.zeros((HD, HD), jnp.float32)
    for head in range(heads):
        top, total, context = results[head, 0]
        outs[0][:HD, head * HD : (head + 1) * HD] = context.astype(outs[0].dtype)
        line = 2 * head
        columns = jnp.where(lane == line, top, jnp.where(lane == line + 1, total, columns))
    lines = columns.T
    sub = lax.broadcasted_iota(jnp.int32, (EXTRA, HD), 0)
    for head in range(heads):
        low = head * HD
        pair = (lines[2 * head : 2 * head + 1, :], lines[2 * head + 1 : 2 * head + 2, :])
        if place == 0:
            for row, value in enumerate(pair):
                outs[1][8 * row : 8 * row + 8, low : low + HD] = jnp.broadcast_to(value, (8, HD))
        else:
            piece_rows = jnp.zeros((EXTRA, HD), jnp.float32)
            for row, value in enumerate(pair):
                first = value.astype(jnp.bfloat16).astype(jnp.float32)
                second = (value - first).astype(jnp.bfloat16).astype(jnp.float32)
                for piece, part_value in enumerate((first, second, value - first - second)):
                    piece_rows = jnp.where(sub == 3 * row + piece, part_value, piece_rows)
            outs[0][HD:, low : low + HD] = piece_rows.astype(jnp.bfloat16)


def gate_kernel(step_ref, table_ref, out_ref):
    rows = out_ref.shape[0] // 2
    start = lax.axis_index("tm") * HD
    first = step_ref[start // FRAME_TOK]
    last = step_ref[(start + HD - 1) // FRAME_TOK]
    out_ref[:rows, :] = jnp.broadcast_to(table_ref[pl.ds(first, 1), :], (rows, out_ref.shape[1]))
    out_ref[rows:, :] = jnp.broadcast_to(table_ref[pl.ds(last, 1), :], (rows, out_ref.shape[1]))


def merge_kernel(own_ref, lines_ref, packet_ref, gate_ref, out_ref):
    rows, width = own_ref.shape
    pieces = packet_ref[rows:, :].astype(jnp.float32)
    own_top, own_total = lines_ref[0:1, :], lines_ref[8:9, :]
    other_top = pieces[0:1] + pieces[1:2] + pieces[2:3]
    other_total = pieces[3:4] + pieces[4:5] + pieces[5:6]
    top = jnp.maximum(own_top, other_top)
    own_share, other_share = jnp.exp2(own_top - top), jnp.exp2(other_top - top)
    scale = 1.0 / (own_total * own_share + other_total * other_share)
    own_share, other_share = own_share * scale, other_share * scale
    start = lax.axis_index("tm") * rows
    first_rows = (start // FRAME_TOK + 1) * FRAME_TOK - start
    row_ids = lax.broadcasted_iota(jnp.int32, (rows, 1), 0)
    for low in range(0, width, HD):
        high = low + HD
        context = own_ref[:, low:high] * spread(own_share[:, low:high])
        other = packet_ref[:rows, low:high].astype(jnp.float32)
        context += other * spread(other_share[:, low:high])
        gate = jnp.where(
            row_ids < first_rows, gate_ref[0:1, low:high], gate_ref[8:9, low:high]
        )
        out_ref[:, low:high] = (context * gate).astype(jnp.bfloat16)


def exchange(array, mask):
    count = lax.axis_size("tm")
    return lax.ppermute(array, "tm", [(i, i ^ mask) for i in range(count)])


def gathered(array, bits):
    held = {0: array}
    for bit in bits:
        for mask in list(held):
            held[mask ^ bit] = exchange(held[mask], bit)
    return held


def cost(flops):
    return pl.CostEstimate(flops=flops, bytes_accessed=0, transcendentals=0)


def local(
    query_proj, key_proj, value_proj, query_gain, key_gain, gate_table, frame_step, far_blocks
):
    rows, width = query_proj.shape
    count = lax.axis_size("tm")
    splits = lax.axis_size("head")
    full_width = width * splits
    params = pltpu.CompilerParams(vmem_limit_bytes=(8 + count // 2) * 2**20)
    query_mask = count // 4
    bits = [1 << place for place in range(1, count.bit_length() - 1)]
    bits = [bit for bit in bits[::-1] if bit != query_mask]
    query_gain = query_gain.reshape(1, width)
    key_gain = key_gain.reshape(1, width)

    far = bits[0]
    far_value = exchange(value_proj, far)
    sums = pl.pallas_call(
        sums_kernel,
        out_shape=jax.ShapeDtypeStruct((8, rows), jnp.float32),
        in_specs=[VMEM] * 2,
        out_specs=VMEM,
        compiler_params=params,
    )(query_proj, key_proj)
    if splits == 2:
        others = lax.ppermute(sums, "head", [(0, 1), (1, 0)])
    else:
        sums = lax.psum(sums, "head")
        others = jnp.zeros_like(sums)
    own_key = pl.pallas_call(
        functools.partial(key_kernel, width * splits),
        out_shape=jax.ShapeDtypeStruct((rows, width), jnp.bfloat16),
        in_specs=[VMEM] * 4,
        out_specs=VMEM,
        compiler_params=params,
    )(key_proj, key_gain, sums, others)
    near_values = gathered(value_proj, bits[1:])
    near_keys = gathered(own_key, bits[1:])
    query_packet = pl.pallas_call(
        functools.partial(query_kernel, width * splits),
        out_shape=jax.ShapeDtypeStruct((rows + EXTRA, width), jnp.bfloat16),
        in_specs=[VMEM] * 5,
        out_specs=VMEM,
        compiler_params=params,
        cost_estimate=cost(4 * UNIT),
    )(query_proj, query_gain, far_blocks, sums, others)
    far_key = exchange(own_key, far)
    queries = [query_packet, exchange(query_packet, query_mask)]
    far_value = pl.pallas_call(
        copy_kernel,
        out_shape=jax.ShapeDtypeStruct((rows, width), jnp.bfloat16),
        in_specs=[VMEM],
        out_specs=VMEM,
        compiler_params=params,
        cost_estimate=cost(4 * UNIT),
    )(far_value)
    late_keys, late_values = gathered(far_key, bits[1:]), gathered(far_value, bits[1:])
    early = [0, far] + sorted(mask for mask in near_keys if mask)
    late = sorted(mask ^ far for mask in late_keys if mask)
    early_masks = early + [mask ^ 1 for mask in early]
    all_masks = early_masks + late + [mask ^ 1 for mask in late]
    biases = pl.pallas_call(
        functools.partial(bias_kernel, all_masks),
        out_shape=jax.ShapeDtypeStruct((16, len(all_masks) * HD), jnp.float32),
        in_specs=[VMEM] * 2,
        out_specs=VMEM,
        compiler_params=params,
    )(*queries)

    def packed(keys, values, flops, *after):
        held = len(keys)
        return pl.pallas_call(
            functools.partial(pack_kernel, held),
            out_shape=jax.ShapeDtypeStruct((2 * held * rows, width), jnp.bfloat16),
            in_specs=[VMEM] * (2 * held + len(after)),
            out_specs=VMEM,
            compiler_params=params,
            cost_estimate=cost(flops),
        )(*keys, *values, *after)

    near_keys[far], near_values[far] = far_key, far_value
    early_pack = packed(
        [near_keys[mask] for mask in early], [near_values[mask] for mask in early], 4 * UNIT
    )

    def step(first, pack, *state):
        return pl.pallas_call(
            functools.partial(step_kernel, first),
            out_shape=[
                jax.ShapeDtypeStruct((2 * rows, width), jnp.float32),
                jax.ShapeDtypeStruct((2 * rows, 2 * width), jnp.float32),
            ],
            in_specs=[VMEM] * (4 + len(state)),
            out_specs=[VMEM] * 2,
            compiler_params=params,
        )(*queries, biases, pack, *state)

    state = step(0, early_pack)
    late_pack = packed(
        [late_keys[mask ^ far] for mask in late],
        [late_values[mask ^ far] for mask in late],
        12 * UNIT,
        state[1],
    )
    state = step(len(early), exchange(early_pack, 1), *state)
    state = step(2 * len(early), late_pack, *state)
    last_pack = exchange(late_pack, 1)

    def last(place, out_shape):
        return pl.pallas_call(
            functools.partial(last_attention, place),
            out_shape=out_shape,
            in_specs=[VMEM] * 5,
            out_specs=[VMEM] * len(out_shape),
            compiler_params=params,
        )(queries[place], biases, last_pack, *state)

    (packet,) = last(1, [jax.ShapeDtypeStruct((rows + EXTRA, width), jnp.bfloat16)])
    own, own_lines = last(
        0,
        [
            jax.ShapeDtypeStruct((rows, width), jnp.float32),
            jax.ShapeDtypeStruct((16, width), jnp.float32),
        ],
    )
    gates = pl.pallas_call(
        gate_kernel,
        out_shape=jax.ShapeDtypeStruct((16, width), jnp.float32),
        in_specs=[SMEM, VMEM],
        out_specs=VMEM,
        compiler_params=params,
    )(frame_step, gate_table)
    packet = exchange(packet, query_mask)

    return pl.pallas_call(
        merge_kernel,
        out_shape=jax.ShapeDtypeStruct((rows, width), jnp.bfloat16),
        in_specs=[VMEM] * 4,
        out_specs=VMEM,
        compiler_params=params,
    )(own, own_lines, packet, gates)


def solution(mesh):
    return jax.shard_map(
        local,
        mesh=mesh,
        in_specs=(
            P("tm", "head"),
            P("tm", "head"),
            P("tm", "head"),
            P("head"),
            P("head"),
            P(None, "head"),
            P(),
            P("tm", None),
        ),
        out_specs=P("tm", "head"),
        check_vma=False,
    )
```

```python
import functools

import jax
import jax.numpy as jnp
from jax import lax
from jax.experimental import pallas as pl
from jax.experimental.pallas import tpu as pltpu
from jax.sharding import PartitionSpec as P

HD = 128
BLK = 64
FRAME_TOK = 1560
EPSILON = 1e-06
LOG2E = 1.4426950408889634
SCALE = HD ** (-0.5) * LOG2E
MASKED = -1e30
EXTRA = 16
UNIT = 10**9
ANY = pl.BlockSpec(memory_space=pl.ANY)
VMEM = pl.BlockSpec(memory_space=pltpu.VMEM)
SMEM = pl.BlockSpec(memory_space=pltpu.SMEM)


def spread(row):
    return jnp.broadcast_to(row, (row.shape[1], row.shape[1])).T


def factor_of(line, full_width):
    return spread(lax.rsqrt(line / full_width + EPSILON))


def normed(source_ref, factor, gain_ref):
    parts = []
    for low in range(0, source_ref.shape[1], HD):
        wide = source_ref[:HD, low : low + HD].astype(jnp.float32)
        parts.append((wide * factor * gain_ref[:, low : low + HD]).astype(jnp.bfloat16))
    return jnp.concatenate(parts, axis=1)


def key_kernel(full_width, key_ref, gain_ref, own_ref, other_ref, out_ref):
    total = own_ref[1:2, :] + other_ref[1:2, :]
    out_ref[...] = normed(key_ref, factor_of(total, full_width), gain_ref)


def query_kernel(
    full_width,
    query_ref,
    gain_ref,
    far_ref,
    own_ref,
    other_ref,
    query_out,
):
    total = own_ref[0:1, :] + other_ref[0:1, :]
    query_out[:HD, :] = normed(query_ref, factor_of(total, full_width), gain_ref)
    far = far_ref[...].astype(jnp.float32)
    far = jnp.concatenate([far, jnp.full((1, HD - far.shape[1]), -1.0)], axis=1)
    query_out[HD:, :HD] = jnp.broadcast_to(far, (EXTRA, HD)).astype(jnp.bfloat16)
    query_out[HD:, HD:] = jnp.zeros((EXTRA, query_out.shape[1] - HD), jnp.bfloat16)


def bias_kernel(key_masks, own_ref, remote_ref, bias_out):
    me = lax.axis_index("tm")
    query_mask = lax.axis_size("tm") // 4
    lane = lax.broadcasted_iota(jnp.int32, (1, HD), 1)
    half = (lane >= BLK).astype(jnp.float32)
    for place, query_ref in enumerate((own_ref, remote_ref)):
        far = query_ref[HD:, :HD].astype(jnp.float32)[:1]
        query_id = me ^ (place * query_mask)
        for block, key_mask in enumerate(key_masks):
            key_id = me ^ key_mask
            choice = jnp.sum(jnp.where(lane == key_id, far, 0.0), axis=1, keepdims=True)
            taken = (choice == half) | (jnp.abs(query_id - key_id) <= 1)
            bias_out[8 * place : 8 * place + 8, block * HD : (block + 1) * HD] = (
                jnp.broadcast_to(jnp.where(taken, 0.0, MASKED), (8, HD))
            )


def copy_kernel(source_ref, out_ref):
    out_ref[...] = source_ref[...]


def pack_kernel(held, *refs):
    for place, source_ref in enumerate(refs[: 2 * held]):
        refs[-1][place * HD : (place + 1) * HD, :] = source_ref[...]


def absorb(queries, pack_ref, biases, olds):
    half = pack_ref.shape[0] // 2
    heads, count = len(queries), len(biases)
    scores = []
    for head, query in enumerate(queries):
        scores.append(
            lax.dot_general(
                query,
                pack_ref[:half, head * HD : (head + 1) * HD],
                (((1,), (1,)), ((), ())),
                preferred_element_type=jnp.float32,
            )
        )
    spots = [(head, place) for head in range(heads) for place in range(count)]
    logits, tops, weights, totals = {}, {}, {}, {}
    for head, place in spots:
        part = scores[head][place * HD : (place + 1) * HD]
        logits[head, place] = part * SCALE + biases[place]
    for spot in spots:
        top = jnp.broadcast_to(jnp.max(logits[spot], axis=1, keepdims=True), (HD, HD))
        tops[spot] = top if olds is None else jnp.maximum(top, olds[spot][0])
    for spot in spots:
        weights[spot] = [
            jnp.exp2(logits[spot][:, left : left + HD] - tops[spot])
            for left in range(0, half, HD)
        ]
    added = []
    for head in range(heads):
        rounded = [
            jnp.concatenate([w.astype(jnp.bfloat16) for w in weights[head, place]], axis=1)
            for place in range(count)
        ]
        added.append(
            jnp.dot(
                jnp.concatenate(rounded, axis=0),
                pack_ref[half:, head * HD : (head + 1) * HD],
                preferred_element_type=jnp.float32,
            )
        )
    for spot in spots:
        total = jnp.sum(functools.reduce(jnp.add, weights[spot]), axis=1, keepdims=True)
        totals[spot] = jnp.broadcast_to(total, (HD, HD))
    results = {}
    for head, place in spots:
        spot = (head, place)
        context, total = added[head][place * HD : (place + 1) * HD], totals[spot]
        if olds is not None:
            fade = jnp.exp2(olds[spot][0] - tops[spot])
            total = total + olds[spot][1] * fade
            context = context + olds[spot][2] * fade
        results[spot] = (tops[spot], total, context)
    return results


def held_state(context_ref, stats_ref, head, place):
    part, low, wide = slice(place * HD, (place + 1) * HD), head * HD, 2 * head * HD
    return (
        stats_ref[part, wide : wide + HD],
        stats_ref[part, wide + HD : wide + 2 * HD],
        context_ref[part, low : low + HD],
    )


def step_kernel(first, own_ref, remote_ref, bias_ref, pack_ref, *refs):
    olds, (context_out, stats_out) = refs[:-2], refs[-2:]
    heads, keys = own_ref.shape[1] // HD, pack_ref.shape[0] // 2
    left = first * HD
    biases = [bias_ref[8 * place : 8 * place + 1, left : left + keys] for place in range(2)]
    state = None
    if olds:
        state = {
            (head, place): held_state(*olds, head, place)
            for head in range(heads)
            for place in range(2)
        }
    queries = [
        jnp.concatenate([ref[:HD, head * HD : (head + 1) * HD] for ref in (own_ref, remote_ref)])
        for head in range(heads)
    ]
    for (head, place), result in absorb(queries, pack_ref, biases, state).items():
        part, low, wide = slice(place * HD, (place + 1) * HD), head * HD, 2 * head * HD
        top, total, context = result
        context_out[part, low : low + HD] = context
        stats_out[part, wide : wide + HD] = top
        stats_out[part, wide + HD : wide + 2 * HD] = total


def last_attention(place, query_ref, bias_ref, pack_ref, context_ref, stats_ref, *outs):
    heads, keys = query_ref.shape[1] // HD, pack_ref.shape[0] // 2
    part = slice(place * HD, (place + 1) * HD)
    bias = bias_ref[8 * place : 8 * place + 1, bias_ref.shape[1] - keys :]
    lane = lax.broadcasted_iota(jnp.int32, (1, HD), 1)
    state = {(h, 0): held_state(context_ref, stats_ref, h, place) for h in range(heads)}
    queries = [query_ref[:HD, head * HD : (head + 1) * HD] for head in range(heads)]
    results = absorb(queries, pack_ref, [bias], state)
    columns = jnp.zeros((HD, HD), jnp.float32)
    for head in range(heads):
        top, total, context = results[head, 0]
        outs[0][:HD, head * HD : (head + 1) * HD] = context.astype(outs[0].dtype)
        line = 2 * head
        columns = jnp.where(lane == line, top, jnp.where(lane == line + 1, total, columns))
    lines = columns.T
    sub = lax.broadcasted_iota(jnp.int32, (EXTRA, HD), 0)
    for head in range(heads):
        low = head * HD
        pair = (lines[2 * head : 2 * head + 1, :], lines[2 * head + 1 : 2 * head + 2, :])
        if place == 0:
            for row, value in enumerate(pair):
                outs[1][8 * row : 8 * row + 8, low : low + HD] = jnp.broadcast_to(value, (8, HD))
        else:
            piece_rows = jnp.zeros((EXTRA, HD), jnp.float32)
            for row, value in enumerate(pair):
                first = value.astype(jnp.bfloat16).astype(jnp.float32)
                second = (value - first).astype(jnp.bfloat16).astype(jnp.float32)
                for piece, part_value in enumerate((first, second, value - first - second)):
                    piece_rows = jnp.where(sub == 3 * row + piece, part_value, piece_rows)
            outs[0][HD:, low : low + HD] = piece_rows.astype(jnp.bfloat16)


def gate_kernel(step_ref, table_ref, out_ref):
    rows = out_ref.shape[0] // 2
    start = lax.axis_index("tm") * HD
    first = step_ref[start // FRAME_TOK]
    last = step_ref[(start + HD - 1) // FRAME_TOK]
    out_ref[:rows, :] = jnp.broadcast_to(table_ref[pl.ds(first, 1), :], (rows, out_ref.shape[1]))
    out_ref[rows:, :] = jnp.broadcast_to(table_ref[pl.ds(last, 1), :], (rows, out_ref.shape[1]))


def merge_kernel(own_ref, lines_ref, packet_ref, gate_ref, out_ref):
    rows, width = own_ref.shape
    pieces = packet_ref[rows:, :].astype(jnp.float32)
    own_top, own_total = lines_ref[0:1, :], lines_ref[8:9, :]
    other_top = pieces[0:1] + pieces[1:2] + pieces[2:3]
    other_total = pieces[3:4] + pieces[4:5] + pieces[5:6]
    top = jnp.maximum(own_top, other_top)
    own_share, other_share = jnp.exp2(own_top - top), jnp.exp2(other_top - top)
    scale = 1.0 / (own_total * own_share + other_total * other_share)
    own_share, other_share = own_share * scale, other_share * scale
    start = lax.axis_index("tm") * rows
    first_rows = (start // FRAME_TOK + 1) * FRAME_TOK - start
    row_ids = lax.broadcasted_iota(jnp.int32, (rows, 1), 0)
    for low in range(0, width, HD):
        high = low + HD
        context = own_ref[:, low:high] * spread(own_share[:, low:high])
        other = packet_ref[:rows, low:high].astype(jnp.float32)
        context += other * spread(other_share[:, low:high])
        gate = jnp.where(
            row_ids < first_rows, gate_ref[0:1, low:high], gate_ref[8:9, low:high]
        )
        out_ref[:, low:high] = (context * gate).astype(jnp.bfloat16)


def exchange(array, mask):
    count = lax.axis_size("tm")
    return lax.ppermute(array, "tm", [(i, i ^ mask) for i in range(count)])


def gathered(array, bits):
    held = {0: array}
    for bit in bits:
        for mask in list(held):
            held[mask ^ bit] = exchange(held[mask], bit)
    return held


def cost(flops):
    return pl.CostEstimate(flops=flops, bytes_accessed=0, transcendentals=0)


def local(
    query_proj, key_proj, value_proj, query_gain, key_gain, gate_table, frame_step, far_blocks
):
    rows, width = query_proj.shape
    count = lax.axis_size("tm")
    splits = lax.axis_size("head")
    full_width = width * splits
    params = pltpu.CompilerParams(vmem_limit_bytes=(8 + count // 2) * 2**20)
    query_mask = count // 4
    bits = [1 << place for place in range(1, count.bit_length() - 1)]
    bits = [bit for bit in bits[::-1] if bit != query_mask]
    query_gain = query_gain.reshape(1, width)
    key_gain = key_gain.reshape(1, width)

    far = bits[0]
    far_value = exchange(value_proj, far)
    query_f, key_f = query_proj.astype(jnp.float32), key_proj.astype(jnp.float32)
    sums = jnp.stack(
        [jnp.sum(query_f * query_f, axis=-1), jnp.sum(key_f * key_f, axis=-1)], axis=0
    )
    if splits == 2:
        others = lax.ppermute(sums, "head", [(0, 1), (1, 0)])
    else:
        sums = lax.psum(sums, "head")
        others = jnp.zeros_like(sums)
    own_key = pl.pallas_call(
        functools.partial(key_kernel, width * splits),
        out_shape=jax.ShapeDtypeStruct((rows, width), jnp.bfloat16),
        in_specs=[VMEM] * 4,
        out_specs=VMEM,
        compiler_params=params,
    )(key_proj, key_gain, sums, others)
    near_values = gathered(value_proj, bits[1:])
    near_keys = gathered(own_key, bits[1:])
    query_packet = pl.pallas_call(
        functools.partial(query_kernel, width * splits),
        out_shape=jax.ShapeDtypeStruct((rows + EXTRA, width), jnp.bfloat16),
        in_specs=[VMEM] * 5,
        out_specs=VMEM,
        compiler_params=params,
    )(query_proj, query_gain, far_blocks, sums, others)
    far_key = exchange(own_key, far)
    queries = [query_packet, exchange(query_packet, query_mask)]
    far_value = pl.pallas_call(
        copy_kernel,
        out_shape=jax.ShapeDtypeStruct((rows, width), jnp.bfloat16),
        in_specs=[VMEM],
        out_specs=VMEM,
        compiler_params=params,
        cost_estimate=cost(4 * UNIT),
    )(far_value)
    late_keys, late_values = gathered(far_key, bits[1:]), gathered(far_value, bits[1:])
    early = [0, far] + sorted(mask for mask in near_keys if mask)
    late = sorted(mask ^ far for mask in late_keys if mask)
    early_masks = early + [mask ^ 1 for mask in early]
    all_masks = early_masks + late + [mask ^ 1 for mask in late]
    biases = pl.pallas_call(
        functools.partial(bias_kernel, all_masks),
        out_shape=jax.ShapeDtypeStruct((16, len(all_masks) * HD), jnp.float32),
        in_specs=[VMEM] * 2,
        out_specs=VMEM,
        compiler_params=params,
    )(*queries)

    def packed(keys, values, flops, *after):
        held = len(keys)
        return pl.pallas_call(
            functools.partial(pack_kernel, held),
            out_shape=jax.ShapeDtypeStruct((2 * held * rows, width), jnp.bfloat16),
            in_specs=[VMEM] * (2 * held + len(after)),
            out_specs=VMEM,
            compiler_params=params,
            cost_estimate=cost(flops),
        )(*keys, *values, *after)

    near_keys[far], near_values[far] = far_key, far_value
    early_pack = packed(
        [near_keys[mask] for mask in early], [near_values[mask] for mask in early], 0
    )

    def step(first, pack, *state):
        return pl.pallas_call(
            functools.partial(step_kernel, first),
            out_shape=[
                jax.ShapeDtypeStruct((2 * rows, width), jnp.float32),
                jax.ShapeDtypeStruct((2 * rows, 2 * width), jnp.float32),
            ],
            in_specs=[VMEM] * (4 + len(state)),
            out_specs=[VMEM] * 2,
            compiler_params=params,
        )(*queries, biases, pack, *state)

    state = step(0, early_pack)
    late_pack = packed(
        [late_keys[mask ^ far] for mask in late],
        [late_values[mask ^ far] for mask in late],
        12 * UNIT,
        state[1],
    )
    state = step(len(early), exchange(early_pack, 1), *state)
    state = step(2 * len(early), late_pack, *state)
    last_pack = exchange(late_pack, 1)

    def last(place, out_shape):
        return pl.pallas_call(
            functools.partial(last_attention, place),
            out_shape=out_shape,
            in_specs=[VMEM] * 5,
            out_specs=[VMEM] * len(out_shape),
            compiler_params=params,
        )(queries[place], biases, last_pack, *state)

    (packet,) = last(1, [jax.ShapeDtypeStruct((rows + EXTRA, width), jnp.bfloat16)])
    own, own_lines = last(
        0,
        [
            jax.ShapeDtypeStruct((rows, width), jnp.float32),
            jax.ShapeDtypeStruct((16, width), jnp.float32),
        ],
    )
    gates = pl.pallas_call(
        gate_kernel,
        out_shape=jax.ShapeDtypeStruct((16, width), jnp.float32),
        in_specs=[SMEM, VMEM],
        out_specs=VMEM,
        compiler_params=params,
    )(frame_step, gate_table)
    packet = exchange(packet, query_mask)

    return pl.pallas_call(
        merge_kernel,
        out_shape=jax.ShapeDtypeStruct((rows, width), jnp.bfloat16),
        in_specs=[VMEM] * 4,
        out_specs=VMEM,
        compiler_params=params,
    )(own, own_lines, packet, gates)


def solution(mesh):
    return jax.shard_map(
        local,
        mesh=mesh,
        in_specs=(
            P("tm", "head"),
            P("tm", "head"),
            P("tm", "head"),
            P("head"),
            P("head"),
            P(None, "head"),
            P(),
            P("tm", None),
        ),
        out_specs=P("tm", "head"),
        check_vma=False,
    )
```

```python
import functools

import jax
import jax.numpy as jnp
from jax import lax
from jax.experimental import pallas as pl
from jax.experimental.pallas import tpu as pltpu
from jax.sharding import PartitionSpec as P

HD = 128
BLK = 64
FRAME_TOK = 1560
EPSILON = 1e-06
LOG2E = 1.4426950408889634
SCALE = HD ** (-0.5) * LOG2E
MASKED = -1e30
EXTRA = 16
UNIT = 10**9
ANY = pl.BlockSpec(memory_space=pl.ANY)
VMEM = pl.BlockSpec(memory_space=pltpu.VMEM)
SMEM = pl.BlockSpec(memory_space=pltpu.SMEM)


def spread(row):
    return jnp.broadcast_to(row, (row.shape[1], row.shape[1])).T


def factor_of(line, full_width):
    return spread(lax.rsqrt(line / full_width + EPSILON))


def normed(source_ref, factor, gain_ref):
    parts = []
    for low in range(0, source_ref.shape[1], HD):
        wide = source_ref[:HD, low : low + HD].astype(jnp.float32)
        parts.append((wide * factor * gain_ref[:, low : low + HD]).astype(jnp.bfloat16))
    return jnp.concatenate(parts, axis=1)


def key_kernel(full_width, key_ref, gain_ref, own_ref, other_ref, out_ref, *piece_refs):
    total = own_ref[1:2, :] + other_ref[1:2, :]
    key = normed(key_ref, factor_of(total, full_width), gain_ref)
    out_ref[...] = key
    low = 0
    for piece_ref in piece_refs:
        high = low + piece_ref.shape[1]
        piece_ref[...] = key[:, low:high]
        low = high


def query_kernel(
    full_width,
    query_ref,
    gain_ref,
    far_ref,
    own_ref,
    other_ref,
    query_out,
):
    total = own_ref[0:1, :] + other_ref[0:1, :]
    query_out[:HD, :] = normed(query_ref, factor_of(total, full_width), gain_ref)
    far = far_ref[...].astype(jnp.float32)
    far = jnp.concatenate([far, jnp.full((1, HD - far.shape[1]), -1.0)], axis=1)
    query_out[HD:, :HD] = jnp.broadcast_to(far, (EXTRA, HD)).astype(jnp.bfloat16)
    query_out[HD:, HD:] = jnp.zeros((EXTRA, query_out.shape[1] - HD), jnp.bfloat16)


def bias_kernel(key_masks, own_ref, remote_ref, bias_out):
    me = lax.axis_index("tm")
    query_mask = lax.axis_size("tm") // 4
    lane = lax.broadcasted_iota(jnp.int32, (1, HD), 1)
    half = (lane >= BLK).astype(jnp.float32)
    for place, query_ref in enumerate((own_ref, remote_ref)):
        far = query_ref[HD:, :HD].astype(jnp.float32)[:1]
        query_id = me ^ (place * query_mask)
        for block, key_mask in enumerate(key_masks):
            key_id = me ^ key_mask
            choice = jnp.sum(jnp.where(lane == key_id, far, 0.0), axis=1, keepdims=True)
            taken = (choice == half) | (jnp.abs(query_id - key_id) <= 1)
            bias_out[8 * place : 8 * place + 8, block * HD : (block + 1) * HD] = (
                jnp.broadcast_to(jnp.where(taken, 0.0, MASKED), (8, HD))
            )


def copy_kernel(source_ref, out_ref):
    out_ref[...] = source_ref[...]


def pack_kernel(spots, *refs):
    for (row, low), source_ref in zip(spots, refs):
        rows, width = source_ref.shape
        refs[-1][row : row + rows, low : low + width] = source_ref[...]


def absorb(queries, pack_ref, biases, olds):
    half = pack_ref.shape[0] // 2
    heads, count = len(queries), len(biases)
    scores = []
    for head, query in enumerate(queries):
        scores.append(
            lax.dot_general(
                query,
                pack_ref[:half, head * HD : (head + 1) * HD],
                (((1,), (1,)), ((), ())),
                preferred_element_type=jnp.float32,
            )
        )
    spots = [(head, place) for head in range(heads) for place in range(count)]
    logits, tops, weights, totals = {}, {}, {}, {}
    for head, place in spots:
        part = scores[head][place * HD : (place + 1) * HD]
        logits[head, place] = part * SCALE + biases[place]
    for spot in spots:
        top = jnp.broadcast_to(jnp.max(logits[spot], axis=1, keepdims=True), (HD, HD))
        tops[spot] = top if olds is None else jnp.maximum(top, olds[spot][0])
    for spot in spots:
        weights[spot] = [
            jnp.exp2(logits[spot][:, left : left + HD] - tops[spot])
            for left in range(0, half, HD)
        ]
    added = []
    for head in range(heads):
        rounded = [
            jnp.concatenate([w.astype(jnp.bfloat16) for w in weights[head, place]], axis=1)
            for place in range(count)
        ]
        added.append(
            jnp.dot(
                jnp.concatenate(rounded, axis=0),
                pack_ref[half:, head * HD : (head + 1) * HD],
                preferred_element_type=jnp.float32,
            )
        )
    for spot in spots:
        total = jnp.sum(functools.reduce(jnp.add, weights[spot]), axis=1, keepdims=True)
        totals[spot] = jnp.broadcast_to(total, (HD, HD))
    results = {}
    for head, place in spots:
        spot = (head, place)
        context, total = added[head][place * HD : (place + 1) * HD], totals[spot]
        if olds is not None:
            fade = jnp.exp2(olds[spot][0] - tops[spot])
            total = total + olds[spot][1] * fade
            context = context + olds[spot][2] * fade
        results[spot] = (tops[spot], total, context)
    return results


def held_state(context_ref, stats_ref, head, place):
    part, low, wide = slice(place * HD, (place + 1) * HD), head * HD, 2 * head * HD
    return (
        stats_ref[part, wide : wide + HD],
        stats_ref[part, wide + HD : wide + 2 * HD],
        context_ref[part, low : low + HD],
    )


def step_kernel(first, own_ref, remote_ref, bias_ref, pack_ref, *refs):
    olds, (context_out, stats_out) = refs[:-2], refs[-2:]
    heads, keys = own_ref.shape[1] // HD, pack_ref.shape[0] // 2
    left = first * HD
    biases = [bias_ref[8 * place : 8 * place + 1, left : left + keys] for place in range(2)]
    state = None
    if olds:
        state = {
            (head, place): held_state(*olds, head, place)
            for head in range(heads)
            for place in range(2)
        }
    queries = [
        jnp.concatenate([ref[:HD, head * HD : (head + 1) * HD] for ref in (own_ref, remote_ref)])
        for head in range(heads)
    ]
    for (head, place), result in absorb(queries, pack_ref, biases, state).items():
        part, low, wide = slice(place * HD, (place + 1) * HD), head * HD, 2 * head * HD
        top, total, context = result
        context_out[part, low : low + HD] = context
        stats_out[part, wide : wide + HD] = top
        stats_out[part, wide + HD : wide + 2 * HD] = total


def last_attention(place, query_ref, bias_ref, pack_ref, context_ref, stats_ref, *outs):
    heads, keys = query_ref.shape[1] // HD, pack_ref.shape[0] // 2
    part = slice(place * HD, (place + 1) * HD)
    bias = bias_ref[8 * place : 8 * place + 1, bias_ref.shape[1] - keys :]
    lane = lax.broadcasted_iota(jnp.int32, (1, HD), 1)
    state = {(h, 0): held_state(context_ref, stats_ref, h, place) for h in range(heads)}
    queries = [query_ref[:HD, head * HD : (head + 1) * HD] for head in range(heads)]
    results = absorb(queries, pack_ref, [bias], state)
    columns = jnp.zeros((HD, HD), jnp.float32)
    for head in range(heads):
        top, total, context = results[head, 0]
        outs[0][:HD, head * HD : (head + 1) * HD] = context.astype(outs[0].dtype)
        line = 2 * head
        columns = jnp.where(lane == line, top, jnp.where(lane == line + 1, total, columns))
    lines = columns.T
    sub = lax.broadcasted_iota(jnp.int32, (EXTRA, HD), 0)
    for head in range(heads):
        low = head * HD
        pair = (lines[2 * head : 2 * head + 1, :], lines[2 * head + 1 : 2 * head + 2, :])
        if place == 0:
            for row, value in enumerate(pair):
                outs[1][8 * row : 8 * row + 8, low : low + HD] = jnp.broadcast_to(value, (8, HD))
        else:
            piece_rows = jnp.zeros((EXTRA, HD), jnp.float32)
            for row, value in enumerate(pair):
                first = value.astype(jnp.bfloat16).astype(jnp.float32)
                second = (value - first).astype(jnp.bfloat16).astype(jnp.float32)
                for piece, part_value in enumerate((first, second, value - first - second)):
                    piece_rows = jnp.where(sub == 3 * row + piece, part_value, piece_rows)
            outs[0][HD:, low : low + HD] = piece_rows.astype(jnp.bfloat16)


def gate_kernel(step_ref, table_ref, out_ref):
    rows = out_ref.shape[0] // 2
    start = lax.axis_index("tm") * HD
    first = step_ref[start // FRAME_TOK]
    last = step_ref[(start + HD - 1) // FRAME_TOK]
    out_ref[:rows, :] = jnp.broadcast_to(table_ref[pl.ds(first, 1), :], (rows, out_ref.shape[1]))
    out_ref[rows:, :] = jnp.broadcast_to(table_ref[pl.ds(last, 1), :], (rows, out_ref.shape[1]))


def merge_kernel(own_ref, lines_ref, packet_ref, gate_ref, out_ref):
    rows, width = own_ref.shape
    pieces = packet_ref[rows:, :].astype(jnp.float32)
    own_top, own_total = lines_ref[0:1, :], lines_ref[8:9, :]
    other_top = pieces[0:1] + pieces[1:2] + pieces[2:3]
    other_total = pieces[3:4] + pieces[4:5] + pieces[5:6]
    top = jnp.maximum(own_top, other_top)
    own_share, other_share = jnp.exp2(own_top - top), jnp.exp2(other_top - top)
    scale = 1.0 / (own_total * own_share + other_total * other_share)
    own_share, other_share = own_share * scale, other_share * scale
    start = lax.axis_index("tm") * rows
    first_rows = (start // FRAME_TOK + 1) * FRAME_TOK - start
    row_ids = lax.broadcasted_iota(jnp.int32, (rows, 1), 0)
    for low in range(0, width, HD):
        high = low + HD
        context = own_ref[:, low:high] * spread(own_share[:, low:high])
        other = packet_ref[:rows, low:high].astype(jnp.float32)
        context += other * spread(other_share[:, low:high])
        gate = jnp.where(
            row_ids < first_rows, gate_ref[0:1, low:high], gate_ref[8:9, low:high]
        )
        out_ref[:, low:high] = (context * gate).astype(jnp.bfloat16)


def exchange(array, mask):
    count = lax.axis_size("tm")
    return lax.ppermute(array, "tm", [(i, i ^ mask) for i in range(count)])


def gathered(array, bits):
    held = {0: array}
    for bit in bits:
        for mask in list(held):
            held[mask ^ bit] = exchange(held[mask], bit)
    return held


def cost(flops):
    return pl.CostEstimate(flops=flops, bytes_accessed=0, transcendentals=0)


def local(
    query_proj, key_proj, value_proj, query_gain, key_gain, gate_table, frame_step, far_blocks
):
    rows, width = query_proj.shape
    count = lax.axis_size("tm")
    splits = lax.axis_size("head")
    full_width = width * splits
    params = pltpu.CompilerParams(vmem_limit_bytes=(8 + count // 2) * 2**20)
    query_mask = count // 4
    bits = [1 << place for place in range(1, count.bit_length() - 1)]
    bits = [bit for bit in bits[::-1] if bit != query_mask]
    query_gain = query_gain.reshape(1, width)
    key_gain = key_gain.reshape(1, width)

    far = bits[0]

    def copied(source, flops):
        return pl.pallas_call(
            copy_kernel,
            out_shape=jax.ShapeDtypeStruct(source.shape, source.dtype),
            in_specs=[VMEM],
            out_specs=VMEM,
            compiler_params=params,
            cost_estimate=cost(flops),
        )(source)

    far_value = exchange(value_proj, far)
    query_f, key_f = query_proj.astype(jnp.float32), key_proj.astype(jnp.float32)
    sums = jnp.stack(
        [jnp.sum(query_f * query_f, axis=-1), jnp.sum(key_f * key_f, axis=-1)], axis=0
    )
    if splits == 2:
        others = lax.ppermute(sums, "head", [(0, 1), (1, 0)])
    else:
        sums = lax.psum(sums, "head")
        others = jnp.zeros_like(sums)
    piece_widths = [width - HD, HD]
    own_key, *own_pieces = pl.pallas_call(
        functools.partial(key_kernel, width * splits),
        out_shape=[
            jax.ShapeDtypeStruct((rows, piece), jnp.bfloat16) for piece in [width] + piece_widths
        ],
        in_specs=[VMEM] * 4,
        out_specs=[VMEM] * 3,
        compiler_params=params,
    )(key_proj, key_gain, sums, others)
    near_values = gathered(value_proj, bits[1:])
    near_keys = gathered(own_key, bits[1:])
    query_packet = pl.pallas_call(
        functools.partial(query_kernel, width * splits),
        out_shape=jax.ShapeDtypeStruct((rows + EXTRA, width), jnp.bfloat16),
        in_specs=[VMEM] * 5,
        out_specs=VMEM,
        compiler_params=params,
    )(query_proj, query_gain, far_blocks, sums, others)
    far_pieces = [
        copied(exchange(piece, far), flops) for piece, flops in zip(own_pieces, (4 * UNIT, 0))
    ]
    queries = [query_packet, exchange(query_packet, query_mask)]
    far_value = copied(far_value, 4 * UNIT)
    late_pieces = [gathered(piece, bits[1:]) for piece in far_pieces]
    late_values = gathered(far_value, bits[1:])
    early = [0, far] + sorted(mask for mask in near_keys if mask)
    late = sorted(mask ^ far for mask in late_values if mask)
    early_masks = early + [mask ^ 1 for mask in early]
    all_masks = early_masks + late + [mask ^ 1 for mask in late]
    biases = pl.pallas_call(
        functools.partial(bias_kernel, all_masks),
        out_shape=jax.ShapeDtypeStruct((16, len(all_masks) * HD), jnp.float32),
        in_specs=[VMEM] * 2,
        out_specs=VMEM,
        compiler_params=params,
    )(*queries)

    def packed(keys, values, flops, *after):
        spots, sources = [], []
        for place, parts in enumerate(keys + [[value] for value in values]):
            low = 0
            for part in parts:
                spots.append((place * rows, low))
                sources.append(part)
                low += part.shape[1]
        return pl.pallas_call(
            functools.partial(pack_kernel, spots),
            out_shape=jax.ShapeDtypeStruct((2 * len(keys) * rows, width), jnp.bfloat16),
            in_specs=[VMEM] * (len(sources) + len(after)),
            out_specs=VMEM,
            compiler_params=params,
            cost_estimate=cost(flops),
        )(*sources, *after)

    near_values[far] = far_value
    early_keys = [far_pieces if mask == far else [near_keys[mask]] for mask in early]
    early_pack = packed(early_keys, [near_values[mask] for mask in early], 0)

    def step(first, pack, *state):
        return pl.pallas_call(
            functools.partial(step_kernel, first),
            out_shape=[
                jax.ShapeDtypeStruct((2 * rows, width), jnp.float32),
                jax.ShapeDtypeStruct((2 * rows, 2 * width), jnp.float32),
            ],
            in_specs=[VMEM] * (4 + len(state)),
            out_specs=[VMEM] * 2,
            compiler_params=params,
        )(*queries, biases, pack, *state)

    state = step(0, early_pack)
    late_pack = packed(
        [[pieces[mask ^ far] for pieces in late_pieces] for mask in late],
        [late_values[mask ^ far] for mask in late],
        12 * UNIT,
        state[1],
    )
    state = step(len(early), exchange(early_pack, 1), *state)
    state = step(2 * len(early), late_pack, *state)
    last_pack = exchange(late_pack, 1)

    def last(place, out_shape):
        return pl.pallas_call(
            functools.partial(last_attention, place),
            out_shape=out_shape,
            in_specs=[VMEM] * 5,
            out_specs=[VMEM] * len(out_shape),
            compiler_params=params,
        )(queries[place], biases, last_pack, *state)

    (packet,) = last(1, [jax.ShapeDtypeStruct((rows + EXTRA, width), jnp.bfloat16)])
    own, own_lines = last(
        0,
        [
            jax.ShapeDtypeStruct((rows, width), jnp.float32),
            jax.ShapeDtypeStruct((16, width), jnp.float32),
        ],
    )
    gates = pl.pallas_call(
        gate_kernel,
        out_shape=jax.ShapeDtypeStruct((16, width), jnp.float32),
        in_specs=[SMEM, VMEM],
        out_specs=VMEM,
        compiler_params=params,
    )(frame_step, gate_table)
    packet = exchange(packet, query_mask)

    return pl.pallas_call(
        merge_kernel,
        out_shape=jax.ShapeDtypeStruct((rows, width), jnp.bfloat16),
        in_specs=[VMEM] * 4,
        out_specs=VMEM,
        compiler_params=params,
    )(own, own_lines, packet, gates)


def solution(mesh):
    return jax.shard_map(
        local,
        mesh=mesh,
        in_specs=(
            P("tm", "head"),
            P("tm", "head"),
            P("tm", "head"),
            P("head"),
            P("head"),
            P(None, "head"),
            P(),
            P("tm", None),
        ),
        out_specs=P("tm", "head"),
        check_vma=False,
    )
```

```python
import functools

import jax
import jax.numpy as jnp
from jax import lax
from jax.experimental import pallas as pl
from jax.experimental.pallas import tpu as pltpu
from jax.sharding import PartitionSpec as P

HD = 128
BLK = 64
FRAME_TOK = 1560
EPSILON = 1e-06
LOG2E = 1.4426950408889634
SCALE = HD ** (-0.5) * LOG2E
MASKED = -1e30
EXTRA = 16
UNIT = 10**9
ANY = pl.BlockSpec(memory_space=pl.ANY)
VMEM = pl.BlockSpec(memory_space=pltpu.VMEM)
SMEM = pl.BlockSpec(memory_space=pltpu.SMEM)


def spread(row):
    return jnp.broadcast_to(row, (row.shape[1], row.shape[1])).T


def factor_of(line, full_width):
    return spread(lax.rsqrt(line / full_width + EPSILON))


def normed(source_ref, factor, gain_ref):
    parts = []
    for low in range(0, source_ref.shape[1], HD):
        wide = source_ref[:HD, low : low + HD].astype(jnp.float32)
        parts.append((wide * factor * gain_ref[:, low : low + HD]).astype(jnp.bfloat16))
    return jnp.concatenate(parts, axis=1)


def key_kernel(full_width, key_ref, gain_ref, own_ref, other_ref, out_ref):
    total = own_ref[...] + other_ref[...]
    out_ref[...] = normed(key_ref, factor_of(total, full_width), gain_ref)


def query_kernel(
    full_width,
    query_ref,
    gain_ref,
    far_ref,
    own_ref,
    other_ref,
    query_out,
):
    total = own_ref[...] + other_ref[...]
    query_out[:HD, :] = normed(query_ref, factor_of(total, full_width), gain_ref)
    far = far_ref[...].astype(jnp.float32)
    far = jnp.concatenate([far, jnp.full((1, HD - far.shape[1]), -1.0)], axis=1)
    query_out[HD:, :HD] = jnp.broadcast_to(far, (EXTRA, HD)).astype(jnp.bfloat16)
    query_out[HD:, HD:] = jnp.zeros((EXTRA, query_out.shape[1] - HD), jnp.bfloat16)


def bias_kernel(key_masks, own_ref, remote_ref, bias_out):
    me = lax.axis_index("tm")
    query_mask = lax.axis_size("tm") // 4
    lane = lax.broadcasted_iota(jnp.int32, (1, HD), 1)
    half = (lane >= BLK).astype(jnp.float32)
    for place, query_ref in enumerate((own_ref, remote_ref)):
        far = query_ref[HD:, :HD].astype(jnp.float32)[:1]
        query_id = me ^ (place * query_mask)
        for block, key_mask in enumerate(key_masks):
            key_id = me ^ key_mask
            choice = jnp.sum(jnp.where(lane == key_id, far, 0.0), axis=1, keepdims=True)
            taken = (choice == half) | (jnp.abs(query_id - key_id) <= 1)
            bias_out[8 * place : 8 * place + 8, block * HD : (block + 1) * HD] = (
                jnp.broadcast_to(jnp.where(taken, 0.0, MASKED), (8, HD))
            )


def copy_kernel(source_ref, out_ref):
    out_ref[...] = source_ref[...]


def pack_kernel(held, *refs):
    for place, source_ref in enumerate(refs[: 2 * held]):
        refs[-1][place * HD : (place + 1) * HD, :] = source_ref[...]


def absorb(queries, pack_ref, biases, olds):
    half = pack_ref.shape[0] // 2
    heads, count = len(queries), len(biases)
    scores = []
    for head, query in enumerate(queries):
        scores.append(
            lax.dot_general(
                query,
                pack_ref[:half, head * HD : (head + 1) * HD],
                (((1,), (1,)), ((), ())),
                preferred_element_type=jnp.float32,
            )
        )
    spots = [(head, place) for head in range(heads) for place in range(count)]
    logits, tops, weights, totals = {}, {}, {}, {}
    for head, place in spots:
        part = scores[head][place * HD : (place + 1) * HD]
        logits[head, place] = part * SCALE + biases[place]
    for spot in spots:
        top = jnp.broadcast_to(jnp.max(logits[spot], axis=1, keepdims=True), (HD, HD))
        tops[spot] = top if olds is None else jnp.maximum(top, olds[spot][0])
    for spot in spots:
        weights[spot] = [
            jnp.exp2(logits[spot][:, left : left + HD] - tops[spot])
            for left in range(0, half, HD)
        ]
    added = []
    for head in range(heads):
        rounded = [
            jnp.concatenate([w.astype(jnp.bfloat16) for w in weights[head, place]], axis=1)
            for place in range(count)
        ]
        added.append(
            jnp.dot(
                jnp.concatenate(rounded, axis=0),
                pack_ref[half:, head * HD : (head + 1) * HD],
                preferred_element_type=jnp.float32,
            )
        )
    for spot in spots:
        total = jnp.sum(functools.reduce(jnp.add, weights[spot]), axis=1, keepdims=True)
        totals[spot] = jnp.broadcast_to(total, (HD, HD))
    results = {}
    for head, place in spots:
        spot = (head, place)
        context, total = added[head][place * HD : (place + 1) * HD], totals[spot]
        if olds is not None:
            fade = jnp.exp2(olds[spot][0] - tops[spot])
            total = total + olds[spot][1] * fade
            context = context + olds[spot][2] * fade
        results[spot] = (tops[spot], total, context)
    return results


def held_state(context_ref, stats_ref, head, place):
    part, low, wide = slice(place * HD, (place + 1) * HD), head * HD, 2 * head * HD
    return (
        stats_ref[part, wide : wide + HD],
        stats_ref[part, wide + HD : wide + 2 * HD],
        context_ref[part, low : low + HD],
    )


def step_kernel(first, own_ref, remote_ref, bias_ref, pack_ref, *refs):
    olds, (context_out, stats_out) = refs[:-2], refs[-2:]
    heads, keys = own_ref.shape[1] // HD, pack_ref.shape[0] // 2
    left = first * HD
    biases = [bias_ref[8 * place : 8 * place + 1, left : left + keys] for place in range(2)]
    state = None
    if olds:
        state = {
            (head, place): held_state(*olds, head, place)
            for head in range(heads)
            for place in range(2)
        }
    queries = [
        jnp.concatenate([ref[:HD, head * HD : (head + 1) * HD] for ref in (own_ref, remote_ref)])
        for head in range(heads)
    ]
    for (head, place), result in absorb(queries, pack_ref, biases, state).items():
        part, low, wide = slice(place * HD, (place + 1) * HD), head * HD, 2 * head * HD
        top, total, context = result
        context_out[part, low : low + HD] = context
        stats_out[part, wide : wide + HD] = top
        stats_out[part, wide + HD : wide + 2 * HD] = total


def last_attention(place, query_ref, bias_ref, pack_ref, context_ref, stats_ref, *outs):
    heads, keys = query_ref.shape[1] // HD, pack_ref.shape[0] // 2
    part = slice(place * HD, (place + 1) * HD)
    bias = bias_ref[8 * place : 8 * place + 1, bias_ref.shape[1] - keys :]
    lane = lax.broadcasted_iota(jnp.int32, (1, HD), 1)
    state = {(h, 0): held_state(context_ref, stats_ref, h, place) for h in range(heads)}
    queries = [query_ref[:HD, head * HD : (head + 1) * HD] for head in range(heads)]
    results = absorb(queries, pack_ref, [bias], state)
    columns = jnp.zeros((HD, HD), jnp.float32)
    for head in range(heads):
        top, total, context = results[head, 0]
        outs[0][:HD, head * HD : (head + 1) * HD] = context.astype(outs[0].dtype)
        line = 2 * head
        columns = jnp.where(lane == line, top, jnp.where(lane == line + 1, total, columns))
    lines = columns.T
    sub = lax.broadcasted_iota(jnp.int32, (EXTRA, HD), 0)
    for head in range(heads):
        low = head * HD
        pair = (lines[2 * head : 2 * head + 1, :], lines[2 * head + 1 : 2 * head + 2, :])
        if place == 0:
            for row, value in enumerate(pair):
                outs[1][8 * row : 8 * row + 8, low : low + HD] = jnp.broadcast_to(value, (8, HD))
        else:
            piece_rows = jnp.zeros((EXTRA, HD), jnp.float32)
            for row, value in enumerate(pair):
                first = value.astype(jnp.bfloat16).astype(jnp.float32)
                second = (value - first).astype(jnp.bfloat16).astype(jnp.float32)
                for piece, part_value in enumerate((first, second, value - first - second)):
                    piece_rows = jnp.where(sub == 3 * row + piece, part_value, piece_rows)
            outs[0][HD:, low : low + HD] = piece_rows.astype(jnp.bfloat16)


def gate_kernel(step_ref, table_ref, out_ref):
    rows = out_ref.shape[0] // 2
    start = lax.axis_index("tm") * HD
    first = step_ref[start // FRAME_TOK]
    last = step_ref[(start + HD - 1) // FRAME_TOK]
    out_ref[:rows, :] = jnp.broadcast_to(table_ref[pl.ds(first, 1), :], (rows, out_ref.shape[1]))
    out_ref[rows:, :] = jnp.broadcast_to(table_ref[pl.ds(last, 1), :], (rows, out_ref.shape[1]))


def merge_kernel(own_ref, lines_ref, packet_ref, gate_ref, out_ref):
    rows, width = own_ref.shape
    pieces = packet_ref[rows:, :].astype(jnp.float32)
    own_top, own_total = lines_ref[0:1, :], lines_ref[8:9, :]
    other_top = pieces[0:1] + pieces[1:2] + pieces[2:3]
    other_total = pieces[3:4] + pieces[4:5] + pieces[5:6]
    top = jnp.maximum(own_top, other_top)
    own_share, other_share = jnp.exp2(own_top - top), jnp.exp2(other_top - top)
    scale = 1.0 / (own_total * own_share + other_total * other_share)
    own_share, other_share = own_share * scale, other_share * scale
    start = lax.axis_index("tm") * rows
    first_rows = (start // FRAME_TOK + 1) * FRAME_TOK - start
    row_ids = lax.broadcasted_iota(jnp.int32, (rows, 1), 0)
    for low in range(0, width, HD):
        high = low + HD
        context = own_ref[:, low:high] * spread(own_share[:, low:high])
        other = packet_ref[:rows, low:high].astype(jnp.float32)
        context += other * spread(other_share[:, low:high])
        gate = jnp.where(
            row_ids < first_rows, gate_ref[0:1, low:high], gate_ref[8:9, low:high]
        )
        out_ref[:, low:high] = (context * gate).astype(jnp.bfloat16)


def exchange(array, mask):
    count = lax.axis_size("tm")
    return lax.ppermute(array, "tm", [(i, i ^ mask) for i in range(count)])


def gathered(array, bits):
    held = {0: array}
    for bit in bits:
        for mask in list(held):
            held[mask ^ bit] = exchange(held[mask], bit)
    return held


def cost(flops):
    return pl.CostEstimate(flops=flops, bytes_accessed=0, transcendentals=0)


def local(
    query_proj, key_proj, value_proj, query_gain, key_gain, gate_table, frame_step, far_blocks
):
    rows, width = query_proj.shape
    count = lax.axis_size("tm")
    splits = lax.axis_size("head")
    full_width = width * splits
    params = pltpu.CompilerParams(vmem_limit_bytes=(8 + count // 2) * 2**20)
    query_mask = count // 4
    bits = [1 << place for place in range(1, count.bit_length() - 1)]
    bits = [bit for bit in bits[::-1] if bit != query_mask]
    query_gain = query_gain.reshape(1, width)
    key_gain = key_gain.reshape(1, width)

    far = bits[0]
    far_value = exchange(value_proj, far)

    def row_sums(source):
        wide = source.astype(jnp.float32)
        own = jnp.sum(wide * wide, axis=-1)[None, :]
        if splits == 2:
            return own, lax.ppermute(own, "head", [(0, 1), (1, 0)])
        own = lax.psum(own, "head")
        return own, jnp.zeros_like(own)

    key_sums, query_sums = row_sums(key_proj), row_sums(query_proj)
    own_key = pl.pallas_call(
        functools.partial(key_kernel, width * splits),
        out_shape=jax.ShapeDtypeStruct((rows, width), jnp.bfloat16),
        in_specs=[VMEM] * 4,
        out_specs=VMEM,
        compiler_params=params,
    )(key_proj, key_gain, *key_sums)
    near_values = gathered(value_proj, bits[1:])
    near_keys = gathered(own_key, bits[1:])
    query_packet = pl.pallas_call(
        functools.partial(query_kernel, width * splits),
        out_shape=jax.ShapeDtypeStruct((rows + EXTRA, width), jnp.bfloat16),
        in_specs=[VMEM] * 5,
        out_specs=VMEM,
        compiler_params=params,
    )(query_proj, query_gain, far_blocks, *query_sums)
    far_key = exchange(own_key, far)
    queries = [query_packet, exchange(query_packet, query_mask)]
    far_value = pl.pallas_call(
        copy_kernel,
        out_shape=jax.ShapeDtypeStruct((rows, width), jnp.bfloat16),
        in_specs=[VMEM],
        out_specs=VMEM,
        compiler_params=params,
        cost_estimate=cost(UNIT),
    )(far_value)
    late_keys, late_values = gathered(far_key, bits[1:]), gathered(far_value, bits[1:])
    early = [0, far] + sorted(mask for mask in near_keys if mask)
    late = sorted(mask ^ far for mask in late_keys if mask)
    early_masks = early + [mask ^ 1 for mask in early]
    all_masks = early_masks + late + [mask ^ 1 for mask in late]
    biases = pl.pallas_call(
        functools.partial(bias_kernel, all_masks),
        out_shape=jax.ShapeDtypeStruct((16, len(all_masks) * HD), jnp.float32),
        in_specs=[VMEM] * 2,
        out_specs=VMEM,
        compiler_params=params,
    )(*queries)

    def packed(keys, values, flops, *after):
        held = len(keys)
        return pl.pallas_call(
            functools.partial(pack_kernel, held),
            out_shape=jax.ShapeDtypeStruct((2 * held * rows, width), jnp.bfloat16),
            in_specs=[VMEM] * (2 * held + len(after)),
            out_specs=VMEM,
            compiler_params=params,
            cost_estimate=cost(flops),
        )(*keys, *values, *after)

    near_keys[far], near_values[far] = far_key, far_value
    early_pack = packed(
        [near_keys[mask] for mask in early], [near_values[mask] for mask in early], 0
    )

    def step(first, pack, *state):
        return pl.pallas_call(
            functools.partial(step_kernel, first),
            out_shape=[
                jax.ShapeDtypeStruct((2 * rows, width), jnp.float32),
                jax.ShapeDtypeStruct((2 * rows, 2 * width), jnp.float32),
            ],
            in_specs=[VMEM] * (4 + len(state)),
            out_specs=[VMEM] * 2,
            compiler_params=params,
        )(*queries, biases, pack, *state)

    state = step(0, early_pack)
    late_pack = packed(
        [late_keys[mask ^ far] for mask in late],
        [late_values[mask ^ far] for mask in late],
        12 * UNIT,
        state[1],
    )
    state = step(len(early), exchange(early_pack, 1), *state)
    state = step(2 * len(early), late_pack, *state)
    last_pack = exchange(late_pack, 1)

    def last(place, out_shape):
        return pl.pallas_call(
            functools.partial(last_attention, place),
            out_shape=out_shape,
            in_specs=[VMEM] * 5,
            out_specs=[VMEM] * len(out_shape),
            compiler_params=params,
        )(queries[place], biases, last_pack, *state)

    (packet,) = last(1, [jax.ShapeDtypeStruct((rows + EXTRA, width), jnp.bfloat16)])
    own, own_lines = last(
        0,
        [
            jax.ShapeDtypeStruct((rows, width), jnp.float32),
            jax.ShapeDtypeStruct((16, width), jnp.float32),
        ],
    )
    gates = pl.pallas_call(
        gate_kernel,
        out_shape=jax.ShapeDtypeStruct((16, width), jnp.float32),
        in_specs=[SMEM, VMEM],
        out_specs=VMEM,
        compiler_params=params,
    )(frame_step, gate_table)
    packet = exchange(packet, query_mask)

    return pl.pallas_call(
        merge_kernel,
        out_shape=jax.ShapeDtypeStruct((rows, width), jnp.bfloat16),
        in_specs=[VMEM] * 4,
        out_specs=VMEM,
        compiler_params=params,
    )(own, own_lines, packet, gates)


def solution(mesh):
    return jax.shard_map(
        local,
        mesh=mesh,
        in_specs=(
            P("tm", "head"),
            P("tm", "head"),
            P("tm", "head"),
            P("head"),
            P("head"),
            P(None, "head"),
            P(),
            P("tm", None),
        ),
        out_specs=P("tm", "head"),
        check_vma=False,
    )
```

```python
import functools

import jax
import jax.numpy as jnp
from jax import lax
from jax.experimental import pallas as pl
from jax.experimental.pallas import tpu as pltpu
from jax.sharding import PartitionSpec as P

HD = 128
BLK = 64
FRAME_TOK = 1560
EPSILON = 1e-06
LOG2E = 1.4426950408889634
SCALE = HD ** (-0.5) * LOG2E
MASKED = -1e30
EXTRA = 16
UNIT = 10**9
ANY = pl.BlockSpec(memory_space=pl.ANY)
VMEM = pl.BlockSpec(memory_space=pltpu.VMEM)
SMEM = pl.BlockSpec(memory_space=pltpu.SMEM)


def spread(row):
    return jnp.broadcast_to(row, (row.shape[1], row.shape[1])).T


def factor_of(line, full_width):
    return spread(lax.rsqrt(line / full_width + EPSILON))


def normed(source_ref, factor, gain_ref):
    parts = []
    for low in range(0, source_ref.shape[1], HD):
        wide = source_ref[:HD, low : low + HD].astype(jnp.float32)
        parts.append((wide * factor * gain_ref[:, low : low + HD]).astype(jnp.bfloat16))
    return jnp.concatenate(parts, axis=1)


def key_kernel(full_width, key_ref, gain_ref, own_ref, other_ref, out_ref):
    total = own_ref[1:2, :] + other_ref[1:2, :]
    out_ref[...] = normed(key_ref, factor_of(total, full_width), gain_ref)


def query_kernel(
    full_width,
    query_ref,
    gain_ref,
    far_ref,
    own_ref,
    other_ref,
    query_out,
):
    total = own_ref[0:1, :] + other_ref[0:1, :]
    query_out[:HD, :] = normed(query_ref, factor_of(total, full_width), gain_ref)
    far = far_ref[...].astype(jnp.float32)
    far = jnp.concatenate([far, jnp.full((1, HD - far.shape[1]), -1.0)], axis=1)
    query_out[HD:, :HD] = jnp.broadcast_to(far, (EXTRA, HD)).astype(jnp.bfloat16)
    query_out[HD:, HD:] = jnp.zeros((EXTRA, query_out.shape[1] - HD), jnp.bfloat16)


def bias_kernel(key_masks, own_ref, remote_ref, bias_out):
    me = lax.axis_index("tm")
    query_mask = lax.axis_size("tm") // 4
    lane = lax.broadcasted_iota(jnp.int32, (1, HD), 1)
    half = (lane >= BLK).astype(jnp.float32)
    for place, query_ref in enumerate((own_ref, remote_ref)):
        far = query_ref[HD:, :HD].astype(jnp.float32)[:1]
        query_id = me ^ (place * query_mask)
        for block, key_mask in enumerate(key_masks):
            key_id = me ^ key_mask
            choice = jnp.sum(jnp.where(lane == key_id, far, 0.0), axis=1, keepdims=True)
            taken = (choice == half) | (jnp.abs(query_id - key_id) <= 1)
            bias_out[8 * place : 8 * place + 8, block * HD : (block + 1) * HD] = (
                jnp.broadcast_to(jnp.where(taken, 0.0, MASKED), (8, HD))
            )


def copy_kernel(source_ref, out_ref):
    out_ref[...] = source_ref[...]


def pack_kernel(held, *refs):
    for place, source_ref in enumerate(refs[: 2 * held]):
        refs[-1][place * HD : (place + 1) * HD, :] = source_ref[...]


def absorb(queries, pack_ref, biases, olds):
    half = pack_ref.shape[0] // 2
    heads, count = len(queries), len(biases)
    scores = []
    for head, query in enumerate(queries):
        scores.append(
            lax.dot_general(
                query,
                pack_ref[:half, head * HD : (head + 1) * HD],
                (((1,), (1,)), ((), ())),
                preferred_element_type=jnp.float32,
            )
        )
    spots = [(head, place) for head in range(heads) for place in range(count)]
    logits, tops, weights, totals = {}, {}, {}, {}
    for head, place in spots:
        part = scores[head][place * HD : (place + 1) * HD]
        logits[head, place] = part * SCALE + biases[place]
    for spot in spots:
        top = jnp.broadcast_to(jnp.max(logits[spot], axis=1, keepdims=True), (HD, HD))
        tops[spot] = top if olds is None else jnp.maximum(top, olds[spot][0])
    for spot in spots:
        weights[spot] = [
            jnp.exp2(logits[spot][:, left : left + HD] - tops[spot])
            for left in range(0, half, HD)
        ]
    added = []
    for head in range(heads):
        rounded = [
            jnp.concatenate([w.astype(jnp.bfloat16) for w in weights[head, place]], axis=1)
            for place in range(count)
        ]
        added.append(
            jnp.dot(
                jnp.concatenate(rounded, axis=0),
                pack_ref[half:, head * HD : (head + 1) * HD],
                preferred_element_type=jnp.float32,
            )
        )
    for spot in spots:
        total = jnp.sum(functools.reduce(jnp.add, weights[spot]), axis=1, keepdims=True)
        totals[spot] = jnp.broadcast_to(total, (HD, HD))
    results = {}
    for head, place in spots:
        spot = (head, place)
        context, total = added[head][place * HD : (place + 1) * HD], totals[spot]
        if olds is not None:
            fade = jnp.exp2(olds[spot][0] - tops[spot])
            total = total + olds[spot][1] * fade
            context = context + olds[spot][2] * fade
        results[spot] = (tops[spot], total, context)
    return results


def held_state(context_ref, stats_ref, head, place):
    part, low, wide = slice(place * HD, (place + 1) * HD), head * HD, 2 * head * HD
    return (
        stats_ref[part, wide : wide + HD],
        stats_ref[part, wide + HD : wide + 2 * HD],
        context_ref[part, low : low + HD],
    )


def step_kernel(first, own_ref, remote_ref, bias_ref, pack_ref, *refs):
    olds, (context_out, stats_out) = refs[:-2], refs[-2:]
    heads, keys = own_ref.shape[1] // HD, pack_ref.shape[0] // 2
    left = first * HD
    biases = [bias_ref[8 * place : 8 * place + 1, left : left + keys] for place in range(2)]
    state = None
    if olds:
        state = {
            (head, place): held_state(*olds, head, place)
            for head in range(heads)
            for place in range(2)
        }
    queries = [
        jnp.concatenate([ref[:HD, head * HD : (head + 1) * HD] for ref in (own_ref, remote_ref)])
        for head in range(heads)
    ]
    for (head, place), result in absorb(queries, pack_ref, biases, state).items():
        part, low, wide = slice(place * HD, (place + 1) * HD), head * HD, 2 * head * HD
        top, total, context = result
        context_out[part, low : low + HD] = context
        stats_out[part, wide : wide + HD] = top
        stats_out[part, wide + HD : wide + 2 * HD] = total


def last_attention(place, query_ref, bias_ref, pack_ref, context_ref, stats_ref, *outs):
    heads, keys = query_ref.shape[1] // HD, pack_ref.shape[0] // 2
    part = slice(place * HD, (place + 1) * HD)
    bias = bias_ref[8 * place : 8 * place + 1, bias_ref.shape[1] - keys :]
    lane = lax.broadcasted_iota(jnp.int32, (1, HD), 1)
    state = {(h, 0): held_state(context_ref, stats_ref, h, place) for h in range(heads)}
    queries = [query_ref[:HD, head * HD : (head + 1) * HD] for head in range(heads)]
    results = absorb(queries, pack_ref, [bias], state)
    columns = jnp.zeros((HD, HD), jnp.float32)
    for head in range(heads):
        top, total, context = results[head, 0]
        outs[0][:HD, head * HD : (head + 1) * HD] = context.astype(outs[0].dtype)
        line = 2 * head
        columns = jnp.where(lane == line, top, jnp.where(lane == line + 1, total, columns))
    lines = columns.T
    sub = lax.broadcasted_iota(jnp.int32, (EXTRA, HD), 0)
    for head in range(heads):
        low = head * HD
        pair = (lines[2 * head : 2 * head + 1, :], lines[2 * head + 1 : 2 * head + 2, :])
        if place == 0:
            for row, value in enumerate(pair):
                outs[1][8 * row : 8 * row + 8, low : low + HD] = jnp.broadcast_to(value, (8, HD))
        else:
            piece_rows = jnp.zeros((EXTRA, HD), jnp.float32)
            for row, value in enumerate(pair):
                first = value.astype(jnp.bfloat16).astype(jnp.float32)
                second = (value - first).astype(jnp.bfloat16).astype(jnp.float32)
                for piece, part_value in enumerate((first, second, value - first - second)):
                    piece_rows = jnp.where(sub == 3 * row + piece, part_value, piece_rows)
            outs[0][HD:, low : low + HD] = piece_rows.astype(jnp.bfloat16)


def gate_kernel(step_ref, table_ref, out_ref):
    rows = out_ref.shape[0] // 2
    start = lax.axis_index("tm") * HD
    first = step_ref[start // FRAME_TOK]
    last = step_ref[(start + HD - 1) // FRAME_TOK]
    out_ref[:rows, :] = jnp.broadcast_to(table_ref[pl.ds(first, 1), :], (rows, out_ref.shape[1]))
    out_ref[rows:, :] = jnp.broadcast_to(table_ref[pl.ds(last, 1), :], (rows, out_ref.shape[1]))


def merge_kernel(own_ref, lines_ref, packet_ref, gate_ref, out_ref):
    rows, width = own_ref.shape
    pieces = packet_ref[rows:, :].astype(jnp.float32)
    own_top, own_total = lines_ref[0:1, :], lines_ref[8:9, :]
    other_top = pieces[0:1] + pieces[1:2] + pieces[2:3]
    other_total = pieces[3:4] + pieces[4:5] + pieces[5:6]
    top = jnp.maximum(own_top, other_top)
    own_share, other_share = jnp.exp2(own_top - top), jnp.exp2(other_top - top)
    scale = 1.0 / (own_total * own_share + other_total * other_share)
    own_share, other_share = own_share * scale, other_share * scale
    start = lax.axis_index("tm") * rows
    first_rows = (start // FRAME_TOK + 1) * FRAME_TOK - start
    row_ids = lax.broadcasted_iota(jnp.int32, (rows, 1), 0)
    for low in range(0, width, HD):
        high = low + HD
        context = own_ref[:, low:high] * spread(own_share[:, low:high])
        other = packet_ref[:rows, low:high].astype(jnp.float32)
        context += other * spread(other_share[:, low:high])
        gate = jnp.where(
            row_ids < first_rows, gate_ref[0:1, low:high], gate_ref[8:9, low:high]
        )
        out_ref[:, low:high] = (context * gate).astype(jnp.bfloat16)


def exchange(array, mask):
    count = lax.axis_size("tm")
    return lax.ppermute(array, "tm", [(i, i ^ mask) for i in range(count)])


def gathered(array, bits):
    held = {0: array}
    for bit in bits:
        for mask in list(held):
            held[mask ^ bit] = exchange(held[mask], bit)
    return held


def cost(flops):
    return pl.CostEstimate(flops=flops, bytes_accessed=0, transcendentals=0)


def local(
    query_proj, key_proj, value_proj, query_gain, key_gain, gate_table, frame_step, far_blocks
):
    rows, width = query_proj.shape
    count = lax.axis_size("tm")
    splits = lax.axis_size("head")
    full_width = width * splits
    params = pltpu.CompilerParams(vmem_limit_bytes=(8 + count // 2) * 2**20)
    query_mask = count // 4
    bits = [1 << place for place in range(1, count.bit_length() - 1)]
    bits = [bit for bit in bits[::-1] if bit != query_mask]
    query_gain = query_gain.reshape(1, width)
    key_gain = key_gain.reshape(1, width)

    far = bits[0] | query_mask
    far_value = exchange(value_proj, far)
    query_f, key_f = query_proj.astype(jnp.float32), key_proj.astype(jnp.float32)
    sums = jnp.stack(
        [jnp.sum(query_f * query_f, axis=-1), jnp.sum(key_f * key_f, axis=-1)], axis=0
    )
    if splits == 2:
        others = lax.ppermute(sums, "head", [(0, 1), (1, 0)])
    else:
        sums = lax.psum(sums, "head")
        others = jnp.zeros_like(sums)
    own_key = pl.pallas_call(
        functools.partial(key_kernel, width * splits),
        out_shape=jax.ShapeDtypeStruct((rows, width), jnp.bfloat16),
        in_specs=[VMEM] * 4,
        out_specs=VMEM,
        compiler_params=params,
    )(key_proj, key_gain, sums, others)
    near_values = gathered(value_proj, bits[1:])
    near_keys = gathered(own_key, bits[1:])
    query_packet = pl.pallas_call(
        functools.partial(query_kernel, width * splits),
        out_shape=jax.ShapeDtypeStruct((rows + EXTRA, width), jnp.bfloat16),
        in_specs=[VMEM] * 5,
        out_specs=VMEM,
        compiler_params=params,
    )(query_proj, query_gain, far_blocks, sums, others)
    far_key = exchange(own_key, far)
    queries = [query_packet, exchange(query_packet, query_mask)]
    far_value = pl.pallas_call(
        copy_kernel,
        out_shape=jax.ShapeDtypeStruct((rows, width), jnp.bfloat16),
        in_specs=[VMEM],
        out_specs=VMEM,
        compiler_params=params,
        cost_estimate=cost(4 * UNIT),
    )(far_value)
    late_keys, late_values = gathered(far_key, bits[1:]), gathered(far_value, bits[1:])
    early = [0, far] + sorted(mask for mask in near_keys if mask)
    late = sorted(mask ^ far for mask in late_keys if mask)
    early_masks = early + [mask ^ 1 for mask in early]
    all_masks = early_masks + late + [mask ^ 1 for mask in late]
    biases = pl.pallas_call(
        functools.partial(bias_kernel, all_masks),
        out_shape=jax.ShapeDtypeStruct((16, len(all_masks) * HD), jnp.float32),
        in_specs=[VMEM] * 2,
        out_specs=VMEM,
        compiler_params=params,
    )(*queries)

    def packed(keys, values, flops, *after):
        held = len(keys)
        return pl.pallas_call(
            functools.partial(pack_kernel, held),
            out_shape=jax.ShapeDtypeStruct((2 * held * rows, width), jnp.bfloat16),
            in_specs=[VMEM] * (2 * held + len(after)),
            out_specs=VMEM,
            compiler_params=params,
            cost_estimate=cost(flops),
        )(*keys, *values, *after)

    near_keys[far], near_values[far] = far_key, far_value
    early_pack = packed(
        [near_keys[mask] for mask in early], [near_values[mask] for mask in early], 0
    )

    def step(first, pack, *state):
        return pl.pallas_call(
            functools.partial(step_kernel, first),
            out_shape=[
                jax.ShapeDtypeStruct((2 * rows, width), jnp.float32),
                jax.ShapeDtypeStruct((2 * rows, 2 * width), jnp.float32),
            ],
            in_specs=[VMEM] * (4 + len(state)),
            out_specs=[VMEM] * 2,
            compiler_params=params,
        )(*queries, biases, pack, *state)

    state = step(0, early_pack)
    late_pack = packed(
        [late_keys[mask ^ far] for mask in late],
        [late_values[mask ^ far] for mask in late],
        12 * UNIT,
        state[1],
    )
    state = step(len(early), exchange(early_pack, 1), *state)
    state = step(2 * len(early), late_pack, *state)
    last_pack = exchange(late_pack, 1)

    def last(place, out_shape):
        return pl.pallas_call(
            functools.partial(last_attention, place),
            out_shape=out_shape,
            in_specs=[VMEM] * 5,
            out_specs=[VMEM] * len(out_shape),
            compiler_params=params,
        )(queries[place], biases, last_pack, *state)

    (packet,) = last(1, [jax.ShapeDtypeStruct((rows + EXTRA, width), jnp.bfloat16)])
    own, own_lines = last(
        0,
        [
            jax.ShapeDtypeStruct((rows, width), jnp.float32),
            jax.ShapeDtypeStruct((16, width), jnp.float32),
        ],
    )
    gates = pl.pallas_call(
        gate_kernel,
        out_shape=jax.ShapeDtypeStruct((16, width), jnp.float32),
        in_specs=[SMEM, VMEM],
        out_specs=VMEM,
        compiler_params=params,
    )(frame_step, gate_table)
    packet = exchange(packet, query_mask)

    return pl.pallas_call(
        merge_kernel,
        out_shape=jax.ShapeDtypeStruct((rows, width), jnp.bfloat16),
        in_specs=[VMEM] * 4,
        out_specs=VMEM,
        compiler_params=params,
    )(own, own_lines, packet, gates)


def solution(mesh):
    return jax.shard_map(
        local,
        mesh=mesh,
        in_specs=(
            P("tm", "head"),
            P("tm", "head"),
            P("tm", "head"),
            P("head"),
            P("head"),
            P(None, "head"),
            P(),
            P("tm", None),
        ),
        out_specs=P("tm", "head"),
        check_vma=False,
    )
```

```python
import functools

import jax
import jax.numpy as jnp
from jax import lax
from jax.experimental import pallas as pl
from jax.experimental.pallas import tpu as pltpu
from jax.sharding import PartitionSpec as P

HD = 128
BLK = 64
FRAME_TOK = 1560
EPSILON = 1e-06
LOG2E = 1.4426950408889634
SCALE = HD ** (-0.5) * LOG2E
MASKED = -1e30
EXTRA = 16
UNIT = 10**9
ANY = pl.BlockSpec(memory_space=pl.ANY)
VMEM = pl.BlockSpec(memory_space=pltpu.VMEM)
SMEM = pl.BlockSpec(memory_space=pltpu.SMEM)


def spread(row):
    return jnp.broadcast_to(row, (row.shape[1], row.shape[1])).T


def factor_of(line, full_width):
    return spread(lax.rsqrt(line / full_width + EPSILON))


def normed(source_ref, factor, gain_ref):
    parts = []
    for low in range(0, source_ref.shape[1], HD):
        wide = source_ref[:HD, low : low + HD].astype(jnp.float32)
        parts.append((wide * factor * gain_ref[:, low : low + HD]).astype(jnp.bfloat16))
    return jnp.concatenate(parts, axis=1)


def key_kernel(full_width, key_ref, gain_ref, own_ref, other_ref, out_ref):
    total = own_ref[1:2, :] + other_ref[1:2, :]
    out_ref[...] = normed(key_ref, factor_of(total, full_width), gain_ref)


def query_kernel(
    full_width,
    query_ref,
    gain_ref,
    far_ref,
    own_ref,
    other_ref,
    query_out,
):
    total = own_ref[0:1, :] + other_ref[0:1, :]
    query_out[:HD, :] = normed(query_ref, factor_of(total, full_width), gain_ref)
    far = far_ref[...].astype(jnp.float32)
    far = jnp.concatenate([far, jnp.full((1, HD - far.shape[1]), -1.0)], axis=1)
    query_out[HD:, :HD] = jnp.broadcast_to(far, (EXTRA, HD)).astype(jnp.bfloat16)
    query_out[HD:, HD:] = jnp.zeros((EXTRA, query_out.shape[1] - HD), jnp.bfloat16)


def bias_kernel(key_masks, own_ref, remote_ref, bias_out):
    me = lax.axis_index("tm")
    query_mask = lax.axis_size("tm") // 4
    lane = lax.broadcasted_iota(jnp.int32, (1, HD), 1)
    half = (lane >= BLK).astype(jnp.float32)
    for place, query_ref in enumerate((own_ref, remote_ref)):
        far = query_ref[HD:, :HD].astype(jnp.float32)[:1]
        query_id = me ^ (place * query_mask)
        for block, key_mask in enumerate(key_masks):
            key_id = me ^ key_mask
            choice = jnp.sum(jnp.where(lane == key_id, far, 0.0), axis=1, keepdims=True)
            taken = (choice == half) | (jnp.abs(query_id - key_id) <= 1)
            bias_out[8 * place : 8 * place + 8, block * HD : (block + 1) * HD] = (
                jnp.broadcast_to(jnp.where(taken, 0.0, MASKED), (8, HD))
            )


def copy_kernel(source_ref, out_ref):
    out_ref[...] = source_ref[...]


def pack_kernel(held, *refs):
    for place, source_ref in enumerate(refs[: 2 * held]):
        refs[-1][place * HD : (place + 1) * HD, :] = source_ref[...]


def absorb(queries, pack_ref, biases, olds):
    half = pack_ref.shape[0] // 2
    heads, count = len(queries), len(biases)
    scores = []
    for head, query in enumerate(queries):
        scores.append(
            lax.dot_general(
                query,
                pack_ref[:half, head * HD : (head + 1) * HD],
                (((1,), (1,)), ((), ())),
                preferred_element_type=jnp.float32,
            )
        )
    spots = [(head, place) for head in range(heads) for place in range(count)]
    logits, tops, weights, totals = {}, {}, {}, {}
    for head, place in spots:
        part = scores[head][place * HD : (place + 1) * HD]
        logits[head, place] = part * SCALE + biases[place]
    for spot in spots:
        top = jnp.broadcast_to(jnp.max(logits[spot], axis=1, keepdims=True), (HD, HD))
        tops[spot] = top if olds is None else jnp.maximum(top, olds[spot][0])
    for spot in spots:
        weights[spot] = [
            jnp.exp2(logits[spot][:, left : left + HD] - tops[spot])
            for left in range(0, half, HD)
        ]
    added = []
    for head in range(heads):
        rounded = [
            jnp.concatenate([w.astype(jnp.bfloat16) for w in weights[head, place]], axis=1)
            for place in range(count)
        ]
        added.append(
            jnp.dot(
                jnp.concatenate(rounded, axis=0),
                pack_ref[half:, head * HD : (head + 1) * HD],
                preferred_element_type=jnp.float32,
            )
        )
    for spot in spots:
        total = jnp.sum(functools.reduce(jnp.add, weights[spot]), axis=1, keepdims=True)
        totals[spot] = jnp.broadcast_to(total, (HD, HD))
    results = {}
    for head, place in spots:
        spot = (head, place)
        context, total = added[head][place * HD : (place + 1) * HD], totals[spot]
        if olds is not None:
            fade = jnp.exp2(olds[spot][0] - tops[spot])
            total = total + olds[spot][1] * fade
            context = context + olds[spot][2] * fade
        results[spot] = (tops[spot], total, context)
    return results


def held_state(context_ref, stats_ref, head, place):
    part, low, wide = slice(place * HD, (place + 1) * HD), head * HD, 2 * head * HD
    return (
        stats_ref[part, wide : wide + HD],
        stats_ref[part, wide + HD : wide + 2 * HD],
        context_ref[part, low : low + HD],
    )


def step_kernel(first, own_ref, remote_ref, bias_ref, pack_ref, *refs):
    olds, (context_out, stats_out) = refs[:-2], refs[-2:]
    heads, keys = own_ref.shape[1] // HD, pack_ref.shape[0] // 2
    left = first * HD
    biases = [bias_ref[8 * place : 8 * place + 1, left : left + keys] for place in range(2)]
    state = None
    if olds:
        state = {
            (head, place): held_state(*olds, head, place)
            for head in range(heads)
            for place in range(2)
        }
    queries = [
        jnp.concatenate([ref[:HD, head * HD : (head + 1) * HD] for ref in (own_ref, remote_ref)])
        for head in range(heads)
    ]
    for (head, place), result in absorb(queries, pack_ref, biases, state).items():
        part, low, wide = slice(place * HD, (place + 1) * HD), head * HD, 2 * head * HD
        top, total, context = result
        context_out[part, low : low + HD] = context
        stats_out[part, wide : wide + HD] = top
        stats_out[part, wide + HD : wide + 2 * HD] = total


def last_attention(place, query_ref, bias_ref, pack_ref, context_ref, stats_ref, *outs):
    heads, keys = query_ref.shape[1] // HD, pack_ref.shape[0] // 2
    part = slice(place * HD, (place + 1) * HD)
    bias = bias_ref[8 * place : 8 * place + 1, bias_ref.shape[1] - keys :]
    lane = lax.broadcasted_iota(jnp.int32, (1, HD), 1)
    state = {(h, 0): held_state(context_ref, stats_ref, h, place) for h in range(heads)}
    queries = [query_ref[:HD, head * HD : (head + 1) * HD] for head in range(heads)]
    results = absorb(queries, pack_ref, [bias], state)
    columns = jnp.zeros((HD, HD), jnp.float32)
    for head in range(heads):
        top, total, context = results[head, 0]
        outs[0][:HD, head * HD : (head + 1) * HD] = context.astype(outs[0].dtype)
        line = 2 * head
        columns = jnp.where(lane == line, top, jnp.where(lane == line + 1, total, columns))
    lines = columns.T
    sub = lax.broadcasted_iota(jnp.int32, (EXTRA, HD), 0)
    for head in range(heads):
        low = head * HD
        pair = (lines[2 * head : 2 * head + 1, :], lines[2 * head + 1 : 2 * head + 2, :])
        if place == 0:
            for row, value in enumerate(pair):
                outs[1][8 * row : 8 * row + 8, low : low + HD] = jnp.broadcast_to(value, (8, HD))
        else:
            piece_rows = jnp.zeros((EXTRA, HD), jnp.float32)
            for row, value in enumerate(pair):
                first = value.astype(jnp.bfloat16).astype(jnp.float32)
                second = (value - first).astype(jnp.bfloat16).astype(jnp.float32)
                for piece, part_value in enumerate((first, second, value - first - second)):
                    piece_rows = jnp.where(sub == 3 * row + piece, part_value, piece_rows)
            outs[0][HD:, low : low + HD] = piece_rows.astype(jnp.bfloat16)


def gate_kernel(step_ref, table_ref, out_ref):
    rows = out_ref.shape[0] // 2
    start = lax.axis_index("tm") * HD
    first = step_ref[start // FRAME_TOK]
    last = step_ref[(start + HD - 1) // FRAME_TOK]
    out_ref[:rows, :] = jnp.broadcast_to(table_ref[pl.ds(first, 1), :], (rows, out_ref.shape[1]))
    out_ref[rows:, :] = jnp.broadcast_to(table_ref[pl.ds(last, 1), :], (rows, out_ref.shape[1]))


def merge_kernel(own_ref, lines_ref, packet_ref, gate_ref, out_hbm, out_ref, sems):
    rows, width = own_ref.shape
    pieces = packet_ref[rows:, :].astype(jnp.float32)
    own_top, own_total = lines_ref[0:1, :], lines_ref[8:9, :]
    other_top = pieces[0:1] + pieces[1:2] + pieces[2:3]
    other_total = pieces[3:4] + pieces[4:5] + pieces[5:6]
    top = jnp.maximum(own_top, other_top)
    own_share, other_share = jnp.exp2(own_top - top), jnp.exp2(other_top - top)
    scale = 1.0 / (own_total * own_share + other_total * other_share)
    own_share, other_share = own_share * scale, other_share * scale
    start = lax.axis_index("tm") * rows
    first_rows = (start // FRAME_TOK + 1) * FRAME_TOK - start
    row_ids = lax.broadcasted_iota(jnp.int32, (rows, 1), 0)
    copies = []
    for low in range(0, width, HD):
        high = low + HD
        context = own_ref[:, low:high] * spread(own_share[:, low:high])
        other = packet_ref[:rows, low:high].astype(jnp.float32)
        context += other * spread(other_share[:, low:high])
        gate = jnp.where(
            row_ids < first_rows, gate_ref[0:1, low:high], gate_ref[8:9, low:high]
        )
        out_ref[:, low:high] = (context * gate).astype(jnp.bfloat16)
        part = (slice(None), pl.ds(low, HD))
        copy = pltpu.make_async_copy(out_ref.at[part], out_hbm.at[part], sems.at[low // HD])
        copy.start()
        copies.append(copy)
    for copy in copies:
        copy.wait()


def exchange(array, mask):
    count = lax.axis_size("tm")
    return lax.ppermute(array, "tm", [(i, i ^ mask) for i in range(count)])


def gathered(array, bits):
    held = {0: array}
    for bit in bits:
        for mask in list(held):
            held[mask ^ bit] = exchange(held[mask], bit)
    return held


def cost(flops):
    return pl.CostEstimate(flops=flops, bytes_accessed=0, transcendentals=0)


def local(
    query_proj, key_proj, value_proj, query_gain, key_gain, gate_table, frame_step, far_blocks
):
    rows, width = query_proj.shape
    count = lax.axis_size("tm")
    splits = lax.axis_size("head")
    full_width = width * splits
    params = pltpu.CompilerParams(vmem_limit_bytes=(8 + count // 2) * 2**20)
    query_mask = count // 4
    bits = [1 << place for place in range(1, count.bit_length() - 1)]
    bits = [bit for bit in bits[::-1] if bit != query_mask]
    query_gain = query_gain.reshape(1, width)
    key_gain = key_gain.reshape(1, width)

    far = bits[0]
    far_value = exchange(value_proj, far)
    query_f, key_f = query_proj.astype(jnp.float32), key_proj.astype(jnp.float32)
    sums = jnp.stack(
        [jnp.sum(query_f * query_f, axis=-1), jnp.sum(key_f * key_f, axis=-1)], axis=0
    )
    if splits == 2:
        others = lax.ppermute(sums, "head", [(0, 1), (1, 0)])
    else:
        sums = lax.psum(sums, "head")
        others = jnp.zeros_like(sums)
    own_key = pl.pallas_call(
        functools.partial(key_kernel, width * splits),
        out_shape=jax.ShapeDtypeStruct((rows, width), jnp.bfloat16),
        in_specs=[VMEM] * 4,
        out_specs=VMEM,
        compiler_params=params,
    )(key_proj, key_gain, sums, others)
    near_values = gathered(value_proj, bits[1:])
    near_keys = gathered(own_key, bits[1:])
    query_packet = pl.pallas_call(
        functools.partial(query_kernel, width * splits),
        out_shape=jax.ShapeDtypeStruct((rows + EXTRA, width), jnp.bfloat16),
        in_specs=[VMEM] * 5,
        out_specs=VMEM,
        compiler_params=params,
    )(query_proj, query_gain, far_blocks, sums, others)
    far_key = exchange(own_key, far)
    queries = [query_packet, exchange(query_packet, query_mask)]
    far_value = pl.pallas_call(
        copy_kernel,
        out_shape=jax.ShapeDtypeStruct((rows, width), jnp.bfloat16),
        in_specs=[VMEM],
        out_specs=VMEM,
        compiler_params=params,
        cost_estimate=cost(4 * UNIT),
    )(far_value)
    late_keys, late_values = gathered(far_key, bits[1:]), gathered(far_value, bits[1:])
    early = [0, far] + sorted(mask for mask in near_keys if mask)
    late = sorted(mask ^ far for mask in late_keys if mask)
    early_masks = early + [mask ^ 1 for mask in early]
    all_masks = early_masks + late + [mask ^ 1 for mask in late]
    biases = pl.pallas_call(
        functools.partial(bias_kernel, all_masks),
        out_shape=jax.ShapeDtypeStruct((16, len(all_masks) * HD), jnp.float32),
        in_specs=[VMEM] * 2,
        out_specs=VMEM,
        compiler_params=params,
    )(*queries)

    def packed(keys, values, flops, *after):
        held = len(keys)
        return pl.pallas_call(
            functools.partial(pack_kernel, held),
            out_shape=jax.ShapeDtypeStruct((2 * held * rows, width), jnp.bfloat16),
            in_specs=[VMEM] * (2 * held + len(after)),
            out_specs=VMEM,
            compiler_params=params,
            cost_estimate=cost(flops),
        )(*keys, *values, *after)

    near_keys[far], near_values[far] = far_key, far_value
    early_pack = packed(
        [near_keys[mask] for mask in early], [near_values[mask] for mask in early], 0
    )

    def step(first, pack, *state):
        return pl.pallas_call(
            functools.partial(step_kernel, first),
            out_shape=[
                jax.ShapeDtypeStruct((2 * rows, width), jnp.float32),
                jax.ShapeDtypeStruct((2 * rows, 2 * width), jnp.float32),
            ],
            in_specs=[VMEM] * (4 + len(state)),
            out_specs=[VMEM] * 2,
            compiler_params=params,
        )(*queries, biases, pack, *state)

    state = step(0, early_pack)
    late_pack = packed(
        [late_keys[mask ^ far] for mask in late],
        [late_values[mask ^ far] for mask in late],
        12 * UNIT,
        state[1],
    )
    state = step(len(early), exchange(early_pack, 1), *state)
    state = step(2 * len(early), late_pack, *state)
    last_pack = exchange(late_pack, 1)

    def last(place, out_shape):
        return pl.pallas_call(
            functools.partial(last_attention, place),
            out_shape=out_shape,
            in_specs=[VMEM] * 5,
            out_specs=[VMEM] * len(out_shape),
            compiler_params=params,
        )(queries[place], biases, last_pack, *state)

    (packet,) = last(1, [jax.ShapeDtypeStruct((rows + EXTRA, width), jnp.bfloat16)])
    own, own_lines = last(
        0,
        [
            jax.ShapeDtypeStruct((rows, width), jnp.float32),
            jax.ShapeDtypeStruct((16, width), jnp.float32),
        ],
    )
    gates = pl.pallas_call(
        gate_kernel,
        out_shape=jax.ShapeDtypeStruct((16, width), jnp.float32),
        in_specs=[SMEM, VMEM],
        out_specs=VMEM,
        compiler_params=params,
    )(frame_step, gate_table)
    packet = exchange(packet, query_mask)

    return pl.pallas_call(
        merge_kernel,
        out_shape=jax.ShapeDtypeStruct((rows, width), jnp.bfloat16),
        in_specs=[VMEM] * 4,
        out_specs=ANY,
        scratch_shapes=[
            pltpu.VMEM((rows, width), jnp.bfloat16),
            pltpu.SemaphoreType.DMA((width // HD,)),
        ],
        compiler_params=params,
    )(own, own_lines, packet, gates)


def solution(mesh):
    return jax.shard_map(
        local,
        mesh=mesh,
        in_specs=(
            P("tm", "head"),
            P("tm", "head"),
            P("tm", "head"),
            P("head"),
            P("head"),
            P(None, "head"),
            P(),
            P("tm", None),
        ),
        out_specs=P("tm", "head"),
        check_vma=False,
    )
```

```python
import functools

import jax
import jax.numpy as jnp
from jax import lax
from jax.experimental import pallas as pl
from jax.experimental.pallas import tpu as pltpu
from jax.sharding import PartitionSpec as P

HD = 128
BLK = 64
FRAME_TOK = 1560
EPSILON = 1e-06
LOG2E = 1.4426950408889634
SCALE = HD ** (-0.5) * LOG2E
MASKED = -1e30
EXTRA = 16
UNIT = 10**9
ANY = pl.BlockSpec(memory_space=pl.ANY)
VMEM = pl.BlockSpec(memory_space=pltpu.VMEM)
SMEM = pl.BlockSpec(memory_space=pltpu.SMEM)


def spread(row):
    return jnp.broadcast_to(row, (row.shape[1], row.shape[1])).T


def factor_of(line, full_width):
    return spread(lax.rsqrt(line / full_width + EPSILON))


def normed(source_ref, factor, gain_ref):
    parts = []
    for low in range(0, source_ref.shape[1], HD):
        wide = source_ref[:HD, low : low + HD].astype(jnp.float32)
        parts.append((wide * factor * gain_ref[:, low : low + HD]).astype(jnp.bfloat16))
    return jnp.concatenate(parts, axis=1)


def key_kernel(full_width, key_ref, gain_ref, own_ref, other_ref, out_ref):
    total = own_ref[1:2, :] + other_ref[1:2, :]
    out_ref[...] = normed(key_ref, factor_of(total, full_width), gain_ref)


def query_kernel(
    full_width,
    query_ref,
    gain_ref,
    far_ref,
    own_ref,
    other_ref,
    query_out,
):
    total = own_ref[0:1, :] + other_ref[0:1, :]
    query_out[:HD, :] = normed(query_ref, factor_of(total, full_width), gain_ref)
    far = far_ref[...].astype(jnp.float32)
    far = jnp.concatenate([far, jnp.full((1, HD - far.shape[1]), -1.0)], axis=1)
    query_out[HD:, :HD] = jnp.broadcast_to(far, (EXTRA, HD)).astype(jnp.bfloat16)
    query_out[HD:, HD:] = jnp.zeros((EXTRA, query_out.shape[1] - HD), jnp.bfloat16)


def bias_kernel(key_masks, own_ref, remote_ref, bias_out):
    me = lax.axis_index("tm")
    query_mask = lax.axis_size("tm") // 4
    lane = lax.broadcasted_iota(jnp.int32, (1, HD), 1)
    half = (lane >= BLK).astype(jnp.float32)
    for place, query_ref in enumerate((own_ref, remote_ref)):
        far = query_ref[HD:, :HD].astype(jnp.float32)[:1]
        query_id = me ^ (place * query_mask)
        for block, key_mask in enumerate(key_masks):
            key_id = me ^ key_mask
            choice = jnp.sum(jnp.where(lane == key_id, far, 0.0), axis=1, keepdims=True)
            taken = (choice == half) | (jnp.abs(query_id - key_id) <= 1)
            bias_out[8 * place : 8 * place + 8, block * HD : (block + 1) * HD] = (
                jnp.broadcast_to(jnp.where(taken, 0.0, MASKED), (8, HD))
            )


def copy_kernel(source_ref, out_ref):
    out_ref[...] = source_ref[...]


def pack_kernel(held, *refs):
    for place, source_ref in enumerate(refs[: 2 * held]):
        refs[-1][place * HD : (place + 1) * HD, :] = source_ref[...]


def absorb(queries, pack_ref, biases, olds):
    half = pack_ref.shape[0] // 2
    heads, count = len(queries), len(biases)
    scores = []
    for head, query in enumerate(queries):
        scores.append(
            lax.dot_general(
                query,
                pack_ref[:half, head * HD : (head + 1) * HD],
                (((1,), (1,)), ((), ())),
                preferred_element_type=jnp.float32,
            )
        )
    spots = [(head, place) for head in range(heads) for place in range(count)]
    logits, tops, weights, totals = {}, {}, {}, {}
    for head, place in spots:
        part = scores[head][place * HD : (place + 1) * HD]
        logits[head, place] = part * SCALE + biases[place]
    for spot in spots:
        top = jnp.broadcast_to(jnp.max(logits[spot], axis=1, keepdims=True), (HD, HD))
        tops[spot] = top if olds is None else jnp.maximum(top, olds[spot][0])
    for spot in spots:
        weights[spot] = [
            jnp.exp2(logits[spot][:, left : left + HD] - tops[spot])
            for left in range(0, half, HD)
        ]
    added = []
    for head in range(heads):
        rounded = [
            jnp.concatenate([w.astype(jnp.bfloat16) for w in weights[head, place]], axis=1)
            for place in range(count)
        ]
        added.append(
            jnp.dot(
                jnp.concatenate(rounded, axis=0),
                pack_ref[half:, head * HD : (head + 1) * HD],
                preferred_element_type=jnp.float32,
            )
        )
    for spot in spots:
        total = jnp.sum(functools.reduce(jnp.add, weights[spot]), axis=1, keepdims=True)
        totals[spot] = jnp.broadcast_to(total, (HD, HD))
    results = {}
    for head, place in spots:
        spot = (head, place)
        context, total = added[head][place * HD : (place + 1) * HD], totals[spot]
        if olds is not None:
            fade = jnp.exp2(olds[spot][0] - tops[spot])
            total = total + olds[spot][1] * fade
            context = context + olds[spot][2] * fade
        results[spot] = (tops[spot], total, context)
    return results


def held_state(context_ref, stats_ref, head, place):
    part, low, wide = slice(place * HD, (place + 1) * HD), head * HD, 2 * head * HD
    return (
        stats_ref[part, wide : wide + HD],
        stats_ref[part, wide + HD : wide + 2 * HD],
        context_ref[part, low : low + HD],
    )


def step_kernel(first, own_ref, remote_ref, bias_ref, pack_ref, *refs):
    olds, (context_out, stats_out) = refs[:-2], refs[-2:]
    heads, keys = own_ref.shape[1] // HD, pack_ref.shape[0] // 2
    left = first * HD
    biases = [bias_ref[8 * place : 8 * place + 1, left : left + keys] for place in range(2)]
    state = None
    if olds:
        state = {
            (head, place): held_state(*olds, head, place)
            for head in range(heads)
            for place in range(2)
        }
    queries = [
        jnp.concatenate([ref[:HD, head * HD : (head + 1) * HD] for ref in (own_ref, remote_ref)])
        for head in range(heads)
    ]
    for (head, place), result in absorb(queries, pack_ref, biases, state).items():
        part, low, wide = slice(place * HD, (place + 1) * HD), head * HD, 2 * head * HD
        top, total, context = result
        context_out[part, low : low + HD] = context
        stats_out[part, wide : wide + HD] = top
        stats_out[part, wide + HD : wide + 2 * HD] = total


def last_attention(place, query_ref, bias_ref, pack_ref, context_ref, stats_ref, *outs):
    heads, keys = query_ref.shape[1] // HD, pack_ref.shape[0] // 2
    part = slice(place * HD, (place + 1) * HD)
    bias = bias_ref[8 * place : 8 * place + 1, bias_ref.shape[1] - keys :]
    lane = lax.broadcasted_iota(jnp.int32, (1, HD), 1)
    state = {(h, 0): held_state(context_ref, stats_ref, h, place) for h in range(heads)}
    queries = [query_ref[:HD, head * HD : (head + 1) * HD] for head in range(heads)]
    results = absorb(queries, pack_ref, [bias], state)
    columns = jnp.zeros((HD, HD), jnp.float32)
    for head in range(heads):
        top, total, context = results[head, 0]
        outs[0][:HD, head * HD : (head + 1) * HD] = context.astype(outs[0].dtype)
        line = 2 * head
        columns = jnp.where(lane == line, top, jnp.where(lane == line + 1, total, columns))
    lines = columns.T
    sub = lax.broadcasted_iota(jnp.int32, (EXTRA, HD), 0)
    for head in range(heads):
        low = head * HD
        pair = (lines[2 * head : 2 * head + 1, :], lines[2 * head + 1 : 2 * head + 2, :])
        if place == 0:
            for row, value in enumerate(pair):
                outs[1][8 * row : 8 * row + 8, low : low + HD] = jnp.broadcast_to(value, (8, HD))
        else:
            piece_rows = jnp.zeros((EXTRA, HD), jnp.float32)
            for row, value in enumerate(pair):
                first = value.astype(jnp.bfloat16).astype(jnp.float32)
                second = (value - first).astype(jnp.bfloat16).astype(jnp.float32)
                for piece, part_value in enumerate((first, second, value - first - second)):
                    piece_rows = jnp.where(sub == 3 * row + piece, part_value, piece_rows)
            outs[0][HD:, low : low + HD] = piece_rows.astype(jnp.bfloat16)


def gate_kernel(step_ref, table_ref, out_ref):
    rows = out_ref.shape[0] // 2
    start = lax.axis_index("tm") * HD
    first = step_ref[start // FRAME_TOK]
    last = step_ref[(start + HD - 1) // FRAME_TOK]
    out_ref[:rows, :] = jnp.broadcast_to(table_ref[pl.ds(first, 1), :], (rows, out_ref.shape[1]))
    out_ref[rows:, :] = jnp.broadcast_to(table_ref[pl.ds(last, 1), :], (rows, out_ref.shape[1]))


def merge_kernel(own_ref, lines_ref, packet_ref, gate_ref, out_hbm, out_ref, sems):
    rows, width = own_ref.shape
    pieces = packet_ref[rows:, :].astype(jnp.float32)
    own_top, own_total = lines_ref[0:1, :], lines_ref[8:9, :]
    other_top = pieces[0:1] + pieces[1:2] + pieces[2:3]
    other_total = pieces[3:4] + pieces[4:5] + pieces[5:6]
    top = jnp.maximum(own_top, other_top)
    own_share, other_share = jnp.exp2(own_top - top), jnp.exp2(other_top - top)
    scale = 1.0 / (own_total * own_share + other_total * other_share)
    own_share, other_share = own_share * scale, other_share * scale
    shares = [share[:, low : low + HD] for share in (own_share, other_share) for low in range(0, width, HD)]
    shares += [jnp.zeros((1, HD), jnp.float32)] * (-len(shares) % 8)
    columns = jnp.concatenate(shares, axis=0).T
    start = lax.axis_index("tm") * rows
    first_rows = (start // FRAME_TOK + 1) * FRAME_TOK - start
    row_ids = lax.broadcasted_iota(jnp.int32, (rows, 1), 0)
    copies = []
    for low in range(0, width, HD):
        high = low + HD
        context = own_ref[:, low:high] * columns[:, low // HD : low // HD + 1]
        other = packet_ref[:rows, low:high].astype(jnp.float32)
        spot = (width + low) // HD
        context += other * columns[:, spot : spot + 1]
        gate = jnp.where(
            row_ids < first_rows, gate_ref[0:1, low:high], gate_ref[8:9, low:high]
        )
        out_ref[:, low:high] = (context * gate).astype(jnp.bfloat16)
        part = (slice(None), pl.ds(low, HD))
        copy = pltpu.make_async_copy(out_ref.at[part], out_hbm.at[part], sems.at[low // HD])
        copy.start()
        copies.append(copy)
    for copy in copies:
        copy.wait()


def exchange(array, mask):
    count = lax.axis_size("tm")
    return lax.ppermute(array, "tm", [(i, i ^ mask) for i in range(count)])


def gathered(array, bits):
    held = {0: array}
    for bit in bits:
        for mask in list(held):
            held[mask ^ bit] = exchange(held[mask], bit)
    return held


def cost(flops):
    return pl.CostEstimate(flops=flops, bytes_accessed=0, transcendentals=0)


def local(
    query_proj, key_proj, value_proj, query_gain, key_gain, gate_table, frame_step, far_blocks
):
    rows, width = query_proj.shape
    count = lax.axis_size("tm")
    splits = lax.axis_size("head")
    full_width = width * splits
    params = pltpu.CompilerParams(vmem_limit_bytes=(8 + count // 2) * 2**20)
    query_mask = count // 4
    bits = [1 << place for place in range(1, count.bit_length() - 1)]
    bits = [bit for bit in bits[::-1] if bit != query_mask]
    query_gain = query_gain.reshape(1, width)
    key_gain = key_gain.reshape(1, width)

    far = bits[0]
    far_value = exchange(value_proj, far)
    query_f, key_f = query_proj.astype(jnp.float32), key_proj.astype(jnp.float32)
    sums = jnp.stack(
        [jnp.sum(query_f * query_f, axis=-1), jnp.sum(key_f * key_f, axis=-1)], axis=0
    )
    if splits == 2:
        others = lax.ppermute(sums, "head", [(0, 1), (1, 0)])
    else:
        sums = lax.psum(sums, "head")
        others = jnp.zeros_like(sums)
    own_key = pl.pallas_call(
        functools.partial(key_kernel, width * splits),
        out_shape=jax.ShapeDtypeStruct((rows, width), jnp.bfloat16),
        in_specs=[VMEM] * 4,
        out_specs=VMEM,
        compiler_params=params,
    )(key_proj, key_gain, sums, others)
    near_values = gathered(value_proj, bits[1:])
    near_keys = gathered(own_key, bits[1:])
    query_packet = pl.pallas_call(
        functools.partial(query_kernel, width * splits),
        out_shape=jax.ShapeDtypeStruct((rows + EXTRA, width), jnp.bfloat16),
        in_specs=[VMEM] * 5,
        out_specs=VMEM,
        compiler_params=params,
    )(query_proj, query_gain, far_blocks, sums, others)
    far_key = exchange(own_key, far)
    queries = [query_packet, exchange(query_packet, query_mask)]
    far_value = pl.pallas_call(
        copy_kernel,
        out_shape=jax.ShapeDtypeStruct((rows, width), jnp.bfloat16),
        in_specs=[VMEM],
        out_specs=VMEM,
        compiler_params=params,
        cost_estimate=cost(4 * UNIT),
    )(far_value)
    late_keys, late_values = gathered(far_key, bits[1:]), gathered(far_value, bits[1:])
    early = [0, far] + sorted(mask for mask in near_keys if mask)
    late = sorted(mask ^ far for mask in late_keys if mask)
    early_masks = early + [mask ^ 1 for mask in early]
    all_masks = early_masks + late + [mask ^ 1 for mask in late]
    biases = pl.pallas_call(
        functools.partial(bias_kernel, all_masks),
        out_shape=jax.ShapeDtypeStruct((16, len(all_masks) * HD), jnp.float32),
        in_specs=[VMEM] * 2,
        out_specs=VMEM,
        compiler_params=params,
    )(*queries)

    def packed(keys, values, flops, *after):
        held = len(keys)
        return pl.pallas_call(
            functools.partial(pack_kernel, held),
            out_shape=jax.ShapeDtypeStruct((2 * held * rows, width), jnp.bfloat16),
            in_specs=[VMEM] * (2 * held + len(after)),
            out_specs=VMEM,
            compiler_params=params,
            cost_estimate=cost(flops),
        )(*keys, *values, *after)

    near_keys[far], near_values[far] = far_key, far_value
    early_pack = packed(
        [near_keys[mask] for mask in early], [near_values[mask] for mask in early], 0
    )

    def step(first, pack, *state):
        return pl.pallas_call(
            functools.partial(step_kernel, first),
            out_shape=[
                jax.ShapeDtypeStruct((2 * rows, width), jnp.float32),
                jax.ShapeDtypeStruct((2 * rows, 2 * width), jnp.float32),
            ],
            in_specs=[VMEM] * (4 + len(state)),
            out_specs=[VMEM] * 2,
            compiler_params=params,
        )(*queries, biases, pack, *state)

    state = step(0, early_pack)
    late_pack = packed(
        [late_keys[mask ^ far] for mask in late],
        [late_values[mask ^ far] for mask in late],
        12 * UNIT,
        state[1],
    )
    state = step(len(early), exchange(early_pack, 1), *state)
    state = step(2 * len(early), late_pack, *state)
    last_pack = exchange(late_pack, 1)

    def last(place, out_shape):
        return pl.pallas_call(
            functools.partial(last_attention, place),
            out_shape=out_shape,
            in_specs=[VMEM] * 5,
            out_specs=[VMEM] * len(out_shape),
            compiler_params=params,
        )(queries[place], biases, last_pack, *state)

    (packet,) = last(1, [jax.ShapeDtypeStruct((rows + EXTRA, width), jnp.bfloat16)])
    own, own_lines = last(
        0,
        [
            jax.ShapeDtypeStruct((rows, width), jnp.float32),
            jax.ShapeDtypeStruct((16, width), jnp.float32),
        ],
    )
    gates = pl.pallas_call(
        gate_kernel,
        out_shape=jax.ShapeDtypeStruct((16, width), jnp.float32),
        in_specs=[SMEM, VMEM],
        out_specs=VMEM,
        compiler_params=params,
    )(frame_step, gate_table)
    packet = exchange(packet, query_mask)

    return pl.pallas_call(
        merge_kernel,
        out_shape=jax.ShapeDtypeStruct((rows, width), jnp.bfloat16),
        in_specs=[VMEM] * 4,
        out_specs=ANY,
        scratch_shapes=[
            pltpu.VMEM((rows, width), jnp.bfloat16),
            pltpu.SemaphoreType.DMA((width // HD,)),
        ],
        compiler_params=params,
    )(own, own_lines, packet, gates)


def solution(mesh):
    return jax.shard_map(
        local,
        mesh=mesh,
        in_specs=(
            P("tm", "head"),
            P("tm", "head"),
            P("tm", "head"),
            P("head"),
            P("head"),
            P(None, "head"),
            P(),
            P("tm", None),
        ),
        out_specs=P("tm", "head"),
        check_vma=False,
    )
```
